32 devices in a mesh: dp: 16 (over z, y, x), fsdp: 2 (over core).
Axes of the slice: x: 2, y: 2, z: 4, core: 2. Of those that a mesh axis runs over, the one named last changes fastest.
Arguments:
- tokens: bfloat16 [2, 32, 256, 1152], P('fsdp', 'dp'), may hold values from -6 to 6
- conditioning: bfloat16 [2, 32, 1152], P('fsdp', 'dp'), may hold values from -6 to 6
- timestep: int32 [2, 32], P('fsdp', 'dp'), may hold values from 0 to 999
- noise_bins: int32 [2, 32], P('fsdp', 'dp'), may hold values from 0 to 15, as said below
- source_slot: int32 [2, 16], P('fsdp'), may hold values from 0 to 31, as said below
- cotangent: bfloat16 [2, 32, 256, 1152], P('fsdp', 'dp'), may hold values from -6 to 6
- ada_weight: bfloat16 [1152, 6912], P('dp', 'fsdp'), may hold values from -0.1875 to 0.1875
- qkv_weight: bfloat16 [1152, 3456], P('dp', 'fsdp'), may hold values from -0.1875 to 0.1875
- proj_weight: bfloat16 [1152, 1152], P('dp', 'fsdp'), may hold values from -0.75 to 0.75
- ffn_in_weight: bfloat16 [1152, 6144], P('dp', 'fsdp'), may hold values from -0.1875 to 0.1875
- ffn_out_weight: bfloat16 [3072, 1152], P('dp', 'fsdp'), may hold values from -0.21875 to 0.21875
- ada_bias: float32 [6912], replicated, may hold values from -3 to 3
- qkv_bias: float32 [3456], replicated, may hold values from -3 to 3
- proj_bias: float32 [1152], replicated, may hold values from -3 to 3
- ffn_in_bias: float32 [6144], replicated, may hold values from -3 to 3
- ffn_out_bias: float32 [1152], replicated, may hold values from -3 to 3
- norm_gains: float32 [2, 1152], replicated, may hold values from 0.5 to 1.5
- qk_gains: float32 [2, 72], replicated, may hold values from 0.1 to 1.9
Outputs:
- output: bfloat16 [2, 32, 256, 1152], P('fsdp', 'dp')
- input_grad: bfloat16 [2, 32, 256, 1152], P('fsdp', 'dp')
- cond_grad: float32 [2, 32, 1152], P('fsdp', 'dp')
- ada_weight_grad: float32 [1152, 6912], P('dp', 'fsdp')
- qkv_weight_grad: float32 [1152, 3456], P('dp', 'fsdp')
- proj_weight_grad: float32 [1152, 1152], P('dp', 'fsdp')
- ffn_in_weight_grad: float32 [1152, 6144], P('dp', 'fsdp')
- ffn_out_weight_grad: float32 [3072, 1152], P('dp', 'fsdp')
- ada_bias_grad: float32 [6912], replicated
- qkv_bias_grad: float32 [3456], replicated
- proj_bias_grad: float32 [1152], replicated
- ffn_in_bias_grad: float32 [6144], replicated
- ffn_out_bias_grad: float32 [1152], replicated
- norm_gains_grad: float32 [2, 1152], replicated
- qk_gains_grad: float32 [2, 72], replicated
The draws below stay inside these ranges and needn't reach their ends.
Inputs may be any that keep to these rules, and one draw needn't show every extreme that they name: `source_slot`: device i of dp holds the items of its group in its slots i * 2 to i * 2 + c - 1 for some c of 0 to 2; each list names every occupied slot of its group once, in ascending order; in each group some device holds 2 items. `noise_bins`: in each group the bins of the occupied slots, read in the order of source_slot, never fall, and every bin is held by some occupied slot of each group. Bins of empty slots are arbitrary.
All inputs are finite; a program needn't handle non-finite values.
Results may differ from the reference program's by a relative error of at most 0.015.
Values may be sent and summed in bfloat16 or wider, within the bound.
A program may use at most 320 MiB of HBM per device.

```python
import math
import jax
import jax.numpy as jnp
from jax import lax

D = 1152
HEADS = 16
HEAD_DIM = 72
FF = 3072
GRID_ROWS = 16
GRID_COLS = 16
NBINS = 16
ITEMS_DEV = 1
SEQ = 256
CAP = 2
SLOTS = 32
N_DP = 16
N_FSDP = 2


def group_loads(group_key):
    cut = jax.random.randint(jax.random.fold_in(group_key, 1), (), N_DP // 4 + 1, N_DP // 2 + 1)
    shifts = jax.random.randint(jax.random.fold_in(group_key, 2), (N_DP // 2,), -ITEMS_DEV, ITEMS_DEV + 1)
    index = jnp.arange(N_DP, dtype=jnp.int32)
    beyond = index - 2 * cut
    pair_index = jnp.clip(beyond // 2, 0, N_DP // 2 - 1)
    sign = jnp.where(beyond % 2 == 0, 1, -1)
    tail = jnp.where(beyond >= 0, sign * shifts[pair_index], 0)
    change = jnp.where(index < cut, ITEMS_DEV, jnp.where(index < 2 * cut, -ITEMS_DEV, tail))
    return (ITEMS_DEV + change).astype(jnp.int32)


def shared_layout(key):
    group_keys = jax.random.split(jax.random.fold_in(key, 77), N_FSDP)
    loads = jax.vmap(group_loads)(group_keys)
    filled = jnp.arange(CAP, dtype=jnp.int32)[None, None, :] < loads[:, :, None]
    return filled.reshape(N_FSDP, N_DP * CAP)


def draw_source_slot(key, part):
    filled = shared_layout(key)

    def listing(slot_row):
        ranks = jnp.argsort(jnp.where(slot_row, 0, 1).astype(jnp.int32), stable=True)
        return ranks[:N_DP * ITEMS_DEV].astype(jnp.int32)
    return jax.vmap(listing)(filled)


def draw_noise_bins(key, part):
    own_key = jax.random.fold_in(key, 5)
    filled = shared_layout(key)
    group_items = N_DP * ITEMS_DEV

    def one_group(group_key, slot_row):
        first_key, second_key, third_key = jax.random.split(group_key, 3)
        extra_bins = jnp.minimum(jax.random.randint(first_key, (group_items - NBINS,), 0, NBINS), jax.random.randint(second_key, (group_items - NBINS,), 0, 2 * NBINS))
        ordered_bins = jnp.sort(jnp.concatenate([jnp.arange(NBINS, dtype=jnp.int32), extra_bins.astype(jnp.int32)]))
        fill_rank = jnp.clip(jnp.cumsum(slot_row.astype(jnp.int32)) - 1, 0, group_items - 1)
        filler = jax.random.randint(third_key, slot_row.shape, 0, NBINS)
        return jnp.where(slot_row, ordered_bins[fill_rank], filler).astype(jnp.int32)
    return jax.vmap(one_group)(jax.random.split(own_key, N_FSDP), filled)


def touch_ends(values, key, smallest, largest):
    longest = values.shape.index(max(values.shape))
    spots = []
    for shift in (0, 1):
        where = [jax.random.randint(jax.random.fold_in(key, axis), (), 0, length) for axis, length in enumerate(values.shape)]
        where[longest] = (where[longest] + shift) % values.shape[longest]
        spots.append(tuple(where))
    return values.at[spots[0]].set(smallest).at[spots[1]].set(largest)


def block_scale(rng, shape, cuts, least, largest):
    factor_of = 1.0
    for position, blocks in cuts:
        heights = jax.random.uniform(jax.random.fold_in(jax.random.fold_in(rng, 6), position), (blocks,), jnp.float32, least / len(cuts), largest / len(cuts))
        factor_of = factor_of * jnp.repeat(jnp.exp(heights), shape[position] // blocks).reshape((-1,) + (1,) * (len(shape) - 1 - position))
    return factor_of


def normal_values(key, shape, width, bound, cuts=(), kind=jnp.bfloat16):
    array = jax.random.normal(key, shape, jnp.float32) * width
    if len(cuts) > 0:
        array = block_scale(key, shape, cuts, -0.22, 0.18) * array
    return jnp.clip(array, min=-bound, max=bound).astype(kind)


def setup_inputs(seed: int = 0) -> dict:
    seeds = jax.random.split(jax.random.key(seed), 19)
    return {
        "tokens": normal_values(seeds[0], (N_FSDP, SLOTS, SEQ, D), 1.0, 6.0, ((0, 2), (1, 16))),
        "conditioning": normal_values(seeds[1], (N_FSDP, SLOTS, D), 1.0, 6.0, ((0, 2), (1, 16))),
        "timestep": touch_ends(jax.random.randint(seeds[2], (N_FSDP, SLOTS), 0, 1000), jax.random.fold_in(seeds[2], 1), 0, 999).astype(jnp.int32),
        "noise_bins": draw_noise_bins(jax.random.fold_in(seeds[18], 71), 0),
        "source_slot": draw_source_slot(jax.random.fold_in(seeds[18], 71), 0),
        "cotangent": normal_values(seeds[5], (N_FSDP, SLOTS, SEQ, D), 1.0, 6.0, ((0, 2), (1, 16))),
        "ada_weight": normal_values(seeds[6], (D, 6 * D), D ** -0.5, 0.1875, ((0, 16), (1, 2))),
        "qkv_weight": normal_values(seeds[7], (D, 3 * D), D ** -0.5, 0.1875, ((0, 16), (1, 2))),
        "proj_weight": normal_values(seeds[8], (D, D), (D // 16) ** -0.5, 0.75, ((0, 16), (1, 2))),
        "ffn_in_weight": normal_values(seeds[9], (D, 2 * FF), D ** -0.5, 0.1875, ((0, 16), (1, 2))),
        "ffn_out_weight": normal_values(seeds[10], (FF, D), (FF // 4) ** -0.5, 0.21875, ((0, 16), (1, 2))),
        "ada_bias": normal_values(seeds[11], (6 * D,), 0.5, 3.0, (), jnp.float32),
        "qkv_bias": normal_values(seeds[12], (3 * D,), 0.5, 3.0, (), jnp.float32),
        "proj_bias": normal_values(seeds[13], (D,), 0.5, 3.0, (), jnp.float32),
        "ffn_in_bias": normal_values(seeds[14], (2 * FF,), 0.5, 3.0, (), jnp.float32),
        "ffn_out_bias": normal_values(seeds[15], (D,), 0.5, 3.0, (), jnp.float32),
        "norm_gains": jnp.clip(1.0 + 0.1 * jax.random.normal(seeds[16], (2, D), jnp.float32), 0.5, 1.5),
        "qk_gains": jnp.clip(1.0 + 0.18 * jax.random.normal(seeds[17], (2, HEAD_DIM), jnp.float32), 0.1, 1.9),
    }


EPS = 1e-06

@jax.custom_vjp
def low(v):
    return lax.optimization_barrier(v.astype(jnp.bfloat16)).astype(jnp.float32)

@jax.custom_vjp
def low_back(v):
    return v

def low_keep(v):
    return (low(v), None)

def low_pass(kept, grad):
    return (grad,)

def back_keep(v):
    return (v, None)

def back_low(kept, grad):
    return (low(grad),)
low.defvjp(low_keep, low_pass)
low_back.defvjp(back_keep, back_low)

def swish(inputs):
    return inputs * jax.nn.sigmoid(inputs)

def norm_scale(inputs):
    return lax.rsqrt(lax.optimization_barrier(jnp.mean(inputs * inputs, axis=-1, keepdims=True)) + EPS)

def time_embed(timesteps, model_width):
    half_width = model_width // 2
    frequencies = jnp.exp(-math.log(10000.0) * jnp.arange(half_width, dtype=jnp.float32) / half_width)
    angles = timesteps.astype(jnp.float32)[..., None] * frequencies
    return jnp.concatenate([jnp.cos(angles), jnp.sin(angles)], axis=-1)

def rotary_tables(head_size):
    quarter = head_size // 4
    frequencies = jnp.exp(-math.log(10000.0) * jnp.arange(quarter, dtype=jnp.float32) * 4.0 / head_size)
    places = jnp.arange(GRID_ROWS * GRID_COLS, dtype=jnp.int32)
    row_place = (places // GRID_COLS).astype(jnp.float32)
    column_place = (places % GRID_COLS).astype(jnp.float32)
    angles = jnp.concatenate([row_place[:, None] * frequencies[None, :], column_place[:, None] * frequencies[None, :]], axis=1)
    return (jnp.cos(angles)[:, None, :], jnp.sin(angles)[:, None, :])

def rotate(vector, cosine_table, sine_table):
    quarter = vector.shape[-1] // 4
    first_half = jnp.concatenate([vector[..., :quarter], vector[..., 2 * quarter:3 * quarter]], axis=-1)
    second_half = jnp.concatenate([vector[..., quarter:2 * quarter], vector[..., 3 * quarter:]], axis=-1)
    new_first = first_half * cosine_table - second_half * sine_table
    new_second = second_half * cosine_table + first_half * sine_table
    return jnp.concatenate([new_first[..., :quarter], new_second[..., :quarter], new_first[..., quarter:], new_second[..., quarter:]], axis=-1)

def dense(former, latter):
    return jnp.dot(former, latter, precision=lax.Precision.HIGHEST)

def block_forward(params, inputs, conds):
    ada_matrix, qkv_matrix, proj_matrix, lift_matrix, drop_matrix, ada_offset, qkv_offset, proj_offset, lift_offset, drop_offset, gains, head_gains = params
    item_count, length, model_width = inputs.shape
    row_count = item_count * length
    cosine_table, sine_table = rotary_tables(HEAD_DIM)
    silu_cond = low(swish(conds))
    modulation = low_back(dense(silu_cond, ada_matrix) + ada_offset)
    pieces = [modulation[:, None, block_index * model_width:(block_index + 1) * model_width] for block_index in range(6)]
    shift_attn, scale_attn, gate_attn, shift_ffn, scale_ffn, gate_ffn = pieces
    normed_one = inputs * norm_scale(inputs) * gains[0]
    modulated_one = low(normed_one * (1.0 + scale_attn) + shift_attn)
    projected = low_back(dense(modulated_one.reshape(row_count, model_width), qkv_matrix) + qkv_offset)
    projected = projected.reshape(item_count, length, 3, HEADS, HEAD_DIM)
    query = projected[:, :, 0]
    key_vec = projected[:, :, 1]
    values = projected[:, :, 2]
    query_turned = low(rotate(query * norm_scale(query) * head_gains[0], cosine_table, sine_table))
    key_turned = low(rotate(key_vec * norm_scale(key_vec) * head_gains[1], cosine_table, sine_table))
    values_low = low(values)
    scores = jnp.einsum('bqhd,bkhd->bhqk', query_turned, key_turned, precision=lax.Precision.HIGHEST)
    scores = low_back(scores * HEAD_DIM ** (-0.5))
    row_top = lax.optimization_barrier(jnp.max(scores, axis=-1, keepdims=True))
    exponent = jnp.exp(scores - row_top)
    probs = exponent / lax.optimization_barrier(jnp.sum(exponent, axis=-1, keepdims=True))
    attended = jnp.einsum('bhqk,bkhd->bqhd', low(probs), values_low, precision=lax.Precision.HIGHEST)
    attended_low = low(low_back(attended)).reshape(row_count, model_width)
    attn_out = low_back(dense(attended_low, proj_matrix) + proj_offset).reshape(item_count, length, model_width)
    residual = inputs + gate_attn * attn_out
    normed_two = residual * norm_scale(residual) * gains[1]
    modulated_two = low(normed_two * (1.0 + scale_ffn) + shift_ffn)
    lifted = low_back(dense(modulated_two.reshape(row_count, model_width), lift_matrix) + lift_offset)
    hidden_low = low(swish(lifted[:, :FF]) * lifted[:, FF:])
    ffn_value = low_back(dense(hidden_low, drop_matrix) + drop_offset).reshape(item_count, length, model_width)
    return residual + gate_ffn * ffn_value

def reference(tokens, conditioning, timestep, noise_bins, source_slot, cotangent, ada_weight, qkv_weight, proj_weight, ffn_in_weight, ffn_out_weight, ada_bias, qkv_bias, proj_bias, ffn_in_bias, ffn_out_bias, norm_gains, qk_gains):
    groups = tokens.shape[0]
    slot_count = tokens.shape[1]
    length = tokens.shape[2]
    model_width = tokens.shape[3]
    group_items = source_slot.shape[1]
    all_items = groups * group_items
    offsets = (jnp.arange(groups, dtype=jnp.int32) * slot_count)[:, None]
    flat_slots = (source_slot.astype(jnp.int32) + offsets).reshape(all_items).astype(jnp.int32)
    slot_taken = jnp.zeros((groups * slot_count,), jnp.int32).at[flat_slots].set(1)
    flat_bins = noise_bins.reshape(groups * slot_count).astype(jnp.int32)
    bin_hits = (flat_bins[:, None] == jnp.arange(NBINS, dtype=jnp.int32)[None, :]) & (slot_taken[:, None] > 0)
    counts = lax.optimization_barrier(jnp.sum(bin_hits.astype(jnp.float32), axis=0))
    bin_share = all_items / (NBINS * counts)
    slot_weight = lax.optimization_barrier(jnp.sum(jnp.where(bin_hits, bin_share[None, :], 0.0), axis=1))
    weighted = (slot_weight[:, None, None] * cotangent.reshape(groups * slot_count, length, model_width).astype(jnp.float32)).astype(jnp.bfloat16)
    cond_vector = (conditioning.reshape(groups * slot_count, model_width).astype(jnp.float32) + time_embed(timestep.reshape(groups * slot_count), model_width)).astype(jnp.bfloat16)
    item_tokens = jnp.take(tokens.reshape(groups * slot_count, length, model_width), flat_slots, axis=0).astype(jnp.float32)
    item_grads = jnp.take(weighted, flat_slots, axis=0).astype(jnp.float32)
    item_conds = jnp.take(cond_vector, flat_slots, axis=0).astype(jnp.float32)
    params = tuple((entry.astype(jnp.float32) for entry in (ada_weight, qkv_weight, proj_weight, ffn_in_weight, ffn_out_weight, ada_bias, qkv_bias, proj_bias, ffn_in_bias, ffn_out_bias, norm_gains, qk_gains)))
    block_items = math.gcd(all_items, 16)
    block_count = all_items // block_items
    stacked = (item_tokens.reshape(block_count, block_items, length, model_width), item_conds.reshape(block_count, block_items, model_width), item_grads.reshape(block_count, block_items, length, model_width))

    def step(totals, portion):
        token_block, cond_block, grad_block = portion
        result, pullback = jax.vjp(block_forward, params, token_block, cond_block)
        param_grads, token_grads, cond_grads = pullback(grad_block)
        totals = jax.tree.map(lambda total_grad, new_grad: total_grad + new_grad, totals, param_grads)
        return (totals, (result, token_grads, cond_grads))
    initial = tuple((jnp.zeros_like(entry) for entry in params))
    totals, (results, token_grads, cond_grads) = lax.scan(step, initial, stacked)
    output = jnp.zeros((groups * slot_count, length, model_width), jnp.float32).at[flat_slots].set(results.reshape(all_items, length, model_width))
    input_grad = jnp.zeros((groups * slot_count, length, model_width), jnp.float32).at[flat_slots].set(token_grads.reshape(all_items, length, model_width))
    cond_grad = jnp.zeros((groups * slot_count, model_width), jnp.float32).at[flat_slots].set(cond_grads.reshape(all_items, model_width))
    output = output.astype(jnp.bfloat16).reshape(groups, slot_count, length, model_width)
    input_grad = input_grad.astype(jnp.bfloat16).reshape(groups, slot_count, length, model_width)
    cond_grad = cond_grad.reshape(groups, slot_count, model_width)
    return (output, input_grad, cond_grad, totals[0], totals[1], totals[2], totals[3], totals[4], totals[5], totals[6], totals[7], totals[8], totals[9], totals[10], totals[11])
```

```python
import functools
import math

import jax
import jax.numpy as jnp
import numpy as np
from jax import lax
from jax.experimental import pallas as pl
from jax.experimental.pallas import tpu as pltpu
from jax.sharding import PartitionSpec as P

HEADS = 16
HEAD_DIM = 72
FF = 3072
GRID_ROWS = 16
GRID_COLS = 16
NBINS = 16


EPS = 1e-06


def swish(inputs):
    return inputs * jax.nn.sigmoid(inputs)


def swish_slope(inputs):
    sigmoid = jax.nn.sigmoid(inputs)
    return sigmoid * (1.0 + inputs * (1.0 - sigmoid))


def norm_scale(inputs):
    return lax.rsqrt(jnp.mean(inputs * inputs, axis=-1, keepdims=True) + EPS)


def norm_back(grad_unit, unit_value, scale_factor):
    return scale_factor * (
        grad_unit - unit_value * jnp.mean(grad_unit * unit_value, axis=-1, keepdims=True)
    )


def time_embed(timesteps, model_width):
    half_width = model_width // 2
    frequencies = jnp.exp(
        -math.log(10000.0) * jnp.arange(half_width, dtype=jnp.float32) / half_width
    )
    angles = timesteps.astype(jnp.float32)[..., None] * frequencies
    return jnp.concatenate([jnp.cos(angles), jnp.sin(angles)], axis=-1)


def product(former, latter):
    return jnp.dot(former, latter, preferred_element_type=jnp.float32)


def product_transposed(former, latter):
    return lax.dot_general(
        former, latter, (((1,), (1,)), ((), ())), preferred_element_type=jnp.float32
    )


def transposed_product(former, latter):
    return lax.dot_general(
        former, latter, (((0,), (0,)), ((), ())), preferred_element_type=jnp.float32
    )


MESH = pl.DeviceIdType.MESH
ANY = pl.BlockSpec(memory_space=pl.ANY)
WHOLE = pl.BlockSpec(memory_space=pltpu.VMEM)
PAIR = 2


class Grid:
    def __init__(self, mesh):
        devices = mesh.devices
        self.count = devices.shape[0]
        places = [tuple(devices[i, 0].coords[:3]) for i in range(self.count)]
        low = [min(p[a] for p in places) for a in range(3)]
        places = [tuple(p[a] - low[a] for a in range(3)) for p in places]
        self.sizes = [max(p[a] for p in places) + 1 for a in range(3)]
        order = {p: i for i, p in enumerate(places)}
        self.strides = [
            order.get(tuple(int(b == a) for b in range(3)), 0) if self.sizes[a] > 1 else 0
            for a in range(3)
        ]
        self.plain = (
            self.sizes[0] == 2
            and self.sizes[1] == 2
            and self.sizes[2] == 4
            and devices.shape[1] == PAIR
            and self.strides == [1, 2, 4]
            and all(
                sum(c * s for c, s in zip(p, self.strides)) == i for p, i in order.items()
            )
        )

    def at(self, x, y, z):
        return x * self.strides[0] + y * self.strides[1] + z * self.strides[2]

    def here(self):
        own = lax.axis_index("dp")
        return tuple(
            lax.rem(own // stride, size) for stride, size in zip(self.strides, self.sizes)
        )


class Copies:
    def __init__(self, send_sems):
        self.send_sems = send_sems
        self.started = []

    def send(self, source, target, recv_sem, dp, core):
        copy = pltpu.make_async_remote_copy(
            src_ref=source,
            dst_ref=target,
            send_sem=self.send_sems.at[len(self.started)],
            recv_sem=recv_sem,
            device_id={"dp": dp, "fsdp": core},
            device_id_type=MESH,
        )
        copy.start()
        self.started.append(copy)

    def finish(self):
        for copy in self.started:
            copy.wait_send()


def arrived(block, recv_sem):
    pltpu.make_async_copy(block, block, recv_sem).wait()


def greet_all(count):
    barrier = pltpu.get_barrier_semaphore()
    own = lax.axis_index("dp") * PAIR + lax.axis_index("fsdp")

    def signal(step, carry):
        other = lax.rem(own + step, count * PAIR)
        pl.semaphore_signal(
            barrier,
            inc=1,
            device_id={"dp": other // PAIR, "fsdp": lax.rem(other, PAIR)},
            device_id_type=MESH,
        )
        return carry

    lax.fori_loop(1, count * PAIR, signal, 0)
    pl.semaphore_wait(barrier, count * PAIR - 1)


def spread(count, source_at, target, send_sems, recv_sems):
    own = lax.axis_index("dp") * PAIR + lax.axis_index("fsdp")

    def start(step, carry):
        other = lax.rem(own + step, count * PAIR)
        pltpu.make_async_remote_copy(
            src_ref=source_at(other),
            dst_ref=target.at[own],
            send_sem=send_sems.at[step],
            recv_sem=recv_sems.at[own],
            device_id={"dp": other // PAIR, "fsdp": lax.rem(other, PAIR)},
            device_id_type=MESH,
        ).start()
        return carry

    lax.fori_loop(1, count * PAIR, start, 0)
    mine = pltpu.make_async_copy(source_at(own), target.at[own], recv_sems.at[own])
    mine.start()


def spread_wait(count, source_at, target, send_sems, recv_sems):
    own = lax.axis_index("dp") * PAIR + lax.axis_index("fsdp")

    def wait(step, carry):
        other = lax.rem(own + step, count * PAIR)
        arrived(target.at[other], recv_sems.at[other])
        return carry

    lax.fori_loop(0, count * PAIR, wait, 0)

    def wait_sent(step, carry):
        other = lax.rem(own + step, count * PAIR)
        pltpu.make_async_copy(source_at(other), source_at(other), send_sems.at[step]).wait()
        return carry

    lax.fori_loop(1, count * PAIR, wait_sent, 0)


def pickers(sources, modes):
    return [
        {
            "each": lambda other, ref=ref: ref.at[other],
            "half": lambda other, ref=ref: ref.at[lax.rem(other, PAIR)],
            "all": lambda other, ref=ref: ref,
        }[mode]
        for ref, mode in zip(sources, modes)
    ]


def landing(count, array, mode):
    part = array.shape if mode == "all" else array.shape[1:]
    return jax.ShapeDtypeStruct((count * PAIR,) + part, array.dtype)


def head_tables():
    width = HEADS * HEAD_DIM
    quarter = HEAD_DIM // 4
    lane = np.arange(width)
    indicator = np.zeros((width, 128), np.float32)
    indicator[lane, lane // HEAD_DIM] = 1.0
    frequencies = np.exp(-math.log(10000.0) * np.arange(quarter, dtype=np.float32) * 4.0 / HEAD_DIM)
    frequencies = frequencies.astype(np.float32)
    places = np.arange(GRID_ROWS * GRID_COLS)
    part = (lane % HEAD_DIM) // quarter
    place = np.where(part[None, :] < 2, (places // GRID_COLS)[:, None], (places % GRID_COLS)[:, None])
    angles = place.astype(np.float32) * frequencies[lane % quarter][None, :]
    sines = np.sin(angles)
    first = (part % 2 == 0)[None, :]
    return (
        jnp.asarray(indicator, jnp.bfloat16),
        jnp.asarray(indicator.T, jnp.bfloat16),
        jnp.asarray(np.cos(angles), jnp.float32),
        jnp.asarray(np.where(first, -sines, 0.0), jnp.float32),
        jnp.asarray(np.where(first, 0.0, sines), jnp.float32),
        jnp.asarray(indicator.T[:HEADS], jnp.bfloat16),
    )


def turn(vector, cosines, before, after, sign=1.0):
    width = vector.shape[1]
    quarter = HEAD_DIM // 4
    shifted = (
        pltpu.roll(vector, width - quarter, axis=1) * before
        + pltpu.roll(vector, quarter, axis=1) * after
    )
    return vector * cosines + shifted if sign > 0 else vector * cosines - shifted


def spread_heads(compact, spreader):
    high = compact.astype(jnp.bfloat16)
    low = (compact - high.astype(jnp.float32)).astype(jnp.bfloat16)
    return product(high, spreader) + product(low, spreader)


def row_loop(rows, per_slot, body, block=128):
    def step(index, carry):
        start = pl.multiple_of(index * block, block)
        body(
            pl.ds(start, block),
            (index * block) // per_slot,
            pl.ds(pl.multiple_of(lax.rem(index * block, per_slot), block), block),
        )
        return carry

    lax.fori_loop(0, rows // block, step, 0)


def head_window(head):
    start = head * HEAD_DIM
    low = start // 128 * 128
    high = -(-(start + HEAD_DIM) // 128) * 128
    return slice(low, high)


def softmax(scores):
    exponent = jnp.exp(scores - jnp.max(scores, axis=-1, keepdims=True))
    return exponent / jnp.sum(exponent, axis=-1, keepdims=True)


def lane_tiles(width, most):
    edges = list(range(0, width, most)) + [width]
    return [slice(a, b) for a, b in zip(edges[:-1], edges[1:])]


def attention_forward(
    tokens, mod, gains, head_gains, qkv_bias, proj_bias,
    indicator, spreader, cosines, before, after, masks,
    qkv_hbm, proj_hbm,
    mod_one, query_unit, key_unit, query_scale, key_scale, query_turned, key_turned, values_low,
    attended_low, attn_out, residual, mod_two,
    qkv_half, proj_half, raw, sems,
):
    rows, width = tokens.shape
    length = cosines.shape[0]
    loads = [
        pltpu.make_async_copy(qkv_hbm, qkv_half, sems.at[0]),
        pltpu.make_async_copy(proj_hbm, proj_half, sems.at[1]),
    ]
    for load in loads:
        load.start()

    def norm_first(here, slot, _):
        inputs = tokens[here, :].astype(jnp.float32)
        normed = inputs * norm_scale(inputs) * gains[0:1, :]
        mod_one[here, :] = (normed * (1.0 + mod[slot, 1:2, :]) + mod[slot, 0:1, :]).astype(
            jnp.bfloat16
        )

    row_loop(rows, length, norm_first)
    loads[0].wait()
    half = qkv_half.shape[2]
    for side in range(PAIR):
        for cols in lane_tiles(half, 640):
            raw[side, :, cols] = (
                product(mod_one[...], qkv_half[side, :, cols])
                + qkv_bias[side : side + 1, cols]
            )

    def heads(here, slot, there):
        query = raw[0, here, :width]
        key_vec = jnp.concatenate(
            [raw[0, here, width:], raw[1, here, : 2 * width - half]], axis=1
        )
        values_low[here, :] = raw[1, here, 2 * width - half :].astype(jnp.bfloat16)
        tables = (cosines[there, :], before[there, :], after[there, :])
        for vector, gain, unit, scale, turned in (
            (query, head_gains[0:1, :], query_unit, query_scale, query_turned),
            (key_vec, head_gains[1:2, :], key_unit, key_scale, key_turned),
        ):
            squares = product((vector * vector).astype(jnp.bfloat16), indicator[...])
            factor = lax.rsqrt(squares * (1.0 / HEAD_DIM) + EPS)
            scale[here, :] = factor
            united = vector * spread_heads(factor, spreader[...])
            unit[here, :] = united
            turned[here, :] = turn(united * gain, *tables).astype(jnp.bfloat16)

    row_loop(rows, length, heads)

    def attend(slot, carry):
        here = pl.ds(pl.multiple_of(slot * length, length), length)
        pieces = [None] * (width // 128)
        for head in range(HEADS):
            window = head_window(head)
            mask = masks[head : head + 1, window]
            scores = (
                product_transposed(query_turned[here, window] * mask, key_turned[here, window])
                * HEAD_DIM**-0.5
            )
            probs = softmax(scores).astype(jnp.bfloat16)
            found = product(probs, values_low[here, window] * mask)
            for tile in range(window.start // 128, window.stop // 128):
                part = found[:, tile * 128 - window.start : (tile + 1) * 128 - window.start]
                pieces[tile] = part if pieces[tile] is None else pieces[tile] + part
                if (tile + 1) * 128 <= (head + 1) * HEAD_DIM:
                    attended_low[here, tile * 128 : (tile + 1) * 128] = pieces[tile].astype(
                        jnp.bfloat16
                    )
                    pieces[tile] = None
        return carry

    lax.fori_loop(0, rows // length, attend, 0)
    loads[1].wait()
    half = proj_half.shape[2]
    for side in range(PAIR):
        attn_out[:, side * half : (side + 1) * half] = (
            product(attended_low[...], proj_half[side]) + proj_bias[side : side + 1, :]
        )

    def norm_second(here, slot, _):
        total = tokens[here, :].astype(jnp.float32) + mod[slot, 2:3, :] * attn_out[here, :]
        residual[here, :] = total
        normed = total * norm_scale(total) * gains[1:2, :]
        mod_two[here, :] = (normed * (1.0 + mod[slot, 4:5, :]) + mod[slot, 3:4, :]).astype(
            jnp.bfloat16
        )

    row_loop(rows, length, norm_second)


def attention_forward_call(tokens, mod, gains, head_gains, qkv_bias, proj_bias, tables, qkv, proj):
    rows, width = tokens.shape
    wide = jax.ShapeDtypeStruct((rows, width), jnp.float32)
    low = jax.ShapeDtypeStruct((rows, width), jnp.bfloat16)
    compact = jax.ShapeDtypeStruct((rows, 128), jnp.float32)
    return pl.pallas_call(
        attention_forward,
        out_shape=[low, wide, wide, compact, compact, low, low, low, low, wide, wide, low],
        in_specs=[WHOLE] * 12 + [ANY] * 2,
        out_specs=[WHOLE] * 12,
        scratch_shapes=[
            pltpu.VMEM(qkv.shape, jnp.bfloat16),
            pltpu.VMEM(proj.shape, jnp.bfloat16),
            pltpu.VMEM((PAIR, rows, qkv.shape[2]), jnp.float32),
            pltpu.SemaphoreType.DMA((2,)),
        ],
        compiler_params=pltpu.CompilerParams(vmem_limit_bytes=52 * 2**20),
    )(tokens, mod, gains, head_gains, qkv_bias, proj_bias, *tables, qkv, proj)


def ffn_pass(
    mod_two, residual, attn_out, cotangent, slot_weight, slot_kept, mod, gains, in_bias, out_bias,
    in_hbm, out_hbm,
    output, grad_residual, grad_attn, slot_sums, gain_sum, in_bias_sum, out_bias_sum,
    in_terms, out_terms,
    turned_two, grad_low, grad_half, lifted_grad, ffn_value, in_chunk, out_chunk, in_stage, out_stage,
    load_sems, store_sems,
):
    rows, width = mod_two.shape
    length = rows // mod.shape[0]
    hidden = in_hbm.shape[2]
    chunk = in_chunk.shape[3]
    half = out_hbm.shape[2]
    steps = hidden // chunk

    def columns(step):
        return pl.ds(pl.multiple_of(step * chunk, chunk), chunk)

    def loads(step, slot):
        return [
            pltpu.make_async_copy(
                in_hbm.at[:, :, columns(step)], in_chunk.at[slot], load_sems.at[slot, 0]
            ),
            pltpu.make_async_copy(
                out_hbm.at[:, columns(step), :], out_chunk.at[slot], load_sems.at[slot, 1]
            ),
        ]

    def stores(step, slot):
        return [
            pltpu.make_async_copy(
                in_stage.at[slot], in_terms.at[:, :, columns(step)], store_sems.at[slot, 0]
            ),
            pltpu.make_async_copy(
                out_stage.at[slot], out_terms.at[:, columns(step), :], store_sems.at[slot, 1]
            ),
        ]

    for load in loads(0, 0):
        load.start()

    def prepare(here, slot, _):
        grad_out = (cotangent[here, :].astype(jnp.float32) * slot_weight[slot]).astype(jnp.bfloat16)
        grad_low[here, :] = grad_out
        grad_ffn = (mod[slot, 5:6, :] * grad_out.astype(jnp.float32)).astype(jnp.bfloat16)
        grad_half[0, here, :] = grad_ffn[:, :half]
        grad_half[1, here, :] = grad_ffn[:, half:]

    row_loop(rows, length, prepare)
    turned_two[...] = mod_two[...].T
    for side in range(PAIR):
        out_bias_sum[side : side + 1, :] = jnp.sum(
            grad_half[side].astype(jnp.float32), axis=0, keepdims=True
        )
    lifted_grad[...] = jnp.zeros_like(lifted_grad)
    ffn_value[...] = jnp.zeros_like(ffn_value)

    def step_body(step, carry):
        slot = lax.rem(step, 2)

        @pl.when(step + 1 < steps)
        def _():
            for load in loads(step + 1, 1 - slot):
                load.start()

        for load in loads(step, slot):
            load.wait()

        @pl.when(step >= 2)
        def _():
            for store in stores(step - 2, slot):
                store.wait()

        here = columns(step)
        gate_part = product(mod_two[...], in_chunk[slot, 0]) + in_bias[0:1, here]
        up_part = product(mod_two[...], in_chunk[slot, 1]) + in_bias[1:2, here]
        sigmoid = 1.0 / (1.0 + jnp.exp(-gate_part))
        swished = gate_part * sigmoid
        hidden_low = (swished * up_part).astype(jnp.bfloat16)
        grad_hidden = product_transposed(grad_half[0], out_chunk[slot, 0]) + product_transposed(
            grad_half[1], out_chunk[slot, 1]
        )
        grad_gate = (
            grad_hidden * up_part * (sigmoid * (1.0 + gate_part * (1.0 - sigmoid)))
        ).astype(jnp.bfloat16)
        grad_up = (grad_hidden * swished).astype(jnp.bfloat16)
        for side in range(PAIR):
            ffn_value[side] += product(hidden_low, out_chunk[slot, side])
        lifted_grad[...] += product_transposed(grad_gate, in_chunk[slot, 0])
        lifted_grad[...] += product_transposed(grad_up, in_chunk[slot, 1])
        for side, grad in ((0, grad_gate), (1, grad_up)):
            in_bias_sum[side : side + 1, here] = jnp.sum(
                grad.astype(jnp.float32), axis=0, keepdims=True
            )
            in_stage[slot, side] = product(turned_two[...], grad).astype(jnp.bfloat16)
        turned_hidden = hidden_low.T
        for side in range(PAIR):
            out_stage[slot, side] = product(turned_hidden, grad_half[side]).astype(jnp.bfloat16)
        for store in stores(step, slot):
            store.start()
        return carry

    lax.fori_loop(0, steps, step_body, 0)
    for step in range(max(steps - 2, 0), steps):
        for store in stores(step, step % 2):
            store.wait()
    slot_sums[...] = jnp.zeros_like(slot_sums)
    gain_sum[...] = jnp.zeros_like(gain_sum)

    def finish(here, slot, _):
        value = jnp.concatenate([ffn_value[0, here, :], ffn_value[1, here, :]], axis=1) + out_bias[...]
        total = residual[here, :]
        output[here, :] = ((total + mod[slot, 5:6, :] * value) * slot_kept[slot]).astype(
            jnp.bfloat16
        )
        grad_out = grad_low[here, :].astype(jnp.float32)
        factor = norm_scale(total)
        unit = total * factor
        normed = unit * gains[1:2, :]
        grad_mod = lifted_grad[here, :]
        grad_normed = grad_mod * (1.0 + mod[slot, 4:5, :])
        gradient = grad_out + norm_back(grad_normed * gains[1:2, :], unit, factor)
        grad_residual[here, :] = gradient
        grad_attn[here, :] = (mod[slot, 2:3, :] * gradient).astype(jnp.bfloat16)
        for place, terms in (
            (2, gradient * attn_out[here, :]),
            (3, grad_mod),
            (4, grad_mod * normed),
            (5, grad_out * value),
        ):
            slot_sums[slot, place : place + 1, :] += jnp.sum(terms, axis=0, keepdims=True)
        gain_sum[...] += jnp.sum(grad_normed * unit, axis=0, keepdims=True)

    row_loop(rows, length, finish)


def ffn_call(
    mod_two, residual, attn_out, cotangent, slot_weight, slot_kept, mod, gains, in_bias, out_bias,
    ffn_in, ffn_out,
):
    rows, width = mod_two.shape
    hidden, half = ffn_in.shape[2], ffn_out.shape[2]
    chunk = 512
    f32, bf16 = jnp.float32, jnp.bfloat16
    return pl.pallas_call(
        ffn_pass,
        out_shape=[
            jax.ShapeDtypeStruct((rows, width), bf16),
            jax.ShapeDtypeStruct((rows, width), f32),
            jax.ShapeDtypeStruct((rows, width), bf16),
            jax.ShapeDtypeStruct(mod.shape, f32),
            jax.ShapeDtypeStruct((1, width), f32),
            jax.ShapeDtypeStruct((PAIR, hidden), f32),
            jax.ShapeDtypeStruct((PAIR, half), f32),
            jax.ShapeDtypeStruct(ffn_in.shape, bf16),
            jax.ShapeDtypeStruct(ffn_out.shape, bf16),
        ],
        in_specs=[WHOLE] * 10 + [ANY] * 2,
        out_specs=[WHOLE] * 7 + [ANY] * 2,
        scratch_shapes=[
            pltpu.VMEM((width, rows), bf16),
            pltpu.VMEM((rows, width), bf16),
            pltpu.VMEM((PAIR, rows, half), bf16),
            pltpu.VMEM((rows, width), f32),
            pltpu.VMEM((PAIR, rows, half), f32),
            pltpu.VMEM((2, PAIR, width, chunk), bf16),
            pltpu.VMEM((2, PAIR, chunk, half), bf16),
            pltpu.VMEM((2, PAIR, width, chunk), bf16),
            pltpu.VMEM((2, PAIR, chunk, half), bf16),
            pltpu.SemaphoreType.DMA((2, 2)),
            pltpu.SemaphoreType.DMA((2, 2)),
        ],
        compiler_params=pltpu.CompilerParams(vmem_limit_bytes=52 * 2**20),
    )(
        mod_two, residual, attn_out, cotangent, slot_weight, slot_kept, mod, gains, in_bias, out_bias,
        ffn_in, ffn_out,
    )


def attention_backward(
    tokens, mod, gains, head_gains, indicator, spreader, cosines, before, after, masks, slot_kept,
    mod_one, query_unit, key_unit, query_scale, key_scale, query_turned, key_turned, values_low,
    attended_low, grad_residual, grad_attn,
    qkv_hbm, proj_hbm,
    input_grad, slot_sums, gain_sum, head_sums, qkv_bias_sum, proj_bias_sum, qkv_terms, proj_terms,
    qkv_half, proj_half, grad_attended, grad_query, grad_key, grad_values, grad_half, turned, sems,
):
    rows, width = tokens.shape
    length = cosines.shape[0]
    loads = [
        pltpu.make_async_copy(proj_hbm, proj_half, sems.at[0]),
        pltpu.make_async_copy(qkv_hbm, qkv_half, sems.at[1]),
    ]
    stores = [
        pltpu.make_async_copy(proj_half, proj_terms, sems.at[2]),
        pltpu.make_async_copy(qkv_half, qkv_terms, sems.at[3]),
    ]
    for load in loads:
        load.start()
    half = proj_half.shape[2]
    turned[...] = attended_low[...].T
    for side in range(PAIR):
        cols = slice(side * half, (side + 1) * half)
        proj_bias_sum[:, cols] = jnp.sum(
            grad_attn[:, cols].astype(jnp.float32), axis=0, keepdims=True
        )
    loads[0].wait()
    grad_attended[...] = (
        product_transposed(grad_attn[:, :half], proj_half[0])
        + product_transposed(grad_attn[:, half:], proj_half[1])
    ).astype(jnp.bfloat16)
    for side in range(PAIR):
        proj_half[side] = product(
            turned[...], grad_attn[:, side * half : (side + 1) * half]
        ).astype(jnp.bfloat16)
    stores[0].start()

    def attend(slot, carry):
        here = pl.ds(pl.multiple_of(slot * length, length), length)
        pieces = [[None] * (width // 128) for _ in range(3)]
        for head in range(HEADS):
            window = head_window(head)
            mask = masks[head : head + 1, window]
            query = query_turned[here, window] * mask
            key_vec = key_turned[here, window]
            value = values_low[here, window]
            grad = grad_attended[here, window] * mask
            probs = softmax(product_transposed(query, key_vec) * HEAD_DIM**-0.5)
            grad_probs = product_transposed(grad, value)
            grad_scores = (
                probs * (grad_probs - jnp.sum(probs * grad_probs, axis=-1, keepdims=True))
            ).astype(jnp.bfloat16)
            founds = (
                product(grad_scores, key_vec * mask) * HEAD_DIM**-0.5,
                transposed_product(grad_scores, query) * HEAD_DIM**-0.5,
                transposed_product(probs.astype(jnp.bfloat16), grad),
            )
            for kind, (found, target) in enumerate(
                zip(founds, (grad_query, grad_key, grad_values))
            ):
                for tile in range(window.start // 128, window.stop // 128):
                    part = found[:, tile * 128 - window.start : (tile + 1) * 128 - window.start]
                    held = pieces[kind][tile]
                    held = part if held is None else held + part
                    pieces[kind][tile] = held
                    if (tile + 1) * 128 <= (head + 1) * HEAD_DIM:
                        target[here, tile * 128 : (tile + 1) * 128] = held
        return carry

    lax.fori_loop(0, rows // length, attend, 0)
    half = qkv_half.shape[2]
    head_sums[...] = jnp.zeros_like(head_sums)

    def heads(here, slot, there):
        tables = (cosines[there, :], before[there, :], after[there, :])
        founds = []
        for kind, (grad, gain, unit, scale) in enumerate(
            (
                (grad_query, head_gains[0:1, :], query_unit, query_scale),
                (grad_key, head_gains[1:2, :], key_unit, key_scale),
            )
        ):
            normed = turn(grad[here, :], *tables, sign=-1.0)
            united = unit[here, :]
            head_sums[kind : kind + 1, :] += jnp.sum(normed * united, axis=0, keepdims=True)
            normed = normed * gain
            means = product((normed * united).astype(jnp.bfloat16), indicator[...]) * (
                1.0 / HEAD_DIM
            )
            founds.append(
                spread_heads(scale[here, :], spreader[...])
                * (normed - united * spread_heads(means, spreader[...]))
            )
        cut = half - width
        grad_half[0, here, :width] = founds[0].astype(jnp.bfloat16)
        grad_half[0, here, width:] = founds[1][:, :cut].astype(jnp.bfloat16)
        grad_half[1, here, : width - cut] = founds[1][:, cut:].astype(jnp.bfloat16)
        grad_half[1, here, width - cut :] = grad_values[here, :].astype(jnp.bfloat16)

    row_loop(rows, length, heads)
    lifted_grad = grad_query
    loads[1].wait()
    for side in range(PAIR):
        qkv_bias_sum[side : side + 1, :] = jnp.sum(
            grad_half[side].astype(jnp.float32), axis=0, keepdims=True
        )
    for cols in lane_tiles(width, 384):
        lifted_grad[:, cols] = product_transposed(
            grad_half[0], qkv_half[0, cols, :]
        ) + product_transposed(grad_half[1], qkv_half[1, cols, :])
    turned[...] = mod_one[...].T
    for side in range(PAIR):
        for cols in lane_tiles(half, 640):
            qkv_half[side, :, cols] = product(turned[...], grad_half[side, :, cols]).astype(
                jnp.bfloat16
            )
    stores[1].start()
    slot_sums[...] = jnp.zeros_like(slot_sums)
    gain_sum[...] = jnp.zeros_like(gain_sum)

    def finish(here, slot, _):
        inputs = tokens[here, :].astype(jnp.float32)
        factor = norm_scale(inputs)
        unit = inputs * factor
        normed = unit * gains[0:1, :]
        grad_mod = lifted_grad[here, :]
        grad_normed = grad_mod * (1.0 + mod[slot, 1:2, :])
        gradient = grad_residual[here, :] + norm_back(grad_normed * gains[0:1, :], unit, factor)
        input_grad[here, :] = (gradient * slot_kept[slot]).astype(jnp.bfloat16)
        for place, terms in ((0, grad_mod), (1, grad_mod * normed)):
            slot_sums[slot, place : place + 1, :] += jnp.sum(terms, axis=0, keepdims=True)
        gain_sum[...] += jnp.sum(grad_normed * unit, axis=0, keepdims=True)

    row_loop(rows, length, finish)
    for store in stores:
        store.wait()


def attention_backward_call(
    tokens, mod, gains, head_gains, tables, slot_kept, forward, grad_residual, grad_attn, qkv, proj
):
    rows, width = tokens.shape
    f32, bf16 = jnp.float32, jnp.bfloat16
    half = qkv.shape[2]
    return pl.pallas_call(
        attention_backward,
        out_shape=[
            jax.ShapeDtypeStruct((rows, width), bf16),
            jax.ShapeDtypeStruct(mod.shape, f32),
            jax.ShapeDtypeStruct((1, width), f32),
            jax.ShapeDtypeStruct((2, width), f32),
            jax.ShapeDtypeStruct((PAIR, half), f32),
            jax.ShapeDtypeStruct((1, width), f32),
            jax.ShapeDtypeStruct(qkv.shape, bf16),
            jax.ShapeDtypeStruct(proj.shape, bf16),
        ],
        in_specs=[WHOLE] * 22 + [ANY] * 2,
        out_specs=[WHOLE] * 6 + [ANY] * 2,
        scratch_shapes=[
            pltpu.VMEM(qkv.shape, bf16),
            pltpu.VMEM(proj.shape, bf16),
            pltpu.VMEM((rows, width), bf16),
            pltpu.VMEM((rows, width), f32),
            pltpu.VMEM((rows, width), f32),
            pltpu.VMEM((rows, width), f32),
            pltpu.VMEM((PAIR, rows, half), bf16),
            pltpu.VMEM((width, rows), bf16),
            pltpu.SemaphoreType.DMA((4,)),
        ],
        compiler_params=pltpu.CompilerParams(vmem_limit_bytes=52 * 2**20),
    )(
        tokens, mod, gains, head_gains, *tables, slot_kept, *forward, grad_residual, grad_attn,
        qkv, proj,
    )


class Piece:
    SENDS = 31

    def __init__(self, grid, source, full_at, send_sem, far_sem, near_sem):
        self.grid, self.source, self.full_at = grid, source, full_at
        self.send_sem, self.far_sem, self.near_sem = send_sem, far_sem, near_sem
        self.x, self.y, self.z = grid.here()
        self.core = lax.axis_index("fsdp")
        self.own = grid.at(self.x, self.y, self.z)

    def copy(self, k, source, block, dp, other_core=False):
        sems = self.near_sem if other_core else self.far_sem
        return pltpu.make_async_remote_copy(
            src_ref=source,
            dst_ref=self.full_at(self.core, block),
            send_sem=self.send_sem(k),
            recv_sem=sems(block),
            device_id={"dp": dp, "fsdp": 1 - self.core if other_core else self.core},
            device_id_type=MESH,
        )

    def across(self):
        return self.grid.at(1 - self.x, self.y, self.z)

    def along(self):
        return self.grid.at(self.x, 1 - self.y, self.z)

    def fan_out(self, k, source, block):
        self.copy(k, source, block, self.across()).start()
        self.copy(k + 1, source, block, self.along()).start()
        self.copy(k + 2, source, block, self.own, True).start()

    def own_line(self):
        for step in (1, 2, 3):
            peer = self.grid.at(self.x, self.y, self.z ^ step)
            self.copy(step - 1, self.source, self.own, peer).start()

    def own_plane(self):
        self.fan_out(3, self.source, self.own)

    def run(self, steps):
        for step in steps:
            if step == "L":
                self.own_line()
            elif step == "P":
                self.own_plane()
            elif step in "123":
                self.line(int(step))
            elif step == "c":
                self.corner()
            else:
                self.plane("ab".index(step))

    def arrive(self, block):
        arrived(self.full_at(self.core, block), self.far_sem(block))
        return self.full_at(self.core, block)

    def line(self, step):
        block = self.grid.at(self.x, self.y, self.z ^ step)
        self.fan_out(3 + 3 * step, self.arrive(block), block)

    def plane(self, half):
        even = ((self.z // 2) ^ half) * 2
        k = 15 + 6 * half
        for odd in (0, 1):
            across = self.grid.at(1 - self.x, self.y, even + odd)
            along = self.grid.at(self.x, 1 - self.y, even + odd)
            view = self.arrive(across)
            if not odd:
                self.copy(k, view, across, self.along()).start()
            self.copy(k + 2 + odd, view, across, self.own, True).start()
            view = self.arrive(along)
            if odd:
                self.copy(k + 1, view, along, self.across()).start()
            self.copy(k + 4 + odd, view, along, self.own, True).start()

    def corner(self):
        for place in range(4):
            block = self.grid.at(1 - self.x, 1 - self.y, self.z ^ place)
            self.copy(27 + place, self.arrive(block), block, self.own, True).start()

    def complete(self):
        for block in range(self.grid.count):
            arrived(self.full_at(1 - self.core, block), self.near_sem(block))

    def sent(self):
        view = self.full_at(self.core, self.own)
        for k in range(self.SENDS):
            arrived(view, self.send_sem(k))


class Column:
    SENDS = 11

    def __init__(self, grid, source, full, cols, send_sem, line_sem, plane_sem, near_sem):
        self.grid, self.source, self.full, self.cols = grid, source, full, cols
        self.send_sem, self.line_sem = send_sem, line_sem
        self.plane_sem, self.near_sem = plane_sem, near_sem
        self.x, self.y, self.z = grid.here()
        self.core = lax.axis_index("fsdp")
        self.spot = 2 * self.y + self.x

    def line_at(self, spot, core=None, low=None):
        core = self.core if core is None else core
        low = slice(None) if low is None else low
        return self.full.at[core, :, low, spot, :, self.cols]

    def block_at(self, z):
        return self.full.at[self.core, z // 2, lax.rem(z, 2), self.spot, :, self.cols]

    def copy(self, k, source, target, sem, dp, other_core=False):
        return pltpu.make_async_remote_copy(
            src_ref=source,
            dst_ref=target,
            send_sem=self.send_sem(k),
            recv_sem=sem,
            device_id={"dp": dp, "fsdp": 1 - self.core if other_core else self.core},
            device_id_type=MESH,
        )

    def across(self):
        return self.grid.at(1 - self.x, self.y, self.z)

    def along(self):
        return self.grid.at(self.x, 1 - self.y, self.z)

    def twin(self, k, spot):
        view = self.line_at(spot)
        own = self.grid.at(self.x, self.y, self.z)
        return self.copy(k, view, view, self.near_sem(spot), own, True)

    def move(self, k):
        line = self.line_at(self.spot)
        by_x, by_y, corner = self.spot ^ 1, self.spot ^ 2, self.spot ^ 3
        if k < 3:
            peer = self.grid.at(self.x, self.y, self.z ^ (k + 1))
            return self.copy(k, self.source, self.block_at(self.z), self.line_sem(self.z), peer)
        if k < 5:
            return self.copy(k, line, line, self.plane_sem(k - 3), (self.across, self.along)[k - 3]())
        if k in (6, 8):
            half = self.line_at(by_x, low=0) if k == 6 else self.line_at(by_y, low=1)
            return self.copy(
                k, half, half, self.plane_sem(k // 2 - 1), self.along() if k == 6 else self.across()
            )
        return self.twin(k, {5: self.spot, 7: by_x, 9: by_y, 10: corner}[k])

    def run(self, steps):
        def start(*numbers):
            for k in numbers:
                self.move(k).start()

        for step in steps:
            if step == "L":
                start(0, 1, 2)
            elif step == "F":
                for other in (1, 2, 3):
                    z = self.z ^ other
                    arrived(self.block_at(z), self.line_sem(z))
                start(3, 4, 5)
            elif step == "X":
                arrived(self.line_at(self.spot ^ 1), self.plane_sem(0))
                start(6, 7)
                arrived(self.line_at(self.spot ^ 2), self.plane_sem(1))
                start(8, 9)
            else:
                for low in (0, 1):
                    arrived(self.line_at(self.spot ^ 3, low=low), self.plane_sem(2 + low))
                start(10)

    def complete(self):
        for spot in range(4):
            arrived(self.line_at(spot, 1 - self.core), self.near_sem(spot))

    def sent(self):
        for k in range(self.SENDS):
            self.move(k).wait_send()


SMALL_ROWS = 24
TILE = 640


def flatten_rows(blocks, target):
    rows = blocks.shape[3]
    count = 16

    def step(index, carry):
        place = (index // 4, lax.rem(index // 2, 2))
        spot = 2 * lax.rem(index, 2)
        both = jnp.concatenate(
            [
                blocks[place + (spot,)].astype(jnp.float32),
                blocks[place + (spot + 1,)].astype(jnp.float32),
            ]
        )
        here = pl.ds(pl.multiple_of(index * 2 * rows, 2 * rows), 2 * rows)
        target[here, :] = both.astype(jnp.bfloat16)
        return carry

    lax.fori_loop(0, count // 2, step, 0)


PLAN = {
    "in": (("qa", "L"), ("qb", "L"), ("p", "L")),
    "product": (
        ("qa", "F"),
        ("qb", "F"),
        ("o", "L"),
        ("qa", "X"),
        ("p", "F"),
        ("qb", "X"),
        ("o", "P"),
        ("i0", "L"),
        ("qa", "C"),
        ("p", "X"),
        ("qb", "C"),
    ),
    "norm": (("p", "C"), ("o", "123"), ("i1", "L")),
    "side0": (("i0", "F"), ("i2", "L")),
    "side1": (("o", "ab"), ("i1", "F"), ("i3", "L")),
    "heads": (("i0", "X"), ("o", "c"), ("i2", "F")),
    "att": (("i1", "X"), ("i0", "C"), ("i4", "L")),
}


def forward_kernel(grid, chunk, share, refs):
    (
        tokens, gains, qk_gains, qkv_flat, proj_flat, in_flat, out_flat, ada_flat,
        cotangent, conditioning, timestep, noise_bins, listed, frequencies,
        indicator, spreader, cosines, before, after, masks,
        ada_shard, qkv_shard, proj_shard, out_shard, in_shard,
        mod, cond_float, slot_kept, output, grad_residual, grad_attn, slot_sums, gain_sum, in_bias_sum, out_bias_sum,
        first_in, mod_parts, qkv_all, proj_all, out_all, in_all, in_terms, out_terms,
        keep_one, keep_query_unit, keep_key_unit, keep_query_scale, keep_key_scale,
        keep_query, keep_key, keep_values, keep_attended,
        attn_out, residual, mod_two, mod_blocks, slot_weight, first_blocks, bin_hits,
        head_gains, qkv_bias, proj_bias, in_bias, out_bias, ada_bias,
        send_sems, line_sems, plane_sems, near_sems, out_send, out_far, out_near, own_sems, first_send, first_recv, mod_send, mod_recv, load_sems, store_sems, keep_sems,
    ) = refs
    count = grid.count
    core = lax.axis_index("fsdp")
    own = grid.at(*grid.here())
    rows, width = tokens.shape
    length = cosines.shape[0]
    hidden = in_shard.shape[1]
    steps = hidden // chunk
    out_rows, out_half = out_shard.shape
    row_share, qkv_half = qkv_shard.shape
    proj_half = proj_shard.shape[1]

    def column(index, source, full, cols):
        return Column(
            grid,
            source,
            full,
            cols,
            lambda k: send_sems.at[index, k],
            lambda z: line_sems.at[index, z],
            lambda kind: plane_sems.at[index, kind],
            lambda spot: near_sems.at[index, spot],
        )

    def in_columns(step):
        return pl.ds(pl.multiple_of(step * chunk, chunk), chunk)

    def in_piece(step):
        cols = in_columns(step)
        return column(step, in_shard.at[:, cols], in_all, cols)

    def out_block(side, block):
        start = pl.multiple_of(block * out_rows, out_rows)
        return out_all.at[side, pl.ds(start, out_rows)]

    cut = qkv_half // 256 * 128
    qkv_parts = [
        column(steps + k, qkv_shard.at[:, cols], qkv_all, cols)
        for k, cols in enumerate((slice(0, cut), slice(cut, qkv_half)))
    ]
    proj = column(steps + 2, proj_shard, proj_all, slice(0, proj_half))
    out = Piece(
        grid,
        out_shard,
        out_block,
        lambda k: out_send.at[k],
        lambda block: out_far.at[block],
        lambda block: out_near.at[block],
    )
    early = qkv_parts + [proj]
    named = {"qa": qkv_parts[0], "qb": qkv_parts[1], "p": proj, "o": out}
    named.update({"i%d" % step: in_piece(step) for step in range(steps)})
    x, y, z = grid.here()
    own_place = (core, z // 2, lax.rem(z, 2), 2 * y + x)

    def forward_at(point):
        for name, moves in PLAN.get(point, ()):
            named[name].run(moves)

    def keep_own(*shards):
        moves = [
            (qkv_shard, shards[0], qkv_all.at[own_place]),
            (proj_shard, shards[1], proj_all.at[own_place]),
            (out_shard, shards[2], out_block(core, own)),
            (in_shard, shards[3], in_all.at[own_place]),
        ]
        for legs in (slice(0, 2), slice(1, 3)):
            copies = [
                pltpu.make_async_copy(*move[legs], own_sems.at[k]) for k, move in enumerate(moves)
            ]
            for copy in copies:
                copy.start()
            for copy in copies:
                copy.wait()

    greet_all(count)
    slots = conditioning.shape[0]
    own_slot = lax.axis_index("dp") * slots
    bins = lax.broadcasted_iota(jnp.int32, (1, row_share), 1)
    for slot in range(slots):
        held = jnp.sum(
            (listed[...] == own_slot + slot).astype(jnp.float32), axis=1, keepdims=True
        )
        slot_kept[slot] = jnp.broadcast_to(held, (1, width))
        here = slice(slot, slot + 1)
        bin_hits[here, :] = (noise_bins[0:1, here] == bins).astype(jnp.float32) * held
        angles = timestep[0:1, here].astype(jnp.float32) * frequencies[...]
        embedded = jnp.concatenate([jnp.cos(angles), jnp.sin(angles)], axis=1)
        cond_float[here, :] = (
            (conditioning[here, :].astype(jnp.float32) + embedded)
            .astype(jnp.bfloat16)
            .astype(jnp.float32)
        )
    silu = swish(cond_float[...]).astype(jnp.bfloat16).astype(jnp.float32)
    below = jnp.concatenate(
        [
            jnp.sum(bin_hits[...], axis=0, keepdims=True),
            jnp.zeros((7 - slots, row_share), jnp.float32),
        ]
    )
    for block in range(count):
        found = jnp.concatenate(
            [silu[:, block * row_share : (block + 1) * row_share], below]
        )
        for side in range(PAIR):
            first_blocks[PAIR * block + side] = found

    def pick_first(other):
        return first_blocks.at[other]

    def pick(other):
        return mod_blocks.at[other]

    spread(count, pick_first, first_in, first_send, first_recv)
    forward_at("in")
    pl.run_scoped(
        keep_own,
        *(
            pltpu.VMEM(shard.shape, jnp.bfloat16)
            for shard in (qkv_shard, proj_shard, out_shard, in_shard)
        ),
    )
    head_gains[...] = jnp.concatenate([qk_gains[...]] * HEADS, axis=1)
    for flat, target in (
        (qkv_flat, qkv_bias),
        (proj_flat, proj_bias),
        (in_flat, in_bias),
        (out_flat, out_bias),
        (ada_flat, ada_bias),
    ):
        across, size = target.shape[1], flat.shape[0]
        line = flat[...].reshape(1, size)
        for row in range(size // across):
            target[row : row + 1, :] = line[:, row * across : (row + 1) * across]
    spread_wait(count, pick_first, first_in, first_send, first_recv)

    def begin(blocks, ada):
        loads = [
            pltpu.make_async_copy(first_in, blocks, load_sems.at[0]),
            pltpu.make_async_copy(ada_shard, ada, load_sems.at[1]),
        ]
        for load in loads:
            load.start()
        for load in loads:
            load.wait()
        counts = jnp.sum(blocks[...], axis=0)[slots : slots + 1, :]
        shares = jnp.where(counts > 0.0, share / jnp.maximum(counts, 1.0), 0.0)
        own_weight = jnp.sum(bin_hits[...] * shares, axis=1, keepdims=True)
        for slot in range(slots):
            slot_weight[slot] = jnp.broadcast_to(own_weight[slot : slot + 1, :], (1, width))
        every = blocks[...].reshape(-1, row_share).astype(jnp.bfloat16)
        for third in range(3):
            cols = slice(third * width, (third + 1) * width)
            found = product(every, ada[:, cols])
            for other in range(count * PAIR):
                mod_blocks[other, :, cols] = found[8 * other : 8 * other + slots]

    pl.run_scoped(
        begin,
        pltpu.VMEM(first_in.shape, jnp.float32),
        pltpu.VMEM(ada_shard.shape, jnp.bfloat16),
    )
    forward_at("first")
    spread(count, pick, mod_parts, mod_send, mod_recv)
    forward_at("product")

    spread_wait(count, pick, mod_parts, mod_send, mod_recv)
    forward_at("modwait")

    def gather_mod(parts):
        load = pltpu.make_async_copy(mod_parts, parts, load_sems.at[0])
        load.start()
        load.wait()
        for side in range(PAIR):
            total = parts[side]
            for block in range(1, count):
                total = total + parts[PAIR * block + side]
            for third in range(3):
                place = 3 * side + third
                for slot in range(total.shape[0]):
                    mod[slot, place : place + 1, :] = (
                        total[slot : slot + 1, third * width : (third + 1) * width]
                        + ada_bias[place : place + 1, :]
                    )

    pl.run_scoped(gather_mod, pltpu.VMEM(mod_parts.shape, jnp.float32))
    forward_at("mod")
    for part in qkv_parts:
        part.complete()
    forward_at("mod+")

    def attention(
        mod_one, query_unit, key_unit, query_scale, key_scale, query_turned, key_turned, values_low,
        attended_low,
    ):
        def lift(blocks, flat, raw):
            loads = [
                pltpu.make_async_copy(qkv_all.at[side], blocks.at[side], load_sems.at[side])
                for side in range(PAIR)
            ]
            for load in loads:
                load.start()

            def norm_first(here, slot, _):
                inputs = tokens[here, :].astype(jnp.float32)
                normed = inputs * norm_scale(inputs) * gains[0:1, :]
                mod_one[here, :] = (
                    normed * (1.0 + mod[slot, 1:2, :]) + mod[slot, 0:1, :]
                ).astype(jnp.bfloat16)

            row_loop(rows, length, norm_first)
            forward_at("norm")
            for side in range(PAIR):
                loads[side].wait()
                flatten_rows(blocks.at[side], flat)
                for cols in lane_tiles(qkv_half, 640):
                    raw[side, :, cols] = (
                        product(mod_one[...], flat[:, cols]) + qkv_bias[side : side + 1, cols]
                    )
                forward_at("side%d" % side)

            def heads(here, slot, there):
                query = raw[0, here, :width]
                key_vec = jnp.concatenate(
                    [raw[0, here, width:], raw[1, here, : 2 * width - qkv_half]], axis=1
                )
                values_low[here, :] = raw[1, here, 2 * width - qkv_half :].astype(jnp.bfloat16)
                tables = (cosines[there, :], before[there, :], after[there, :])
                for vector, gain, unit, scale, turned in (
                    (query, head_gains[0:1, :], query_unit, query_scale, query_turned),
                    (key_vec, head_gains[1:2, :], key_unit, key_scale, key_turned),
                ):
                    squares = product((vector * vector).astype(jnp.bfloat16), indicator[...])
                    factor = lax.rsqrt(squares * (1.0 / HEAD_DIM) + EPS)
                    scale[here, :] = factor
                    united = vector * spread_heads(factor, spreader[...])
                    unit[here, :] = united
                    turned[here, :] = turn(united * gain, *tables).astype(jnp.bfloat16)

            row_loop(rows, length, heads)

        pl.run_scoped(
            lift,
            pltpu.VMEM(qkv_all.shape, jnp.bfloat16),
            pltpu.VMEM((width, qkv_half), jnp.bfloat16),
            pltpu.VMEM((PAIR, rows, qkv_half), jnp.float32),
        )
        forward_at("heads")

        def attend(slot, carry):
            here = pl.ds(pl.multiple_of(slot * length, length), length)
            pieces = [None] * (width // 128)
            for head in range(HEADS):
                window = head_window(head)
                mask = masks[head : head + 1, window]
                scores = (
                    product_transposed(query_turned[here, window] * mask, key_turned[here, window])
                    * HEAD_DIM**-0.5
                )
                probs = softmax(scores).astype(jnp.bfloat16)
                found = product(probs, values_low[here, window] * mask)
                for tile in range(window.start // 128, window.stop // 128):
                    part = found[:, tile * 128 - window.start : (tile + 1) * 128 - window.start]
                    pieces[tile] = part if pieces[tile] is None else pieces[tile] + part
                    if (tile + 1) * 128 <= (head + 1) * HEAD_DIM:
                        attended_low[here, tile * 128 : (tile + 1) * 128] = pieces[tile].astype(
                            jnp.bfloat16
                        )
                        pieces[tile] = None
            return carry

        lax.fori_loop(0, rows // length, attend, 0)
        forward_at("att")
        proj.complete()

        def lower(blocks, flat):
            load = pltpu.make_async_copy(proj_all, blocks, load_sems.at[0])
            load.start()
            load.wait()
            for side in range(PAIR):
                flatten_rows(blocks.at[side], flat)
                attn_out[:, side * proj_half : (side + 1) * proj_half] = (
                    product(attended_low[...], flat[...]) + proj_bias[side : side + 1, :]
                )

        pl.run_scoped(
            lower,
            pltpu.VMEM(proj_all.shape, jnp.bfloat16),
            pltpu.VMEM((width, proj_half), jnp.bfloat16),
        )
        forward_at("proj")
        keeps = [
            pltpu.make_async_copy(source, target, keep_sems.at[k])
            for k, (source, target) in enumerate(
                (
                    (mod_one, keep_one),
                    (query_unit, keep_query_unit),
                    (key_unit, keep_key_unit),
                    (query_scale, keep_query_scale),
                    (key_scale, keep_key_scale),
                    (query_turned, keep_query),
                    (key_turned, keep_key),
                    (values_low, keep_values),
                    (attended_low, keep_attended),
                )
            )
        ]
        for keep in keeps:
            keep.start()

        def norm_second(here, slot, _):
            total = tokens[here, :].astype(jnp.float32) + mod[slot, 2:3, :] * attn_out[here, :]
            residual[here, :] = total
            normed = total * norm_scale(total) * gains[1:2, :]
            mod_two[here, :] = (normed * (1.0 + mod[slot, 4:5, :]) + mod[slot, 3:4, :]).astype(
                jnp.bfloat16
            )

        row_loop(rows, length, norm_second)
        for keep in keeps:
            keep.wait()

    low = pltpu.VMEM((rows, width), jnp.bfloat16)
    wide = pltpu.VMEM((rows, width), jnp.float32)
    compact = pltpu.VMEM((rows, 128), jnp.float32)
    pl.run_scoped(attention, low, wide, wide, compact, compact, low, low, low, low)
    forward_at("norm2")
    out.complete()
    forward_at("norm2+")

    def ffn(
        turned_two, grad_low, grad_half, lifted_grad, ffn_value,
        in_blocks, in_chunk, out_chunk, in_stage, out_stage,
    ):
        def stores(step, slot):
            return [
                pltpu.make_async_copy(
                    in_stage.at[slot], in_terms.at[:, :, :, in_columns(step)], store_sems.at[slot, 0]
                ),
                pltpu.make_async_copy(
                    out_stage.at[slot], out_terms.at[:, in_columns(step)], store_sems.at[slot, 1]
                ),
            ]

        def prepare(here, slot, _):
            grad_out = (cotangent[here, :].astype(jnp.float32) * slot_weight[slot]).astype(
                jnp.bfloat16
            )
            grad_low[here, :] = grad_out
            grad_ffn = (mod[slot, 5:6, :] * grad_out.astype(jnp.float32)).astype(jnp.bfloat16)
            grad_half[0, here, :] = grad_ffn[:, :out_half]
            grad_half[1, here, :] = grad_ffn[:, out_half:]

        row_loop(rows, length, prepare)
        turned_two[...] = mod_two[...].T
        for side in range(PAIR):
            out_bias_sum[side : side + 1, :] = jnp.sum(
                grad_half[side].astype(jnp.float32), axis=0, keepdims=True
            )
        lifted_grad[...] = jnp.zeros_like(lifted_grad)
        ffn_value[...] = jnp.zeros_like(ffn_value)

        def loads(step):
            here = in_columns(step)
            return [
                pltpu.make_async_copy(in_all.at[:, :, :, :, :, here], in_blocks, load_sems.at[0]),
                pltpu.make_async_copy(
                    out_all.at[:, here], out_chunk.at[lax.rem(step, 2)], load_sems.at[1]
                ),
            ]

        def fetch(step):
            in_piece(step).complete()
            for load in loads(step):
                load.start()

        forward_at("prep")
        fetch(0)

        def step_body(step, carry):
            slot = lax.rem(step, 2)

            for moves, ahead in (("L", 5), ("F", 3), ("X", 2), ("C", 1)):

                @pl.when(step + ahead < steps)
                def _(moves=moves, ahead=ahead):
                    in_piece(step + ahead).run(moves)

            here = in_columns(step)
            for load in loads(step):
                load.wait()
            for side in range(PAIR):
                flatten_rows(in_blocks.at[side], in_chunk.at[side])
            gate_part = product(mod_two[...], in_chunk[0]) + in_bias[0:1, here]
            up_part = product(mod_two[...], in_chunk[1]) + in_bias[1:2, here]
            sigmoid = 1.0 / (1.0 + jnp.exp(-gate_part))
            swished = gate_part * sigmoid
            hidden_low = (swished * up_part).astype(jnp.bfloat16)
            grad_hidden = product_transposed(grad_half[0], out_chunk[slot, 0]) + product_transposed(
                grad_half[1], out_chunk[slot, 1]
            )
            grad_gate = (
                grad_hidden * up_part * (sigmoid * (1.0 + gate_part * (1.0 - sigmoid)))
            ).astype(jnp.bfloat16)
            grad_up = (grad_hidden * swished).astype(jnp.bfloat16)
            for side in range(PAIR):
                ffn_value[side] += product(hidden_low, out_chunk[slot, side])
            lifted_grad[...] += product_transposed(grad_gate, in_chunk[0])
            lifted_grad[...] += product_transposed(grad_up, in_chunk[1])

            @pl.when(step + 1 < steps)
            def _():
                fetch(step + 1)

            @pl.when(step >= 2)
            def _():
                for store in stores(step - 2, slot):
                    store.wait()

            for side, grad in ((0, grad_gate), (1, grad_up)):
                in_bias_sum[side : side + 1, here] = jnp.sum(
                    grad.astype(jnp.float32), axis=0, keepdims=True
                )
                terms = product(turned_two[...], grad)
                for block in range(count):
                    in_stage[slot, side, block] = terms[
                        block * row_share : (block + 1) * row_share
                    ].astype(jnp.bfloat16)
            turned_hidden = hidden_low.T
            for side in range(PAIR):
                out_stage[slot, side, :, :out_half] = product(
                    turned_hidden, grad_half[side]
                ).astype(jnp.bfloat16)
            for store in stores(step, slot):
                store.start()
            return carry

        lax.fori_loop(0, steps, step_body, 0)
        slot_sums[...] = jnp.zeros_like(slot_sums)
        gain_sum[...] = jnp.zeros_like(gain_sum)

        def finish(here, slot, _):
            value = (
                jnp.concatenate([ffn_value[0, here, :], ffn_value[1, here, :]], axis=1)
                + out_bias[...]
            )
            total = residual[here, :]
            output[here, :] = ((total + mod[slot, 5:6, :] * value) * slot_kept[slot]).astype(
                jnp.bfloat16
            )
            grad_out = grad_low[here, :].astype(jnp.float32)
            factor = norm_scale(total)
            unit = total * factor
            normed = unit * gains[1:2, :]
            grad_mod = lifted_grad[here, :]
            grad_normed = grad_mod * (1.0 + mod[slot, 4:5, :])
            gradient = grad_out + norm_back(grad_normed * gains[1:2, :], unit, factor)
            grad_residual[here, :] = gradient
            grad_attn[here, :] = (mod[slot, 2:3, :] * gradient).astype(jnp.bfloat16)
            for place, terms in (
                (2, gradient * attn_out[here, :]),
                (3, grad_mod),
                (4, grad_mod * normed),
                (5, grad_out * value),
            ):
                slot_sums[slot, place : place + 1, :] += jnp.sum(terms, axis=0, keepdims=True)
            gain_sum[...] += jnp.sum(grad_normed * unit, axis=0, keepdims=True)

        row_loop(rows, length, finish)
        for step in range(steps - 2, steps):
            for store in stores(step, step % 2):
                store.wait()

    pl.run_scoped(
        ffn,
        pltpu.VMEM((width, rows), jnp.bfloat16),
        low,
        pltpu.VMEM((PAIR, rows, out_half), jnp.bfloat16),
        wide,
        pltpu.VMEM((PAIR, rows, out_half), jnp.float32),
        pltpu.VMEM(in_all.shape[:5] + (chunk,), jnp.bfloat16),
        pltpu.VMEM((PAIR, width, chunk), jnp.bfloat16),
        pltpu.VMEM((2, PAIR, chunk, out_half), jnp.bfloat16),
        pltpu.VMEM((2, PAIR, count, row_share, chunk), jnp.bfloat16),
        pltpu.VMEM((2, PAIR, chunk, TILE), jnp.bfloat16),
    )
    for part in early + [out]:
        part.sent()

    def sent(step, carry):
        in_piece(step).sent()
        return carry

    lax.fori_loop(0, steps, sent, 0)


def forward_call(grid, collective, share, tokens, small, tables, ada, shards):
    rows, width = tokens.shape
    count = grid.count
    total = count * PAIR
    qkv, proj, ffn_in, ffn_out = shards
    hidden, out_half = ffn_in.shape[1], ffn_out.shape[1]
    chunk = 512
    steps = hidden // chunk
    f32, bf16 = jnp.float32, jnp.bfloat16
    wide = jax.ShapeDtypeStruct((rows, width), f32)
    low = jax.ShapeDtypeStruct((rows, width), bf16)
    compact = jax.ShapeDtypeStruct((rows, 128), f32)
    slots = small[8].shape[0]
    mod_shape = (total, slots, ada.shape[1])

    def blocks(shard):
        return jax.ShapeDtypeStruct((PAIR, 2, 2, 4) + shard.shape, bf16)

    flat_out = jax.ShapeDtypeStruct((PAIR, count * ffn_out.shape[0], out_half), bf16)
    outs = [
        jax.ShapeDtypeStruct((slots, 6, width), f32),
        jax.ShapeDtypeStruct((slots, width), f32),
        jax.ShapeDtypeStruct((slots, 1, width), f32),
        low,
        wide,
        low,
        jax.ShapeDtypeStruct((slots, 6, width), f32),
        jax.ShapeDtypeStruct((1, width), f32),
        jax.ShapeDtypeStruct((PAIR, hidden), f32),
        jax.ShapeDtypeStruct((PAIR, out_half), f32),
        jax.ShapeDtypeStruct((total, 8, qkv.shape[0]), f32),
        jax.ShapeDtypeStruct(mod_shape, f32),
        blocks(qkv),
        blocks(proj),
        flat_out,
        blocks(ffn_in),
        jax.ShapeDtypeStruct((PAIR, count) + ffn_in.shape, bf16),
        jax.ShapeDtypeStruct((PAIR, count * ffn_out.shape[0], TILE), bf16),
    ] + [low, wide, wide, compact, compact, low, low, low, low]
    pieces = 3 + steps
    return pl.pallas_call(
        lambda *refs: forward_kernel(grid, chunk, share, refs),
        out_shape=outs,
        in_specs=[WHOLE] * 20 + [ANY] * 5,
        out_specs=[WHOLE] * 10 + [ANY] * 17,
        scratch_shapes=[
            pltpu.VMEM((rows, width), f32),
            pltpu.VMEM((rows, width), f32),
            pltpu.VMEM((rows, width), bf16),
            pltpu.VMEM(mod_shape, f32),
            pltpu.VMEM((slots, 1, width), f32),
            pltpu.VMEM((total, 8, qkv.shape[0]), f32),
            pltpu.VMEM((slots, qkv.shape[0]), f32),
            pltpu.VMEM((2, width), f32),
            pltpu.VMEM((PAIR, qkv.shape[1]), f32),
            pltpu.VMEM((PAIR, proj.shape[1]), f32),
            pltpu.VMEM((PAIR, hidden), f32),
            pltpu.VMEM((1, width), f32),
            pltpu.VMEM((6, width), f32),
            pltpu.SemaphoreType.DMA((pieces, Column.SENDS)),
            pltpu.SemaphoreType.DMA((pieces, 4)),
            pltpu.SemaphoreType.DMA((pieces, 4)),
            pltpu.SemaphoreType.DMA((pieces, 4)),
            pltpu.SemaphoreType.DMA((Piece.SENDS,)),
            pltpu.SemaphoreType.DMA((count,)),
            pltpu.SemaphoreType.DMA((count,)),
            pltpu.SemaphoreType.DMA((4,)),
            pltpu.SemaphoreType.DMA((total,)),
            pltpu.SemaphoreType.DMA((total,)),
            pltpu.SemaphoreType.DMA((total,)),
            pltpu.SemaphoreType.DMA((total,)),
            pltpu.SemaphoreType.DMA((2,)),
            pltpu.SemaphoreType.DMA((2, 2)),
            pltpu.SemaphoreType.DMA((9,)),
        ],
        compiler_params=pltpu.CompilerParams(
            collective_id=collective, has_side_effects=True, vmem_limit_bytes=56 * 2**20
        ),
    )(tokens, *small, *tables, ada, qkv, proj, ffn_out, ffn_in)


class Total:
    HELD, PAIRED, PLANE, LINE = 4, 2, 3, 2
    SIBLING, ACROSS, ALONG, STEPS = 0, 1, 2, 2

    def __init__(self, grid, index, count, source, rows, cols, deliver, buffers):
        self.grid, self.index, self.count = grid, index, count
        self.source, self.deliver = source, deliver
        self.rows, self.cols = rows, cols
        (
            self.held_all, self.paired_all, self.turned_all, self.plane_all, self.line_all,
            self.result_all, self.send_sems, self.load_sems, self.pair_sems, self.turn_sems,
            self.plane_sems, self.line_sems, self.credits,
        ) = buffers
        self.x, self.y, self.z = grid.here()
        self.core = lax.axis_index("fsdp")

    def cut(self, ref):
        lead = (slice(None),) * (len(ref.shape) - 2)
        return ref.at[lead + (slice(0, self.rows), slice(0, self.cols))]

    @property
    def held(self):
        return self.cut(self.held_all.at[self.index % self.HELD])

    @property
    def paired(self):
        return self.cut(self.paired_all.at[self.index % self.PAIRED])

    @property
    def turned(self):
        return self.cut(self.turned_all.at[self.index % self.PLANE])

    @property
    def plane(self):
        return self.cut(self.plane_all.at[self.index % self.PLANE])

    @property
    def line(self):
        return self.cut(self.line_all.at[self.index % self.LINE])

    @property
    def result(self):
        return self.cut(self.result_all.at[self.index % self.LINE])

    def place_of(self, kind):
        if kind == self.SIBLING:
            return self.grid.at(self.x, self.y, self.z), 1 - self.core
        if kind == self.ACROSS:
            return self.grid.at(1 - self.x, self.y, self.z), self.core
        if kind == self.ALONG:
            return self.grid.at(self.x, 1 - self.y, self.z), self.core
        return self.grid.at(self.x, self.y, self.z ^ (kind - self.STEPS)), self.core

    def give(self, kinds, ahead):
        if self.index + ahead < self.count:
            for kind in kinds:
                dp, core = self.place_of(kind)
                pl.semaphore_signal(
                    self.credits.at[kind],
                    inc=1,
                    device_id={"dp": dp, "fsdp": core},
                    device_id_type=MESH,
                )

    def take(self, kinds, ahead):
        if self.index >= ahead:
            for kind in kinds:
                pl.semaphore_wait(self.credits.at[kind], 1)

    def send(self, k, source, target, recv_sem, dp):
        pltpu.make_async_remote_copy(
            src_ref=source,
            dst_ref=target,
            send_sem=self.send_sems.at[self.index, k],
            recv_sem=recv_sem,
            device_id={"dp": dp, "fsdp": self.core},
            device_id_type=MESH,
        ).start()

    def pair_copy(self):
        return pltpu.make_async_remote_copy(
            src_ref=self.source(1 - self.core),
            dst_ref=self.paired,
            send_sem=self.send_sems.at[self.index, 15],
            recv_sem=self.pair_sems.at[self.index],
            device_id={"dp": self.grid.at(self.x, self.y, self.z), "fsdp": 1 - self.core},
            device_id_type=MESH,
        )

    def begin(self):
        self.take((self.SIBLING,), self.PAIRED)
        self.pair_copy().start()
        pltpu.make_async_copy(
            self.source(self.core), self.held, self.load_sems.at[self.index]
        ).start()

    def sent(self):
        block = self.held.at[0]
        for k in range(15):
            arrived(block, self.send_sems.at[self.index, k])
        self.pair_copy().wait_send()

    def pair_sum(self, block):
        held, paired = self.held, self.paired
        held[block] = (
            held[block].astype(jnp.float32) + paired[block].astype(jnp.float32)
        ).astype(jnp.bfloat16)

    def sides(self, place, odd):
        across = self.grid.at(1 - self.x, self.y, place)
        along = self.grid.at(self.x, 1 - self.y, place)
        return odd * across + (1 - odd) * along, odd * along + (1 - odd) * across

    def start(self):
        arrived(self.held, self.load_sems.at[self.index])
        arrived(self.paired, self.pair_sems.at[self.index])
        self.take((self.ACROSS, self.ALONG), self.PLANE)
        across = self.grid.at(1 - self.x, self.y, self.z)
        along = self.grid.at(self.x, 1 - self.y, self.z)
        held, turned, plane = self.held, self.turned, self.plane

        def corner(step, carry):
            place = self.z ^ (3 - step)
            odd = lax.rem(place, 2)
            block = self.grid.at(1 - self.x, 1 - self.y, place)
            self.pair_sum(block)
            self.send(
                step,
                held.at[block],
                turned.at[place],
                self.turn_sems.at[self.index, place],
                odd * across + (1 - odd) * along,
            )
            return carry

        lax.fori_loop(0, 4, corner, 0)

        def side(step, carry):
            place = self.z ^ (3 - step)
            odd = lax.rem(place, 2)
            passed, added = self.sides(place, odd)
            self.pair_sum(passed)
            self.send(
                4 + step,
                held.at[passed],
                plane.at[1 - odd, place],
                self.plane_sems.at[self.index, 1 - odd, place],
                odd * across + (1 - odd) * along,
            )
            self.pair_sum(added)
            return carry

        lax.fori_loop(0, 4, side, 0)

        def column(step, carry):
            self.pair_sum(self.grid.at(self.x, self.y, step))
            return carry

        lax.fori_loop(0, 4, column, 0)
        self.give((self.SIBLING,), self.PAIRED)

    def turn(self):
        held, turned, plane = self.held, self.turned, self.plane
        across = self.grid.at(1 - self.x, self.y, self.z)
        along = self.grid.at(self.x, 1 - self.y, self.z)

        def step_body(step, carry):
            place = self.z ^ (3 - step)
            odd = lax.rem(place, 2)
            _, block = self.sides(place, odd)
            arrived(turned.at[place], self.turn_sems.at[self.index, place])
            held[block] = (
                held[block].astype(jnp.float32) + turned[place].astype(jnp.float32)
            ).astype(jnp.bfloat16)
            self.send(
                8 + step,
                held.at[block],
                plane.at[odd, place],
                self.plane_sems.at[self.index, odd, place],
                odd * along + (1 - odd) * across,
            )
            return carry

        lax.fori_loop(0, 4, step_body, 0)

    def column(self):
        held, plane, line = self.held, self.plane, self.line
        self.take([self.STEPS + step for step in (1, 2, 3)], self.LINE)

        def total(place):
            for kind in (0, 1):
                arrived(plane.at[kind, place], self.plane_sems.at[self.index, kind, place])
            return (
                held[self.grid.at(self.x, self.y, place)].astype(jnp.float32)
                + plane[0, place].astype(jnp.float32)
                + plane[1, place].astype(jnp.float32)
            )

        def step_body(step, carry):
            place = self.z ^ (3 - step)
            block = self.grid.at(self.x, self.y, place)
            held[block] = total(place).astype(jnp.bfloat16)
            self.send(
                12 + step,
                held.at[block],
                line.at[self.z],
                self.line_sems.at[self.index, self.z],
                block,
            )
            return carry

        lax.fori_loop(0, 3, step_body, 0)
        self.result[...] = total(self.z)
        self.give((self.ACROSS, self.ALONG), self.PLANE)

    def end(self):
        line = self.line
        total = self.result[...]
        for step in (1, 2, 3):
            place = self.z ^ step
            arrived(line.at[place], self.line_sems.at[self.index, place])
            total = total + line[place].astype(jnp.float32)
        self.deliver(total)
        self.give([self.STEPS + step for step in (1, 2, 3)], self.LINE)


class Relay:
    def __init__(self, parts):
        self.parts, self.slot = parts, 0

    def part(self, back):
        place = self.slot - back
        return self.parts[place] if 0 <= place < len(self.parts) else None

    def more(self, slots=1):
        for _ in range(slots):
            for back, step in ((4, "end"), (3, "column"), (2, "turn"), (1, "start")):
                if self.part(back):
                    getattr(self.part(back), step)()
            if self.part(0):
                if self.part(Total.HELD):
                    self.part(Total.HELD).sent()
                self.part(0).begin()
            self.slot += 1

    def finish(self):
        while self.slot < len(self.parts) + 4:
            self.more()
        for part in self.parts[-Total.HELD :]:
            part.sent()


def backward_kernel(grid, refs):
    (
        mod, cond_float, gains, qk_gains, indicator, spreader, cosines, before, after, masks,
        slot_kept,
        late_sums, late_gain, in_bias_sum, out_bias_sum, silu_rows,
        tokens, keep_one, keep_query_unit, keep_key_unit, keep_query_scale, keep_key_scale,
        keep_query, keep_key, keep_values, keep_attended, grad_residual_hbm, grad_attn_hbm,
        qkv_all, proj_all, in_terms, out_terms, ada_shard,
        input_grad, in_grad, out_grad, qkv_grad, proj_grad, ada_grad, cond_grad,
        ada_bias_grad, qkv_bias_grad, proj_bias_grad, in_bias_grad, out_bias_grad, norm_grad,
        head_grad,
        cond_parts, every_mod, qkv_terms, proj_terms,
        held, paired, turned_in, plane_in, line_in, result, small_in, mod_halves, cond_blocks, small,
        head_gains,
        send_sems, load_sems, pair_sems, turn_sems, plane_sems, line_sems, credits,
        small_send, small_recv, mod_send, mod_recv, cond_send, cond_recv, local_sems, store_sems,
    ) = refs
    count = grid.count
    rows, width = tokens.shape
    length = cosines.shape[0]
    slots = rows // length
    hidden = in_grad.shape[1]
    row_share, qkv_half = qkv_all.shape[4:]
    proj_half = proj_all.shape[5]
    third = out_grad.shape[0] // 3
    out_half = out_grad.shape[1]
    x, y, z = grid.here()
    core = lax.axis_index("fsdp")
    greet_all(count)
    head_gains[...] = jnp.concatenate([qk_gains[...]] * HEADS, axis=1)

    buffers = (
        held, paired, turned_in, plane_in, line_in, result,
        send_sems, load_sems, pair_sems, turn_sems, plane_sems, line_sems, credits,
    )
    plans = []
    for cols in lane_tiles(hidden, TILE):

        def deliver(total, cols=cols):
            in_grad[:, cols] = total

        plans.append(
            (
                lambda side, cols=cols: in_terms.at[side, :, :, cols],
                row_share,
                cols.stop - cols.start,
                deliver,
            )
        )
    for place in range(3):
        here = slice(place * third, (place + 1) * third)

        def deliver(total, here=here):
            out_grad[here, :] = total[:, :out_half]

        plans.append((lambda side, here=here: out_terms.at[side, :, here], third, TILE, deliver))

    def deliver_proj(total):
        proj_grad[...] = total[:, :proj_half]

    plans.append((lambda side: proj_terms.at[side], row_share, TILE, deliver_proj))
    for cols in lane_tiles(qkv_half, TILE):

        def deliver(total, cols=cols):
            qkv_grad[:, cols] = total[:, : cols.stop - cols.start]

        wide_cols = slice(cols.start, cols.start + TILE)
        plans.append(
            (
                lambda side, wide_cols=wide_cols: qkv_terms.at[side, :, :, wide_cols],
                row_share,
                TILE,
                deliver,
            )
        )
    relay = Relay(
        [Total(grid, index, len(plans), *plan, buffers) for index, plan in enumerate(plans)]
    )
    relay.more(2)

    def fetch(*pairs):
        copies = [
            pltpu.make_async_copy(source, target, local_sems.at[k])
            for k, (source, target) in enumerate(pairs)
        ]
        for copy in copies:
            copy.start()
        return copies

    def body(grad_half, lifted_grad):
        def heads_part(grad_query, grad_key, grad_values, grad_attended):
            def first(blocks, flat, attended_low, grad_attn, turned, stage):
                loads = fetch(
                    (keep_attended, attended_low), (grad_attn_hbm, grad_attn), (proj_all, blocks)
                )
                for load in loads:
                    load.wait()
                turned[...] = attended_low[...].T
                for side in range(PAIR):
                    cols = slice(side * proj_half, (side + 1) * proj_half)
                    small[9:10, cols] = jnp.sum(
                        grad_attn[:, cols].astype(jnp.float32), axis=0, keepdims=True
                    )
                    flatten_rows(blocks.at[side], flat)
                    found = product_transposed(grad_attn[:, cols], flat[...])
                    if side == 0:
                        grad_query[...] = found
                    else:
                        grad_attended[...] = (grad_query[...] + found).astype(jnp.bfloat16)
                    terms = product(turned[...], grad_attn[:, cols])
                    for block in range(count):
                        stage[side, block, :, :proj_half] = terms[
                            block * row_share : (block + 1) * row_share
                        ].astype(jnp.bfloat16)
                store = pltpu.make_async_copy(stage, proj_terms, store_sems.at[0])
                store.start()
                store.wait()

            low = pltpu.VMEM((rows, width), jnp.bfloat16)
            pl.run_scoped(
                first,
                pltpu.VMEM(proj_all.shape, jnp.bfloat16),
                pltpu.VMEM((width, proj_half), jnp.bfloat16),
                low,
                low,
                pltpu.VMEM((width, rows), jnp.bfloat16),
                pltpu.VMEM((PAIR, count, row_share, TILE), jnp.bfloat16),
            )
            relay.more(1)

            def second(query_turned, key_turned, values_low):
                loads = fetch(
                    (keep_query, query_turned), (keep_key, key_turned), (keep_values, values_low)
                )
                for load in loads:
                    load.wait()

                def attend(slot):
                    here = slice(slot * length, (slot + 1) * length)
                    pieces = [[None] * (width // 128) for _ in range(3)]
                    for head in range(HEADS):
                        window = head_window(head)
                        mask = masks[head : head + 1, window]
                        query = query_turned[here, window] * mask
                        key_vec = key_turned[here, window]
                        value = values_low[here, window]
                        grad = grad_attended[here, window] * mask
                        probs = softmax(product_transposed(query, key_vec) * HEAD_DIM**-0.5)
                        grad_probs = product_transposed(grad, value)
                        grad_scores = (
                            probs
                            * (grad_probs - jnp.sum(probs * grad_probs, axis=-1, keepdims=True))
                        ).astype(jnp.bfloat16)
                        founds = (
                            product(grad_scores, key_vec * mask) * HEAD_DIM**-0.5,
                            transposed_product(grad_scores, query) * HEAD_DIM**-0.5,
                            transposed_product(probs.astype(jnp.bfloat16), grad),
                        )
                        for kind, (found, target) in enumerate(
                            zip(founds, (grad_query, grad_key, grad_values))
                        ):
                            for tile in range(window.start // 128, window.stop // 128):
                                begin = tile * 128 - window.start
                                part = found[:, begin : begin + 128]
                                kept = pieces[kind][tile]
                                kept = part if kept is None else kept + part
                                pieces[kind][tile] = kept
                                if (tile + 1) * 128 <= (head + 1) * HEAD_DIM:
                                    target[here, tile * 128 : (tile + 1) * 128] = kept

                for slot in range(slots):
                    attend(slot)
                    relay.more(1)

            pl.run_scoped(second, low, low, low)

            def third_part(query_unit, key_unit, query_scale, key_scale):
                loads = fetch(
                    (keep_query_unit, query_unit),
                    (keep_key_unit, key_unit),
                    (keep_query_scale, query_scale),
                    (keep_key_scale, key_scale),
                )
                for load in loads:
                    load.wait()
                small[13:15, :] = jnp.zeros((2, width), jnp.float32)

                def heads(here, slot, there):
                    tables = (cosines[there, :], before[there, :], after[there, :])
                    founds = []
                    for kind, (grad, gain, unit, scale) in enumerate(
                        (
                            (grad_query, head_gains[0:1, :], query_unit, query_scale),
                            (grad_key, head_gains[1:2, :], key_unit, key_scale),
                        )
                    ):
                        normed = turn(grad[here, :], *tables, sign=-1.0)
                        united = unit[here, :]
                        small[13 + kind : 14 + kind, :] += jnp.sum(
                            normed * united, axis=0, keepdims=True
                        )
                        normed = normed * gain
                        means = product(
                            (normed * united).astype(jnp.bfloat16), indicator[...]
                        ) * (1.0 / HEAD_DIM)
                        founds.append(
                            spread_heads(scale[here, :], spreader[...])
                            * (normed - united * spread_heads(means, spreader[...]))
                        )
                    cut = qkv_half - width
                    grad_half[0, here, :width] = founds[0].astype(jnp.bfloat16)
                    grad_half[0, here, width:] = founds[1][:, :cut].astype(jnp.bfloat16)
                    grad_half[1, here, : width - cut] = founds[1][:, cut:].astype(jnp.bfloat16)
                    grad_half[1, here, width - cut :] = grad_values[here, :].astype(jnp.bfloat16)

                row_loop(rows, length, heads)

            compact = pltpu.VMEM((rows, 128), jnp.float32)
            wide = pltpu.VMEM((rows, width), jnp.float32)
            pl.run_scoped(third_part, wide, wide, compact, compact)

        wide = pltpu.VMEM((rows, width), jnp.float32)
        low = pltpu.VMEM((rows, width), jnp.bfloat16)
        pl.run_scoped(heads_part, wide, wide, wide, low)
        relay.more(1)

        def fourth(mod_one, turned, blocks, flat, stage):
            fetch((keep_one, mod_one))[0].wait()
            turned[...] = mod_one[...].T
            number = 0
            stores = []
            for side in range(PAIR):
                fetch((qkv_all.at[side], blocks))[0].wait()
                flatten_rows(blocks, flat)
                for tile in range(3):
                    sums = jnp.sum(
                        grad_half[side, :, tile * 576 : (tile + 1) * 576].astype(jnp.float32),
                        axis=0,
                        keepdims=True,
                    )
                    start = side * qkv_half + tile * 576
                    small[
                        6 + start // width : 7 + start // width,
                        start % width : start % width + 576,
                    ] = sums
                for cols in lane_tiles(width, 384):
                    found = product_transposed(grad_half[side], flat[cols, :])
                    if side == 0:
                        lifted_grad[:, cols] = found
                    else:
                        lifted_grad[:, cols] += found
                for cols in lane_tiles(qkv_half, TILE):
                    terms = product(turned[...], grad_half[side, :, cols])
                    if number >= 2:
                        stores[number - 2].wait()
                    for block in range(count):
                        stage[number % 2, block, :, : cols.stop - cols.start] = terms[
                            block * row_share : (block + 1) * row_share
                        ].astype(jnp.bfloat16)
                    stores.append(
                        pltpu.make_async_copy(
                            stage.at[number % 2],
                            qkv_terms.at[side, :, :, cols.start : cols.start + TILE],
                            store_sems.at[number % 2],
                        )
                    )
                    stores[-1].start()
                    number += 1
                if side == 0:
                    relay.more(1)
            for store in stores[-2:]:
                store.wait()

        pl.run_scoped(
            fourth,
            low,
            pltpu.VMEM((width, rows), jnp.bfloat16),
            pltpu.VMEM(qkv_all.shape[1:], jnp.bfloat16),
            pltpu.VMEM((width, qkv_half), jnp.bfloat16),
            pltpu.VMEM((2, count, row_share, TILE), jnp.bfloat16),
        )
        relay.more(1)

        def last(token_rows, grad_residual, early):
            for load in fetch((tokens, token_rows), (grad_residual_hbm, grad_residual)):
                load.wait()
            early[...] = late_sums[...]
            small[11:12, :] = jnp.zeros((1, width), jnp.float32)
            small[12:13, :] = late_gain[...]

            def finish(here, slot, _):
                inputs = token_rows[here, :].astype(jnp.float32)
                factor = norm_scale(inputs)
                unit = inputs * factor
                normed = unit * gains[0:1, :]
                grad_mod = lifted_grad[here, :]
                grad_normed = grad_mod * (1.0 + mod[slot, 1:2, :])
                gradient = grad_residual[here, :] + norm_back(
                    grad_normed * gains[0:1, :], unit, factor
                )
                input_grad[here, :] = (gradient * slot_kept[slot]).astype(jnp.bfloat16)
                for place, terms in ((0, grad_mod), (1, grad_mod * normed)):
                    early[slot, place : place + 1, :] += jnp.sum(terms, axis=0, keepdims=True)
                small[11:12, :] += jnp.sum(grad_normed * unit, axis=0, keepdims=True)

            row_loop(rows, length, finish)
            for place in range(6):
                low_sums = jnp.concatenate(
                    [early[slot, place : place + 1, :] for slot in range(slots)]
                ).astype(jnp.bfloat16)
                mod_halves[place // 3, :, (place % 3) * width : (place % 3 + 1) * width] = low_sums
                small[place : place + 1, :] = jnp.sum(
                    low_sums.astype(jnp.float32), axis=0, keepdims=True
                )

        pl.run_scoped(last, low, wide, pltpu.VMEM(late_sums.shape, jnp.float32))

    pl.run_scoped(
        body,
        pltpu.VMEM((PAIR, rows, qkv_half), jnp.bfloat16),
        pltpu.VMEM((rows, width), jnp.float32),
    )

    def pick(other):
        return mod_halves.at[lax.rem(other, PAIR)]

    spread(count, pick, every_mod, mod_send, mod_recv)
    for side in range(PAIR):
        small[10:11, side * out_half : (side + 1) * out_half] = out_bias_sum[side : side + 1, :]
        for part in range(3):
            wide_part = min(width, hidden - part * width)
            row = 15 + 3 * side + part
            if wide_part < width:
                small[row : row + 1, :] = jnp.zeros((1, width), jnp.float32)
            small[row : row + 1, :wide_part] = in_bias_sum[
                side : side + 1, part * width : part * width + wide_part
            ]
    small[21:, :] = jnp.zeros((SMALL_ROWS - 21, width), jnp.float32)
    peers = [
        (grid.at(x, y, z), 1 - core),
        (grid.at(1 - x, y, z), core),
        (grid.at(x, 1 - y, z), core),
        (grid.at(x, y, z ^ 1), core),
        (grid.at(x, y, z ^ 2), core),
    ]
    for k, (dp, other) in enumerate(peers):
        copy = pltpu.make_async_remote_copy(
            src_ref=small,
            dst_ref=small_in.at[k],
            send_sem=small_send.at[k],
            recv_sem=small_recv.at[k],
            device_id={"dp": dp, "fsdp": other},
            device_id_type=MESH,
        )
        copy.start()
        relay.more(1)
        copy.wait()
        small[...] = small[...] + small_in[k]
    spread_wait(count, pick, every_mod, mod_send, mod_recv)

    def condition(parts, flat, ada):
        for load in fetch((every_mod, parts), (ada_shard, ada)):
            load.wait()
        for other in range(count * PAIR):
            flat[slots * other : slots * (other + 1), :] = parts[other].astype(jnp.float32)
        grads = flat[...].astype(jnp.bfloat16)
        ada_grad[...] = transposed_product(silu_rows[...], grads)
        found = product_transposed(grads, ada[...])
        for other in range(count * PAIR):
            cond_blocks[other] = found[slots * other : slots * (other + 1), :]

    pl.run_scoped(
        condition,
        pltpu.VMEM(every_mod.shape, jnp.bfloat16),
        pltpu.VMEM((count * PAIR * slots, every_mod.shape[2]), jnp.float32),
        pltpu.VMEM(ada_shard.shape, jnp.bfloat16),
    )

    def pick_cond(other):
        return cond_blocks.at[other]

    spread(count, pick_cond, cond_parts, cond_send, cond_recv)
    relay.finish()
    for target, row in ((ada_bias_grad, 0), (qkv_bias_grad, 6), (proj_bias_grad, 9), (out_bias_grad, 10)):
        for part in range(target.shape[0] // width):
            target[pl.ds(part * width, width)] = small[row + part]
    for side in range(PAIR):
        for part in range(3):
            wide_part = min(width, hidden - part * width)
            in_bias_grad[pl.ds(side * hidden + part * width, wide_part)] = small[
                15 + 3 * side + part, :wide_part
            ]
    norm_grad[...] = small[11:13, :]
    sums = small[13:15, :]
    found = sums[:, :HEAD_DIM]
    for head in range(1, HEADS):
        found = found + sums[:, head * HEAD_DIM : (head + 1) * HEAD_DIM]
    head_grad[...] = found
    spread_wait(count, pick_cond, cond_parts, cond_send, cond_recv)

    def settle(parts):
        fetch((cond_parts, parts))[0].wait()
        found = jnp.concatenate(
            [parts[PAIR * block] + parts[PAIR * block + 1] for block in range(count)], axis=1
        )
        kept = jnp.concatenate([slot_kept[slot] for slot in range(slots)])
        cond_grad[...] = found * swish_slope(cond_float[...]) * kept

    pl.run_scoped(settle, pltpu.VMEM(cond_parts.shape, jnp.float32))


def backward_call(grid, collective, whole, parts):
    count = grid.count
    total = count * PAIR
    f32, bf16 = jnp.float32, jnp.bfloat16
    tokens, grad_residual = parts[0], parts[10]
    qkv_all, proj_all, in_terms, out_terms, ada = parts[12:]
    rows, width = tokens.shape
    row_share = qkv_all.shape[4]
    slots = whole[0].shape[0]
    half_width = 3 * width
    qkv_half, proj_half, hidden = qkv_all.shape[5], proj_all.shape[5], in_terms.shape[3]
    out_rows = out_terms.shape[2]
    qkv_tiles = len(lane_tiles(qkv_half, TILE))
    pieces = len(lane_tiles(hidden, TILE)) + 3 + 1 + qkv_tiles
    block = (row_share, TILE)
    return pl.pallas_call(
        lambda *refs: backward_kernel(grid, refs),
        out_shape=[
            jax.ShapeDtypeStruct((rows, width), bf16),
            jax.ShapeDtypeStruct((row_share, hidden), f32),
            jax.ShapeDtypeStruct((out_rows, proj_half), f32),
            jax.ShapeDtypeStruct((row_share, qkv_half), f32),
            jax.ShapeDtypeStruct((row_share, proj_half), f32),
            jax.ShapeDtypeStruct(ada.shape, f32),
            jax.ShapeDtypeStruct((slots, width), f32),
            jax.ShapeDtypeStruct((6 * width,), f32),
            jax.ShapeDtypeStruct((PAIR * qkv_half,), f32),
            jax.ShapeDtypeStruct((width,), f32),
            jax.ShapeDtypeStruct((PAIR * hidden,), f32),
            jax.ShapeDtypeStruct((width,), f32),
            jax.ShapeDtypeStruct((2, width), f32),
            jax.ShapeDtypeStruct((2, HEAD_DIM), f32),
            jax.ShapeDtypeStruct((total, slots, row_share), f32),
            jax.ShapeDtypeStruct((total, slots, half_width), bf16),
            jax.ShapeDtypeStruct((PAIR, count, row_share, qkv_tiles * TILE), bf16),
            jax.ShapeDtypeStruct((PAIR, count, row_share, TILE), bf16),
        ],
        in_specs=[WHOLE] * len(whole) + [ANY] * len(parts),
        out_specs=[WHOLE] * 14 + [ANY] * 4,
        scratch_shapes=[
            pltpu.VMEM((Total.HELD, count) + block, bf16),
            pltpu.VMEM((Total.PAIRED, count) + block, bf16),
            pltpu.VMEM((Total.PLANE, 4) + block, bf16),
            pltpu.VMEM((Total.PLANE, 2, 4) + block, bf16),
            pltpu.VMEM((Total.LINE, 4) + block, bf16),
            pltpu.VMEM((Total.LINE,) + block, f32),
            pltpu.VMEM((5, SMALL_ROWS, width), f32),
            pltpu.VMEM((PAIR, slots, half_width), bf16),
            pltpu.VMEM((total, slots, row_share), f32),
            pltpu.VMEM((SMALL_ROWS, width), f32),
            pltpu.VMEM((2, width), f32),
            pltpu.SemaphoreType.DMA((pieces, 16)),
            pltpu.SemaphoreType.DMA((pieces,)),
            pltpu.SemaphoreType.DMA((pieces,)),
            pltpu.SemaphoreType.DMA((pieces, 4)),
            pltpu.SemaphoreType.DMA((pieces, 2, 4)),
            pltpu.SemaphoreType.DMA((pieces, 4)),
            pltpu.SemaphoreType.REGULAR((6,)),
            pltpu.SemaphoreType.DMA((5,)),
            pltpu.SemaphoreType.DMA((5,)),
            pltpu.SemaphoreType.DMA((total,)),
            pltpu.SemaphoreType.DMA((total,)),
            pltpu.SemaphoreType.DMA((total,)),
            pltpu.SemaphoreType.DMA((total,)),
            pltpu.SemaphoreType.DMA((4,)),
            pltpu.SemaphoreType.DMA((2,)),
        ],
        compiler_params=pltpu.CompilerParams(
            collective_id=collective, has_side_effects=True, vmem_limit_bytes=56 * 2**20
        ),
    )(*whole, *parts)


def deliver_call(arrays):
    def kernel(*refs):
        sources, targets, sems = refs[: len(arrays)], refs[len(arrays) : -1], refs[-1]
        copies = [
            pltpu.make_async_copy(source, target, sems.at[k])
            for k, (source, target) in enumerate(zip(sources, targets))
        ]
        for copy in copies:
            copy.start()
        for copy in copies:
            copy.wait()

    return pl.pallas_call(
        kernel,
        out_shape=[jax.ShapeDtypeStruct(a.shape, a.dtype) for a in arrays],
        in_specs=[WHOLE] * len(arrays),
        out_specs=[ANY] * len(arrays),
        scratch_shapes=[pltpu.SemaphoreType.DMA((len(arrays),))],
        compiler_params=pltpu.CompilerParams(vmem_limit_bytes=56 * 2**20),
    )(*arrays)


def fused_block(
    grid,
    tokens,
    conditioning,
    timestep,
    noise_bins,
    source_slot,
    cotangent,
    ada_weight,
    qkv_weight,
    proj_weight,
    ffn_in_weight,
    ffn_out_weight,
    ada_bias,
    qkv_bias,
    proj_bias,
    ffn_in_bias,
    ffn_out_bias,
    norm_gains,
    qk_gains,
):
    capacity, length, model_width = tokens.shape[1:]
    rows = capacity * length
    group_items = source_slot.shape[1]
    half_width = model_width // 2
    frequencies = np.exp(
        -math.log(10000.0) * np.arange(half_width, dtype=np.float32) / half_width
    ).astype(np.float32)
    tables = head_tables()
    token_rows = tokens.reshape(rows, model_width)
    results = forward_call(
        grid,
        1,
        group_items * PAIR / NBINS,
        token_rows,
        (
            norm_gains,
            qk_gains,
            qkv_bias,
            proj_bias,
            ffn_in_bias,
            ffn_out_bias,
            ada_bias,
            cotangent.reshape(rows, model_width),
            conditioning[0],
            timestep,
            noise_bins,
            source_slot,
            jnp.asarray(frequencies)[None],
        ),
        tables,
        ada_weight,
        (qkv_weight, proj_weight, ffn_in_weight, ffn_out_weight),
    )
    (
        modulation,
        cond_float,
        slot_kept,
        output_rows,
        grad_residual,
        grad_attn,
        late_sums,
        late_gain,
        in_bias_sum,
        out_bias_sum,
        first_in,
        _,
        qkv_all,
        proj_all,
        _,
        _,
        in_terms,
        out_terms,
        *kept,
    ) = results
    silu_rows = first_in[:, :capacity].reshape(-1, first_in.shape[2]).astype(jnp.bfloat16)
    whole = (
        modulation,
        cond_float,
        norm_gains,
        qk_gains,
        *tables,
        slot_kept,
        late_sums,
        late_gain,
        in_bias_sum,
        out_bias_sum,
        silu_rows,
    )
    parts = (
        token_rows,
        *kept,
        grad_residual,
        grad_attn,
        qkv_all,
        proj_all,
        in_terms,
        out_terms.reshape(PAIR, grid.count, -1, out_terms.shape[2]),
        ada_weight,
    )
    (
        grad_rows,
        in_grad,
        out_grad,
        qkv_grad,
        proj_grad,
        ada_grad,
        cond_grad,
        *small,
    ) = backward_call(grid, 2, whole, parts)[:14]
    delivered = deliver_call(
        (
            output_rows,
            grad_rows,
            cond_grad,
            ada_grad,
            qkv_grad,
            proj_grad,
            in_grad,
            out_grad,
            *small,
        )
    )
    return (
        delivered[0].reshape(tokens.shape),
        delivered[1].reshape(tokens.shape),
        delivered[2][None],
        *delivered[3:],
    )


def per_device(
    grid,
    tokens,
    conditioning,
    timestep,
    noise_bins,
    source_slot,
    cotangent,
    ada_weight,
    qkv_weight,
    proj_weight,
    ffn_in_weight,
    ffn_out_weight,
    ada_bias,
    qkv_bias,
    proj_bias,
    ffn_in_bias,
    ffn_out_bias,
    norm_gains,
    qk_gains,
):
    if grid.plain:
        return fused_block(
            grid,
            tokens,
            conditioning,
            timestep,
            noise_bins,
            source_slot,
            cotangent,
            ada_weight,
            qkv_weight,
            proj_weight,
            ffn_in_weight,
            ffn_out_weight,
            ada_bias,
            qkv_bias,
            proj_bias,
            ffn_in_bias,
            ffn_out_bias,
            norm_gains,
            qk_gains,
        )
    dp_count = lax.axis_size("dp")
    pair_count = lax.axis_size("fsdp")
    capacity = tokens.shape[1]
    length = tokens.shape[2]
    model_width = tokens.shape[3]
    listed = source_slot[0]
    group_items = listed.shape[0]
    row_count = capacity * length
    own_index = lax.axis_index("dp")
    own_slots = own_index * capacity + jnp.arange(capacity, dtype=jnp.int32)
    held = jnp.any(listed[None, :] == own_slots[:, None], axis=1)
    bin_hits = (
        noise_bins[0][:, None] == jnp.arange(NBINS, dtype=jnp.int32)[None, :]
    ) & held[:, None]
    local_counts = jnp.sum(bin_hits.astype(jnp.float32), axis=0)
    cond_float = lax.reduce_precision(
        conditioning[0].astype(jnp.float32) + time_embed(timestep[0], model_width), 8, 7
    )
    silu_cond = swish(cond_float).astype(jnp.bfloat16)
    row_share, half_width = ada_weight.shape
    total = dp_count * pair_count
    silu_blocks = jnp.repeat(
        silu_cond.reshape(capacity, dp_count, row_share).transpose(1, 0, 2), pair_count, axis=0
    )
    shards = (qkv_weight, proj_weight, ffn_in_weight, ffn_out_weight)
    share = group_items * pair_count / NBINS
    token_rows = tokens.reshape(row_count, model_width)
    cotangent_rows = cotangent.reshape(row_count, model_width)
    tables = head_tables()
    head_gains = jnp.tile(qk_gains, (1, HEADS))
    lanes = (capacity, 1, model_width)
    slot_kept = jnp.broadcast_to(held.astype(jnp.float32)[:, None, None], lanes)
    qkv_halves, proj_halves, in_halves = [
        bias.reshape(pair_count, -1) for bias in (qkv_bias, proj_bias, ffn_in_bias)
    ]
    every_count = lax.all_gather(local_counts, ("dp", "fsdp"))
    bin_share = share / jnp.sum(every_count, axis=0)
    slot_weight = jnp.sum(jnp.where(bin_hits, bin_share[None, :], 0.0), axis=1)
    weight_lanes = jnp.broadcast_to(slot_weight[:, None, None], lanes)
    silu_rows = lax.all_to_all(silu_blocks, ("dp", "fsdp"), 0, 0, tiled=True)
    silu_rows = silu_rows.reshape(total * capacity, row_share)
    mod_blocks = product(silu_rows, ada_weight).reshape(total, capacity, half_width)
    mod_parts = lax.all_to_all(mod_blocks, ("dp", "fsdp"), 0, 0, tiled=True)
    modulation = (
        jnp.sum(mod_parts.reshape(dp_count, pair_count, capacity, half_width), axis=0)
        .transpose(1, 0, 2)
        .reshape(capacity, -1)
        + ada_bias
    ).reshape(capacity, 6, model_width)
    fulls = [lax.all_gather(lax.all_gather(s, "dp"), "fsdp") for s in shards]
    qkv_full, proj_full, ffn_in_full, ffn_out_full = [
        full.reshape(pair_count, -1, full.shape[3]) for full in fulls
    ]
    forward = attention_forward_call(
        token_rows,
        modulation,
        norm_gains,
        head_gains,
        qkv_halves,
        proj_halves,
        tables,
        qkv_full,
        proj_full,
    )
    kept, (attn_out, residual, mod_two) = forward[:9], forward[9:]
    *middle, in_terms, out_terms = ffn_call(
        mod_two,
        residual,
        attn_out,
        cotangent_rows,
        weight_lanes,
        slot_kept,
        modulation,
        norm_gains,
        in_halves,
        ffn_out_bias[None],
        ffn_in_full,
        ffn_out_full,
    )
    (
        output_rows,
        grad_residual,
        grad_attn,
        late_sums,
        late_gain,
        in_bias_sum,
        out_bias_sum,
    ) = middle
    (
        grad_rows,
        early_sums,
        early_gain,
        head_sums,
        qkv_bias_sum,
        proj_bias_sum,
        qkv_terms,
        proj_terms,
    ) = attention_backward_call(
        token_rows,
        modulation,
        norm_gains,
        head_gains,
        tables,
        slot_kept,
        kept,
        grad_residual,
        grad_attn,
        qkv_full,
        proj_full,
    )
    ffn_grads, attn_grads = [
        [
            lax.psum_scatter(
                lax.psum_scatter(
                    term.reshape(pair_count, dp_count, -1, term.shape[-1]), "fsdp"
                ),
                "dp",
            ).astype(jnp.float32)
            for term in terms
        ]
        for terms in ((in_terms, out_terms), (qkv_terms, proj_terms))
    ]
    grad_modulation = (late_sums + early_sums).reshape(capacity, -1).astype(jnp.bfloat16)
    mod_halves = grad_modulation.reshape(capacity, pair_count, half_width).transpose(1, 0, 2)
    small_out = lax.psum(
        (
            jnp.sum(grad_modulation.astype(jnp.float32), axis=0),
            qkv_bias_sum.reshape(-1),
            proj_bias_sum.reshape(-1),
            in_bias_sum.reshape(-1),
            out_bias_sum.reshape(-1),
            jnp.concatenate([early_gain, late_gain]),
            jnp.sum(head_sums.reshape(2, HEADS, HEAD_DIM), axis=1),
        ),
        ("dp", "fsdp"),
    )
    every_mod = lax.all_gather(lax.all_to_all(mod_halves, "fsdp", 0, 0, tiled=True), "dp")
    every_mod = every_mod.reshape(total * capacity, half_width)
    ada_grad = transposed_product(silu_rows, every_mod)
    cond_blocks = product_transposed(every_mod, ada_weight)
    cond_parts = lax.all_to_all(
        cond_blocks.reshape(total, capacity, row_share), ("dp", "fsdp"), 0, 0, tiled=True
    )
    grad_cond = (
        jnp.sum(cond_parts.reshape(dp_count, pair_count, capacity, row_share), axis=1)
        .transpose(1, 0, 2)
        .reshape(capacity, model_width)
    )
    cond_grad = jnp.where(held[:, None], grad_cond * swish_slope(cond_float), 0.0)
    shape = tokens.shape
    return (
        output_rows.reshape(shape),
        grad_rows.reshape(shape),
        cond_grad[None],
        ada_grad,
        attn_grads[0],
        attn_grads[1],
        ffn_grads[0],
        ffn_grads[1],
        small_out[0],
        small_out[1],
        small_out[2],
        small_out[3],
        small_out[4],
        small_out[5],
        small_out[6],
    )


def solution(mesh):
    return jax.shard_map(
        functools.partial(per_device, Grid(mesh)),
        mesh=mesh,
        in_specs=(
            P("fsdp", "dp", None, None),
            P("fsdp", "dp", None),
            P("fsdp", "dp"),
            P("fsdp", "dp"),
            P("fsdp", None),
            P("fsdp", "dp", None, None),
            P("dp", "fsdp"),
            P("dp", "fsdp"),
            P("dp", "fsdp"),
            P("dp", "fsdp"),
            P("dp", "fsdp"),
            P(),
            P(),
            P(),
            P(),
            P(),
            P(),
            P(),
        ),
        out_specs=(
            P("fsdp", "dp", None, None),
            P("fsdp", "dp", None, None),
            P("fsdp", "dp", None),
            P("dp", "fsdp"),
            P("dp", "fsdp"),
            P("dp", "fsdp"),
            P("dp", "fsdp"),
            P("dp", "fsdp"),
            P(),
            P(),
            P(),
            P(),
            P(),
            P(),
            P(),
        ),
        check_vma=False,
    )
```

```python
import functools
import math

import jax
import jax.numpy as jnp
import numpy as np
from jax import lax
from jax.experimental import pallas as pl
from jax.experimental.pallas import tpu as pltpu
from jax.sharding import PartitionSpec as P

HEADS = 16
HEAD_DIM = 72
FF = 3072
GRID_ROWS = 16
GRID_COLS = 16
NBINS = 16


EPS = 1e-06


def swish(inputs):
    return inputs * jax.nn.sigmoid(inputs)


def swish_slope(inputs):
    sigmoid = jax.nn.sigmoid(inputs)
    return sigmoid * (1.0 + inputs * (1.0 - sigmoid))


def norm_scale(inputs):
    return lax.rsqrt(jnp.mean(inputs * inputs, axis=-1, keepdims=True) + EPS)


def norm_back(grad_unit, unit_value, scale_factor):
    return scale_factor * (
        grad_unit - unit_value * jnp.mean(grad_unit * unit_value, axis=-1, keepdims=True)
    )


def time_embed(timesteps, model_width):
    half_width = model_width // 2
    frequencies = jnp.exp(
        -math.log(10000.0) * jnp.arange(half_width, dtype=jnp.float32) / half_width
    )
    angles = timesteps.astype(jnp.float32)[..., None] * frequencies
    return jnp.concatenate([jnp.cos(angles), jnp.sin(angles)], axis=-1)


def product(former, latter):
    return jnp.dot(former, latter, preferred_element_type=jnp.float32)


def product_transposed(former, latter):
    return lax.dot_general(
        former, latter, (((1,), (1,)), ((), ())), preferred_element_type=jnp.float32
    )


def transposed_product(former, latter):
    return lax.dot_general(
        former, latter, (((0,), (0,)), ((), ())), preferred_element_type=jnp.float32
    )


MESH = pl.DeviceIdType.MESH
ANY = pl.BlockSpec(memory_space=pl.ANY)
WHOLE = pl.BlockSpec(memory_space=pltpu.VMEM)
PAIR = 2


class Grid:
    def __init__(self, mesh):
        devices = mesh.devices
        self.count = devices.shape[0]
        places = [tuple(devices[i, 0].coords[:3]) for i in range(self.count)]
        low = [min(p[a] for p in places) for a in range(3)]
        places = [tuple(p[a] - low[a] for a in range(3)) for p in places]
        self.sizes = [max(p[a] for p in places) + 1 for a in range(3)]
        order = {p: i for i, p in enumerate(places)}
        self.strides = [
            order.get(tuple(int(b == a) for b in range(3)), 0) if self.sizes[a] > 1 else 0
            for a in range(3)
        ]
        self.plain = (
            self.sizes[0] == 2
            and self.sizes[1] == 2
            and self.sizes[2] == 4
            and devices.shape[1] == PAIR
            and all(
                sum(c * s for c, s in zip(p, self.strides)) == i for p, i in order.items()
            )
        )

    def at(self, x, y, z):
        return x * self.strides[0] + y * self.strides[1] + z * self.strides[2]

    def here(self):
        own = lax.axis_index("dp")
        return tuple(
            lax.rem(own // stride, size) for stride, size in zip(self.strides, self.sizes)
        )


class Copies:
    def __init__(self, send_sems):
        self.send_sems = send_sems
        self.started = []

    def send(self, source, target, recv_sem, dp, core):
        copy = pltpu.make_async_remote_copy(
            src_ref=source,
            dst_ref=target,
            send_sem=self.send_sems.at[len(self.started)],
            recv_sem=recv_sem,
            device_id={"dp": dp, "fsdp": core},
            device_id_type=MESH,
        )
        copy.start()
        self.started.append(copy)

    def finish(self):
        for copy in self.started:
            copy.wait_send()


def arrived(block, recv_sem):
    pltpu.make_async_copy(block, block, recv_sem).wait()


def greet_all(count):
    barrier = pltpu.get_barrier_semaphore()
    own = lax.axis_index("dp") * PAIR + lax.axis_index("fsdp")

    def signal(step, carry):
        other = lax.rem(own + step, count * PAIR)
        pl.semaphore_signal(
            barrier,
            inc=1,
            device_id={"dp": other // PAIR, "fsdp": lax.rem(other, PAIR)},
            device_id_type=MESH,
        )
        return carry

    lax.fori_loop(1, count * PAIR, signal, 0)
    pl.semaphore_wait(barrier, count * PAIR - 1)


def spread(count, source_at, target, send_sems, recv_sems):
    own = lax.axis_index("dp") * PAIR + lax.axis_index("fsdp")

    def start(step, carry):
        other = lax.rem(own + step, count * PAIR)
        pltpu.make_async_remote_copy(
            src_ref=source_at(other),
            dst_ref=target.at[own],
            send_sem=send_sems.at[step],
            recv_sem=recv_sems.at[own],
            device_id={"dp": other // PAIR, "fsdp": lax.rem(other, PAIR)},
            device_id_type=MESH,
        ).start()
        return carry

    lax.fori_loop(1, count * PAIR, start, 0)
    mine = pltpu.make_async_copy(source_at(own), target.at[own], recv_sems.at[own])
    mine.start()


def spread_wait(count, source_at, target, send_sems, recv_sems):
    own = lax.axis_index("dp") * PAIR + lax.axis_index("fsdp")

    def wait(step, carry):
        other = lax.rem(own + step, count * PAIR)
        arrived(target.at[other], recv_sems.at[other])
        return carry

    lax.fori_loop(0, count * PAIR, wait, 0)

    def wait_sent(step, carry):
        other = lax.rem(own + step, count * PAIR)
        pltpu.make_async_copy(source_at(other), source_at(other), send_sems.at[step]).wait()
        return carry

    lax.fori_loop(1, count * PAIR, wait_sent, 0)


def pickers(sources, modes):
    return [
        {
            "each": lambda other, ref=ref: ref.at[other],
            "half": lambda other, ref=ref: ref.at[lax.rem(other, PAIR)],
            "all": lambda other, ref=ref: ref,
        }[mode]
        for ref, mode in zip(sources, modes)
    ]


def landing(count, array, mode):
    part = array.shape if mode == "all" else array.shape[1:]
    return jax.ShapeDtypeStruct((count * PAIR,) + part, array.dtype)


def head_tables():
    width = HEADS * HEAD_DIM
    quarter = HEAD_DIM // 4
    lane = np.arange(width)
    indicator = np.zeros((width, 128), np.float32)
    indicator[lane, lane // HEAD_DIM] = 1.0
    frequencies = np.exp(-math.log(10000.0) * np.arange(quarter, dtype=np.float32) * 4.0 / HEAD_DIM)
    frequencies = frequencies.astype(np.float32)
    places = np.arange(GRID_ROWS * GRID_COLS)
    part = (lane % HEAD_DIM) // quarter
    place = np.where(part[None, :] < 2, (places // GRID_COLS)[:, None], (places % GRID_COLS)[:, None])
    angles = place.astype(np.float32) * frequencies[lane % quarter][None, :]
    sines = np.sin(angles)
    first = (part % 2 == 0)[None, :]
    return (
        jnp.asarray(indicator, jnp.bfloat16),
        jnp.asarray(indicator.T, jnp.bfloat16),
        jnp.asarray(np.cos(angles), jnp.float32),
        jnp.asarray(np.where(first, -sines, 0.0), jnp.float32),
        jnp.asarray(np.where(first, 0.0, sines), jnp.float32),
        jnp.asarray(indicator.T[:HEADS], jnp.bfloat16),
    )


def turn(vector, cosines, before, after, sign=1.0):
    width = vector.shape[1]
    quarter = HEAD_DIM // 4
    shifted = (
        pltpu.roll(vector, width - quarter, axis=1) * before
        + pltpu.roll(vector, quarter, axis=1) * after
    )
    return vector * cosines + shifted if sign > 0 else vector * cosines - shifted


def spread_heads(compact, spreader):
    high = compact.astype(jnp.bfloat16)
    low = (compact - high.astype(jnp.float32)).astype(jnp.bfloat16)
    return product(high, spreader) + product(low, spreader)


def row_loop(rows, per_slot, body, block=128):
    def step(index, carry):
        start = pl.multiple_of(index * block, block)
        body(
            pl.ds(start, block),
            (index * block) // per_slot,
            pl.ds(pl.multiple_of(lax.rem(index * block, per_slot), block), block),
        )
        return carry

    lax.fori_loop(0, rows // block, step, 0)


def head_window(head):
    start = head * HEAD_DIM
    low = start // 128 * 128
    high = -(-(start + HEAD_DIM) // 128) * 128
    return slice(low, high)


def softmax(scores):
    exponent = jnp.exp(scores - jnp.max(scores, axis=-1, keepdims=True))
    return exponent / jnp.sum(exponent, axis=-1, keepdims=True)


def lane_tiles(width, most):
    edges = list(range(0, width, most)) + [width]
    return [slice(a, b) for a, b in zip(edges[:-1], edges[1:])]


def attention_forward(
    tokens, mod, gains, head_gains, qkv_bias, proj_bias,
    indicator, spreader, cosines, before, after, masks,
    qkv_hbm, proj_hbm,
    mod_one, query_unit, key_unit, query_scale, key_scale, query_turned, key_turned, values_low,
    attended_low, attn_out, residual, mod_two,
    qkv_half, proj_half, raw, sems,
):
    rows, width = tokens.shape
    length = cosines.shape[0]
    loads = [
        pltpu.make_async_copy(qkv_hbm, qkv_half, sems.at[0]),
        pltpu.make_async_copy(proj_hbm, proj_half, sems.at[1]),
    ]
    for load in loads:
        load.start()

    def norm_first(here, slot, _):
        inputs = tokens[here, :].astype(jnp.float32)
        normed = inputs * norm_scale(inputs) * gains[0:1, :]
        mod_one[here, :] = (normed * (1.0 + mod[slot, 1:2, :]) + mod[slot, 0:1, :]).astype(
            jnp.bfloat16
        )

    row_loop(rows, length, norm_first)
    loads[0].wait()
    half = qkv_half.shape[2]
    for side in range(PAIR):
        for cols in lane_tiles(half, 640):
            raw[side, :, cols] = (
                product(mod_one[...], qkv_half[side, :, cols])
                + qkv_bias[side : side + 1, cols]
            )

    def heads(here, slot, there):
        query = raw[0, here, :width]
        key_vec = jnp.concatenate(
            [raw[0, here, width:], raw[1, here, : 2 * width - half]], axis=1
        )
        values_low[here, :] = raw[1, here, 2 * width - half :].astype(jnp.bfloat16)
        tables = (cosines[there, :], before[there, :], after[there, :])
        for vector, gain, unit, scale, turned in (
            (query, head_gains[0:1, :], query_unit, query_scale, query_turned),
            (key_vec, head_gains[1:2, :], key_unit, key_scale, key_turned),
        ):
            squares = product((vector * vector).astype(jnp.bfloat16), indicator[...])
            factor = lax.rsqrt(squares * (1.0 / HEAD_DIM) + EPS)
            scale[here, :] = factor
            united = vector * spread_heads(factor, spreader[...])
            unit[here, :] = united
            turned[here, :] = turn(united * gain, *tables).astype(jnp.bfloat16)

    row_loop(rows, length, heads)

    def attend(slot, carry):
        here = pl.ds(pl.multiple_of(slot * length, length), length)
        pieces = [None] * (width // 128)
        for head in range(HEADS):
            window = head_window(head)
            mask = masks[head : head + 1, window]
            scores = (
                product_transposed(query_turned[here, window] * mask, key_turned[here, window])
                * HEAD_DIM**-0.5
            )
            probs = softmax(scores).astype(jnp.bfloat16)
            found = product(probs, values_low[here, window] * mask)
            for tile in range(window.start // 128, window.stop // 128):
                part = found[:, tile * 128 - window.start : (tile + 1) * 128 - window.start]
                pieces[tile] = part if pieces[tile] is None else pieces[tile] + part
                if (tile + 1) * 128 <= (head + 1) * HEAD_DIM:
                    attended_low[here, tile * 128 : (tile + 1) * 128] = pieces[tile].astype(
                        jnp.bfloat16
                    )
                    pieces[tile] = None
        return carry

    lax.fori_loop(0, rows // length, attend, 0)
    loads[1].wait()
    half = proj_half.shape[2]
    for side in range(PAIR):
        attn_out[:, side * half : (side + 1) * half] = (
            product(attended_low[...], proj_half[side]) + proj_bias[side : side + 1, :]
        )

    def norm_second(here, slot, _):
        total = tokens[here, :].astype(jnp.float32) + mod[slot, 2:3, :] * attn_out[here, :]
        residual[here, :] = total
        normed = total * norm_scale(total) * gains[1:2, :]
        mod_two[here, :] = (normed * (1.0 + mod[slot, 4:5, :]) + mod[slot, 3:4, :]).astype(
            jnp.bfloat16
        )

    row_loop(rows, length, norm_second)


def attention_forward_call(tokens, mod, gains, head_gains, qkv_bias, proj_bias, tables, qkv, proj):
    rows, width = tokens.shape
    wide = jax.ShapeDtypeStruct((rows, width), jnp.float32)
    low = jax.ShapeDtypeStruct((rows, width), jnp.bfloat16)
    compact = jax.ShapeDtypeStruct((rows, 128), jnp.float32)
    return pl.pallas_call(
        attention_forward,
        out_shape=[low, wide, wide, compact, compact, low, low, low, low, wide, wide, low],
        in_specs=[WHOLE] * 12 + [ANY] * 2,
        out_specs=[WHOLE] * 12,
        scratch_shapes=[
            pltpu.VMEM(qkv.shape, jnp.bfloat16),
            pltpu.VMEM(proj.shape, jnp.bfloat16),
            pltpu.VMEM((PAIR, rows, qkv.shape[2]), jnp.float32),
            pltpu.SemaphoreType.DMA((2,)),
        ],
        compiler_params=pltpu.CompilerParams(vmem_limit_bytes=52 * 2**20),
    )(tokens, mod, gains, head_gains, qkv_bias, proj_bias, *tables, qkv, proj)


def ffn_pass(
    mod_two, residual, attn_out, cotangent, slot_weight, slot_kept, mod, gains, in_bias, out_bias,
    in_hbm, out_hbm,
    output, grad_residual, grad_attn, slot_sums, gain_sum, in_bias_sum, out_bias_sum,
    in_terms, out_terms,
    turned_two, grad_low, grad_half, lifted_grad, ffn_value, in_chunk, out_chunk, in_stage, out_stage,
    load_sems, store_sems,
):
    rows, width = mod_two.shape
    length = rows // mod.shape[0]
    hidden = in_hbm.shape[2]
    chunk = in_chunk.shape[3]
    half = out_hbm.shape[2]
    steps = hidden // chunk

    def columns(step):
        return pl.ds(pl.multiple_of(step * chunk, chunk), chunk)

    def loads(step, slot):
        return [
            pltpu.make_async_copy(
                in_hbm.at[:, :, columns(step)], in_chunk.at[slot], load_sems.at[slot, 0]
            ),
            pltpu.make_async_copy(
                out_hbm.at[:, columns(step), :], out_chunk.at[slot], load_sems.at[slot, 1]
            ),
        ]

    def stores(step, slot):
        return [
            pltpu.make_async_copy(
                in_stage.at[slot], in_terms.at[:, :, columns(step)], store_sems.at[slot, 0]
            ),
            pltpu.make_async_copy(
                out_stage.at[slot], out_terms.at[:, columns(step), :], store_sems.at[slot, 1]
            ),
        ]

    for load in loads(0, 0):
        load.start()

    def prepare(here, slot, _):
        grad_out = (cotangent[here, :].astype(jnp.float32) * slot_weight[slot]).astype(jnp.bfloat16)
        grad_low[here, :] = grad_out
        grad_ffn = (mod[slot, 5:6, :] * grad_out.astype(jnp.float32)).astype(jnp.bfloat16)
        grad_half[0, here, :] = grad_ffn[:, :half]
        grad_half[1, here, :] = grad_ffn[:, half:]

    row_loop(rows, length, prepare)
    turned_two[...] = mod_two[...].T
    for side in range(PAIR):
        out_bias_sum[side : side + 1, :] = jnp.sum(
            grad_half[side].astype(jnp.float32), axis=0, keepdims=True
        )
    lifted_grad[...] = jnp.zeros_like(lifted_grad)
    ffn_value[...] = jnp.zeros_like(ffn_value)

    def step_body(step, carry):
        slot = lax.rem(step, 2)

        @pl.when(step + 1 < steps)
        def _():
            for load in loads(step + 1, 1 - slot):
                load.start()

        for load in loads(step, slot):
            load.wait()

        @pl.when(step >= 2)
        def _():
            for store in stores(step - 2, slot):
                store.wait()

        here = columns(step)
        gate_part = product(mod_two[...], in_chunk[slot, 0]) + in_bias[0:1, here]
        up_part = product(mod_two[...], in_chunk[slot, 1]) + in_bias[1:2, here]
        sigmoid = 1.0 / (1.0 + jnp.exp(-gate_part))
        swished = gate_part * sigmoid
        hidden_low = (swished * up_part).astype(jnp.bfloat16)
        grad_hidden = product_transposed(grad_half[0], out_chunk[slot, 0]) + product_transposed(
            grad_half[1], out_chunk[slot, 1]
        )
        grad_gate = (
            grad_hidden * up_part * (sigmoid * (1.0 + gate_part * (1.0 - sigmoid)))
        ).astype(jnp.bfloat16)
        grad_up = (grad_hidden * swished).astype(jnp.bfloat16)
        for side in range(PAIR):
            ffn_value[side] += product(hidden_low, out_chunk[slot, side])
        lifted_grad[...] += product_transposed(grad_gate, in_chunk[slot, 0])
        lifted_grad[...] += product_transposed(grad_up, in_chunk[slot, 1])
        for side, grad in ((0, grad_gate), (1, grad_up)):
            in_bias_sum[side : side + 1, here] = jnp.sum(
                grad.astype(jnp.float32), axis=0, keepdims=True
            )
            in_stage[slot, side] = product(turned_two[...], grad).astype(jnp.bfloat16)
        turned_hidden = hidden_low.T
        for side in range(PAIR):
            out_stage[slot, side] = product(turned_hidden, grad_half[side]).astype(jnp.bfloat16)
        for store in stores(step, slot):
            store.start()
        return carry

    lax.fori_loop(0, steps, step_body, 0)
    for step in range(max(steps - 2, 0), steps):
        for store in stores(step, step % 2):
            store.wait()
    slot_sums[...] = jnp.zeros_like(slot_sums)
    gain_sum[...] = jnp.zeros_like(gain_sum)

    def finish(here, slot, _):
        value = jnp.concatenate([ffn_value[0, here, :], ffn_value[1, here, :]], axis=1) + out_bias[...]
        total = residual[here, :]
        output[here, :] = ((total + mod[slot, 5:6, :] * value) * slot_kept[slot]).astype(
            jnp.bfloat16
        )
        grad_out = grad_low[here, :].astype(jnp.float32)
        factor = norm_scale(total)
        unit = total * factor
        normed = unit * gains[1:2, :]
        grad_mod = lifted_grad[here, :]
        grad_normed = grad_mod * (1.0 + mod[slot, 4:5, :])
        gradient = grad_out + norm_back(grad_normed * gains[1:2, :], unit, factor)
        grad_residual[here, :] = gradient
        grad_attn[here, :] = (mod[slot, 2:3, :] * gradient).astype(jnp.bfloat16)
        for place, terms in (
            (2, gradient * attn_out[here, :]),
            (3, grad_mod),
            (4, grad_mod * normed),
            (5, grad_out * value),
        ):
            slot_sums[slot, place : place + 1, :] += jnp.sum(terms, axis=0, keepdims=True)
        gain_sum[...] += jnp.sum(grad_normed * unit, axis=0, keepdims=True)

    row_loop(rows, length, finish)


def ffn_call(
    mod_two, residual, attn_out, cotangent, slot_weight, slot_kept, mod, gains, in_bias, out_bias,
    ffn_in, ffn_out,
):
    rows, width = mod_two.shape
    hidden, half = ffn_in.shape[2], ffn_out.shape[2]
    chunk = 512
    f32, bf16 = jnp.float32, jnp.bfloat16
    return pl.pallas_call(
        ffn_pass,
        out_shape=[
            jax.ShapeDtypeStruct((rows, width), bf16),
            jax.ShapeDtypeStruct((rows, width), f32),
            jax.ShapeDtypeStruct((rows, width), bf16),
            jax.ShapeDtypeStruct(mod.shape, f32),
            jax.ShapeDtypeStruct((1, width), f32),
            jax.ShapeDtypeStruct((PAIR, hidden), f32),
            jax.ShapeDtypeStruct((PAIR, half), f32),
            jax.ShapeDtypeStruct(ffn_in.shape, bf16),
            jax.ShapeDtypeStruct(ffn_out.shape, bf16),
        ],
        in_specs=[WHOLE] * 10 + [ANY] * 2,
        out_specs=[WHOLE] * 7 + [ANY] * 2,
        scratch_shapes=[
            pltpu.VMEM((width, rows), bf16),
            pltpu.VMEM((rows, width), bf16),
            pltpu.VMEM((PAIR, rows, half), bf16),
            pltpu.VMEM((rows, width), f32),
            pltpu.VMEM((PAIR, rows, half), f32),
            pltpu.VMEM((2, PAIR, width, chunk), bf16),
            pltpu.VMEM((2, PAIR, chunk, half), bf16),
            pltpu.VMEM((2, PAIR, width, chunk), bf16),
            pltpu.VMEM((2, PAIR, chunk, half), bf16),
            pltpu.SemaphoreType.DMA((2, 2)),
            pltpu.SemaphoreType.DMA((2, 2)),
        ],
        compiler_params=pltpu.CompilerParams(vmem_limit_bytes=52 * 2**20),
    )(
        mod_two, residual, attn_out, cotangent, slot_weight, slot_kept, mod, gains, in_bias, out_bias,
        ffn_in, ffn_out,
    )


def attention_backward(
    tokens, mod, gains, head_gains, indicator, spreader, cosines, before, after, masks, slot_kept,
    mod_one, query_unit, key_unit, query_scale, key_scale, query_turned, key_turned, values_low,
    attended_low, grad_residual, grad_attn,
    qkv_hbm, proj_hbm,
    input_grad, slot_sums, gain_sum, head_sums, qkv_bias_sum, proj_bias_sum, qkv_terms, proj_terms,
    qkv_half, proj_half, grad_attended, grad_query, grad_key, grad_values, grad_half, turned, sems,
):
    rows, width = tokens.shape
    length = cosines.shape[0]
    loads = [
        pltpu.make_async_copy(proj_hbm, proj_half, sems.at[0]),
        pltpu.make_async_copy(qkv_hbm, qkv_half, sems.at[1]),
    ]
    stores = [
        pltpu.make_async_copy(proj_half, proj_terms, sems.at[2]),
        pltpu.make_async_copy(qkv_half, qkv_terms, sems.at[3]),
    ]
    for load in loads:
        load.start()
    half = proj_half.shape[2]
    turned[...] = attended_low[...].T
    for side in range(PAIR):
        cols = slice(side * half, (side + 1) * half)
        proj_bias_sum[:, cols] = jnp.sum(
            grad_attn[:, cols].astype(jnp.float32), axis=0, keepdims=True
        )
    loads[0].wait()
    grad_attended[...] = (
        product_transposed(grad_attn[:, :half], proj_half[0])
        + product_transposed(grad_attn[:, half:], proj_half[1])
    ).astype(jnp.bfloat16)
    for side in range(PAIR):
        proj_half[side] = product(
            turned[...], grad_attn[:, side * half : (side + 1) * half]
        ).astype(jnp.bfloat16)
    stores[0].start()

    def attend(slot, carry):
        here = pl.ds(pl.multiple_of(slot * length, length), length)
        pieces = [[None] * (width // 128) for _ in range(3)]
        for head in range(HEADS):
            window = head_window(head)
            mask = masks[head : head + 1, window]
            query = query_turned[here, window] * mask
            key_vec = key_turned[here, window]
            value = values_low[here, window]
            grad = grad_attended[here, window] * mask
            probs = softmax(product_transposed(query, key_vec) * HEAD_DIM**-0.5)
            grad_probs = product_transposed(grad, value)
            grad_scores = (
                probs * (grad_probs - jnp.sum(probs * grad_probs, axis=-1, keepdims=True))
            ).astype(jnp.bfloat16)
            founds = (
                product(grad_scores, key_vec * mask) * HEAD_DIM**-0.5,
                transposed_product(grad_scores, query) * HEAD_DIM**-0.5,
                transposed_product(probs.astype(jnp.bfloat16), grad),
            )
            for kind, (found, target) in enumerate(
                zip(founds, (grad_query, grad_key, grad_values))
            ):
                for tile in range(window.start // 128, window.stop // 128):
                    part = found[:, tile * 128 - window.start : (tile + 1) * 128 - window.start]
                    held = pieces[kind][tile]
                    held = part if held is None else held + part
                    pieces[kind][tile] = held
                    if (tile + 1) * 128 <= (head + 1) * HEAD_DIM:
                        target[here, tile * 128 : (tile + 1) * 128] = held
        return carry

    lax.fori_loop(0, rows // length, attend, 0)
    half = qkv_half.shape[2]
    head_sums[...] = jnp.zeros_like(head_sums)

    def heads(here, slot, there):
        tables = (cosines[there, :], before[there, :], after[there, :])
        founds = []
        for kind, (grad, gain, unit, scale) in enumerate(
            (
                (grad_query, head_gains[0:1, :], query_unit, query_scale),
                (grad_key, head_gains[1:2, :], key_unit, key_scale),
            )
        ):
            normed = turn(grad[here, :], *tables, sign=-1.0)
            united = unit[here, :]
            head_sums[kind : kind + 1, :] += jnp.sum(normed * united, axis=0, keepdims=True)
            normed = normed * gain
            means = product((normed * united).astype(jnp.bfloat16), indicator[...]) * (
                1.0 / HEAD_DIM
            )
            founds.append(
                spread_heads(scale[here, :], spreader[...])
                * (normed - united * spread_heads(means, spreader[...]))
            )
        cut = half - width
        grad_half[0, here, :width] = founds[0].astype(jnp.bfloat16)
        grad_half[0, here, width:] = founds[1][:, :cut].astype(jnp.bfloat16)
        grad_half[1, here, : width - cut] = founds[1][:, cut:].astype(jnp.bfloat16)
        grad_half[1, here, width - cut :] = grad_values[here, :].astype(jnp.bfloat16)

    row_loop(rows, length, heads)
    lifted_grad = grad_query
    loads[1].wait()
    for side in range(PAIR):
        qkv_bias_sum[side : side + 1, :] = jnp.sum(
            grad_half[side].astype(jnp.float32), axis=0, keepdims=True
        )
    for cols in lane_tiles(width, 384):
        lifted_grad[:, cols] = product_transposed(
            grad_half[0], qkv_half[0, cols, :]
        ) + product_transposed(grad_half[1], qkv_half[1, cols, :])
    turned[...] = mod_one[...].T
    for side in range(PAIR):
        for cols in lane_tiles(half, 640):
            qkv_half[side, :, cols] = product(turned[...], grad_half[side, :, cols]).astype(
                jnp.bfloat16
            )
    stores[1].start()
    slot_sums[...] = jnp.zeros_like(slot_sums)
    gain_sum[...] = jnp.zeros_like(gain_sum)

    def finish(here, slot, _):
        inputs = tokens[here, :].astype(jnp.float32)
        factor = norm_scale(inputs)
        unit = inputs * factor
        normed = unit * gains[0:1, :]
        grad_mod = lifted_grad[here, :]
        grad_normed = grad_mod * (1.0 + mod[slot, 1:2, :])
        gradient = grad_residual[here, :] + norm_back(grad_normed * gains[0:1, :], unit, factor)
        input_grad[here, :] = (gradient * slot_kept[slot]).astype(jnp.bfloat16)
        for place, terms in ((0, grad_mod), (1, grad_mod * normed)):
            slot_sums[slot, place : place + 1, :] += jnp.sum(terms, axis=0, keepdims=True)
        gain_sum[...] += jnp.sum(grad_normed * unit, axis=0, keepdims=True)

    row_loop(rows, length, finish)
    for store in stores:
        store.wait()


def attention_backward_call(
    tokens, mod, gains, head_gains, tables, slot_kept, forward, grad_residual, grad_attn, qkv, proj
):
    rows, width = tokens.shape
    f32, bf16 = jnp.float32, jnp.bfloat16
    half = qkv.shape[2]
    return pl.pallas_call(
        attention_backward,
        out_shape=[
            jax.ShapeDtypeStruct((rows, width), bf16),
            jax.ShapeDtypeStruct(mod.shape, f32),
            jax.ShapeDtypeStruct((1, width), f32),
            jax.ShapeDtypeStruct((2, width), f32),
            jax.ShapeDtypeStruct((PAIR, half), f32),
            jax.ShapeDtypeStruct((1, width), f32),
            jax.ShapeDtypeStruct(qkv.shape, bf16),
            jax.ShapeDtypeStruct(proj.shape, bf16),
        ],
        in_specs=[WHOLE] * 22 + [ANY] * 2,
        out_specs=[WHOLE] * 6 + [ANY] * 2,
        scratch_shapes=[
            pltpu.VMEM(qkv.shape, bf16),
            pltpu.VMEM(proj.shape, bf16),
            pltpu.VMEM((rows, width), bf16),
            pltpu.VMEM((rows, width), f32),
            pltpu.VMEM((rows, width), f32),
            pltpu.VMEM((rows, width), f32),
            pltpu.VMEM((PAIR, rows, half), bf16),
            pltpu.VMEM((width, rows), bf16),
            pltpu.SemaphoreType.DMA((4,)),
        ],
        compiler_params=pltpu.CompilerParams(vmem_limit_bytes=52 * 2**20),
    )(
        tokens, mod, gains, head_gains, *tables, slot_kept, *forward, grad_residual, grad_attn,
        qkv, proj,
    )


class Piece:
    SENDS = 31

    def __init__(self, grid, source, full_at, send_sem, far_sem, near_sem):
        self.grid, self.source, self.full_at = grid, source, full_at
        self.send_sem, self.far_sem, self.near_sem = send_sem, far_sem, near_sem
        self.x, self.y, self.z = grid.here()
        self.core = lax.axis_index("fsdp")
        self.own = grid.at(self.x, self.y, self.z)

    def copy(self, k, source, block, dp, other_core=False):
        sems = self.near_sem if other_core else self.far_sem
        return pltpu.make_async_remote_copy(
            src_ref=source,
            dst_ref=self.full_at(self.core, block),
            send_sem=self.send_sem(k),
            recv_sem=sems(block),
            device_id={"dp": dp, "fsdp": 1 - self.core if other_core else self.core},
            device_id_type=MESH,
        )

    def across(self):
        return self.grid.at(1 - self.x, self.y, self.z)

    def along(self):
        return self.grid.at(self.x, 1 - self.y, self.z)

    def fan_out(self, k, source, block):
        self.copy(k, source, block, self.across()).start()
        self.copy(k + 1, source, block, self.along()).start()
        self.copy(k + 2, source, block, self.own, True).start()

    def own_line(self):
        for step in (1, 2, 3):
            peer = self.grid.at(self.x, self.y, self.z ^ step)
            self.copy(step - 1, self.source, self.own, peer).start()

    def own_plane(self):
        self.fan_out(3, self.source, self.own)

    def run(self, steps):
        for step in steps:
            if step == "L":
                self.own_line()
            elif step == "P":
                self.own_plane()
            elif step in "123":
                self.line(int(step))
            elif step == "c":
                self.corner()
            else:
                self.plane("ab".index(step))

    def arrive(self, block):
        arrived(self.full_at(self.core, block), self.far_sem(block))
        return self.full_at(self.core, block)

    def line(self, step):
        block = self.grid.at(self.x, self.y, self.z ^ step)
        self.fan_out(3 + 3 * step, self.arrive(block), block)

    def plane(self, half):
        even = ((self.z // 2) ^ half) * 2
        k = 15 + 6 * half
        for odd in (0, 1):
            across = self.grid.at(1 - self.x, self.y, even + odd)
            along = self.grid.at(self.x, 1 - self.y, even + odd)
            view = self.arrive(across)
            if not odd:
                self.copy(k, view, across, self.along()).start()
            self.copy(k + 2 + odd, view, across, self.own, True).start()
            view = self.arrive(along)
            if odd:
                self.copy(k + 1, view, along, self.across()).start()
            self.copy(k + 4 + odd, view, along, self.own, True).start()

    def corner(self):
        for place in range(4):
            block = self.grid.at(1 - self.x, 1 - self.y, self.z ^ place)
            self.copy(27 + place, self.arrive(block), block, self.own, True).start()

    def complete(self):
        for block in range(self.grid.count):
            arrived(self.full_at(1 - self.core, block), self.near_sem(block))

    def sent(self):
        view = self.full_at(self.core, self.own)
        for k in range(self.SENDS):
            arrived(view, self.send_sem(k))


SMALL_ROWS = 24
TILE = 640


def flatten_rows(blocks, target):
    count, rows, _ = blocks.shape

    def step(index, carry):
        both = jnp.concatenate(
            [blocks[2 * index].astype(jnp.float32), blocks[2 * index + 1].astype(jnp.float32)]
        )
        here = pl.ds(pl.multiple_of(index * 2 * rows, 2 * rows), 2 * rows)
        target[here, :] = both.astype(jnp.bfloat16)
        return carry

    lax.fori_loop(0, count // 2, step, 0)


PLAN = {
    "in": (("qa", "LP"), ("qb", "LP"), ("p", "LP")),
    "product": (
        ("o", "P"),
        ("qa", "1"),
        ("qb", "1"),
        ("p", "1"),
        ("o", "L"),
        ("qa", "23"),
        ("qb", "23"),
        ("p", "23"),
        ("qa", "a"),
        ("qb", "a"),
        ("p", "a"),
        ("i0", "L"),
        ("qa", "b"),
        ("qb", "b"),
        ("p", "b"),
        ("qa", "c"),
        ("qb", "c"),
        ("p", "c"),
    ),
    "norm": (("o", "123"), ("i1", "L")),
    "side0": (("o", "a"), ("i0", "P123"), ("i2", "L")),
    "side1": (("o", "b"), ("i1", "P123"), ("i3", "L")),
    "heads": (("o", "c"), ("i0", "ab")),
    "att": (("i2", "P123"), ("i4", "L"), ("i1", "ab"), ("i0", "c")),
}


def forward_kernel(grid, chunk, share, refs):
    (
        tokens, gains, qk_gains, qkv_flat, proj_flat, in_flat, out_flat, ada_flat,
        cotangent, conditioning, timestep, noise_bins, listed, frequencies,
        indicator, spreader, cosines, before, after, masks,
        ada_shard, qkv_shard, proj_shard, out_shard, in_shard,
        mod, cond_float, slot_kept, output, grad_residual, grad_attn, slot_sums, gain_sum, in_bias_sum, out_bias_sum,
        first_in, mod_parts, qkv_all, proj_all, out_all, in_all, in_terms, out_terms,
        keep_one, keep_query_unit, keep_key_unit, keep_query_scale, keep_key_scale,
        keep_query, keep_key, keep_values, keep_attended,
        attn_out, residual, mod_two, mod_blocks, slot_weight, first_blocks, bin_hits,
        head_gains, qkv_bias, proj_bias, in_bias, out_bias, ada_bias,
        send_sems, far_sems, near_sems, own_sems, first_send, first_recv, mod_send, mod_recv, load_sems, store_sems, keep_sems,
    ) = refs
    count = grid.count
    core = lax.axis_index("fsdp")
    own = grid.at(*grid.here())
    rows, width = tokens.shape
    length = cosines.shape[0]
    hidden = in_shard.shape[1]
    steps = hidden // chunk
    out_rows, out_half = out_shard.shape
    row_share, qkv_half = qkv_shard.shape
    proj_half = proj_shard.shape[1]

    def piece(index, source, full_at):
        return Piece(
            grid,
            source,
            full_at,
            lambda k: send_sems.at[index, k],
            lambda block: far_sems.at[index, block],
            lambda block: near_sems.at[index, block],
        )

    def out_block(side, block):
        start = pl.multiple_of(block * out_rows, out_rows)
        return out_all.at[side, pl.ds(start, out_rows)]

    def in_columns(step):
        return pl.ds(pl.multiple_of(step * chunk, chunk), chunk)

    def in_piece(step):
        cols = in_columns(step)
        return piece(
            step, in_shard.at[:, cols], lambda side, block: in_all.at[side, block, :, cols]
        )

    cut = qkv_half // 256 * 128
    qkv_parts = [
        piece(
            steps + k,
            qkv_shard.at[:, cols],
            lambda side, block, cols=cols: qkv_all.at[side, block, :, cols],
        )
        for k, cols in enumerate((slice(0, cut), slice(cut, qkv_half)))
    ]
    proj = piece(steps + 2, proj_shard, lambda side, block: proj_all.at[side, block])
    out = piece(steps + 3, out_shard, out_block)
    early = qkv_parts + [proj]

    named = {"qa": qkv_parts[0], "qb": qkv_parts[1], "p": proj, "o": out}
    named.update({"i%d" % step: in_piece(step) for step in range(steps)})

    def forward_at(point):
        for name, moves in PLAN.get(point, ()):
            named[name].run(moves)

    def keep_own(*shards):
        moves = [
            (qkv_shard, shards[0], qkv_all.at[core, own]),
            (proj_shard, shards[1], proj_all.at[core, own]),
            (out_shard, shards[2], out_block(core, own)),
            (in_shard, shards[3], in_all.at[core, own]),
        ]
        for legs in (slice(0, 2), slice(1, 3)):
            copies = [
                pltpu.make_async_copy(*move[legs], own_sems.at[k]) for k, move in enumerate(moves)
            ]
            for copy in copies:
                copy.start()
            for copy in copies:
                copy.wait()

    greet_all(count)
    slots = conditioning.shape[0]
    own_slot = lax.axis_index("dp") * slots
    bins = lax.broadcasted_iota(jnp.int32, (1, row_share), 1)
    for slot in range(slots):
        held = jnp.sum(
            (listed[...] == own_slot + slot).astype(jnp.float32), axis=1, keepdims=True
        )
        slot_kept[slot] = jnp.broadcast_to(held, (1, width))
        here = slice(slot, slot + 1)
        bin_hits[here, :] = (noise_bins[0:1, here] == bins).astype(jnp.float32) * held
        angles = timestep[0:1, here].astype(jnp.float32) * frequencies[...]
        embedded = jnp.concatenate([jnp.cos(angles), jnp.sin(angles)], axis=1)
        cond_float[here, :] = (
            (conditioning[here, :].astype(jnp.float32) + embedded)
            .astype(jnp.bfloat16)
            .astype(jnp.float32)
        )
    silu = swish(cond_float[...]).astype(jnp.bfloat16).astype(jnp.float32)
    below = jnp.concatenate(
        [
            jnp.sum(bin_hits[...], axis=0, keepdims=True),
            jnp.zeros((7 - slots, row_share), jnp.float32),
        ]
    )
    for block in range(count):
        found = jnp.concatenate(
            [silu[:, block * row_share : (block + 1) * row_share], below]
        )
        for side in range(PAIR):
            first_blocks[PAIR * block + side] = found

    def pick_first(other):
        return first_blocks.at[other]

    def pick(other):
        return mod_blocks.at[other]

    spread(count, pick_first, first_in, first_send, first_recv)
    forward_at("in")
    pl.run_scoped(
        keep_own,
        *(
            pltpu.VMEM(shard.shape, jnp.bfloat16)
            for shard in (qkv_shard, proj_shard, out_shard, in_shard)
        ),
    )
    head_gains[...] = jnp.concatenate([qk_gains[...]] * HEADS, axis=1)
    for flat, target in (
        (qkv_flat, qkv_bias),
        (proj_flat, proj_bias),
        (in_flat, in_bias),
        (out_flat, out_bias),
        (ada_flat, ada_bias),
    ):
        across, size = target.shape[1], flat.shape[0]
        line = flat[...].reshape(1, size)
        for row in range(size // across):
            target[row : row + 1, :] = line[:, row * across : (row + 1) * across]
    spread_wait(count, pick_first, first_in, first_send, first_recv)

    def begin(blocks, ada):
        loads = [
            pltpu.make_async_copy(first_in, blocks, load_sems.at[0]),
            pltpu.make_async_copy(ada_shard, ada, load_sems.at[1]),
        ]
        for load in loads:
            load.start()
        for load in loads:
            load.wait()
        counts = jnp.sum(blocks[...], axis=0)[slots : slots + 1, :]
        shares = jnp.where(counts > 0.0, share / jnp.maximum(counts, 1.0), 0.0)
        own_weight = jnp.sum(bin_hits[...] * shares, axis=1, keepdims=True)
        for slot in range(slots):
            slot_weight[slot] = jnp.broadcast_to(own_weight[slot : slot + 1, :], (1, width))
        every = blocks[...].reshape(-1, row_share).astype(jnp.bfloat16)
        for third in range(3):
            cols = slice(third * width, (third + 1) * width)
            found = product(every, ada[:, cols])
            for other in range(count * PAIR):
                mod_blocks[other, :, cols] = found[8 * other : 8 * other + slots]

    pl.run_scoped(
        begin,
        pltpu.VMEM(first_in.shape, jnp.float32),
        pltpu.VMEM(ada_shard.shape, jnp.bfloat16),
    )
    forward_at("first")
    spread(count, pick, mod_parts, mod_send, mod_recv)
    forward_at("product")

    spread_wait(count, pick, mod_parts, mod_send, mod_recv)
    forward_at("modwait")

    def gather_mod(parts):
        load = pltpu.make_async_copy(mod_parts, parts, load_sems.at[0])
        load.start()
        load.wait()
        for side in range(PAIR):
            total = parts[side]
            for block in range(1, count):
                total = total + parts[PAIR * block + side]
            for third in range(3):
                place = 3 * side + third
                for slot in range(total.shape[0]):
                    mod[slot, place : place + 1, :] = (
                        total[slot : slot + 1, third * width : (third + 1) * width]
                        + ada_bias[place : place + 1, :]
                    )

    pl.run_scoped(gather_mod, pltpu.VMEM(mod_parts.shape, jnp.float32))
    forward_at("mod")
    for part in qkv_parts:
        part.complete()
    forward_at("mod+")

    def attention(
        mod_one, query_unit, key_unit, query_scale, key_scale, query_turned, key_turned, values_low,
        attended_low,
    ):
        def lift(blocks, flat, raw):
            loads = [
                pltpu.make_async_copy(qkv_all.at[side], blocks.at[side], load_sems.at[side])
                for side in range(PAIR)
            ]
            for load in loads:
                load.start()

            def norm_first(here, slot, _):
                inputs = tokens[here, :].astype(jnp.float32)
                normed = inputs * norm_scale(inputs) * gains[0:1, :]
                mod_one[here, :] = (
                    normed * (1.0 + mod[slot, 1:2, :]) + mod[slot, 0:1, :]
                ).astype(jnp.bfloat16)

            row_loop(rows, length, norm_first)
            forward_at("norm")
            for side in range(PAIR):
                loads[side].wait()
                flatten_rows(blocks.at[side], flat)
                for cols in lane_tiles(qkv_half, 640):
                    raw[side, :, cols] = (
                        product(mod_one[...], flat[:, cols]) + qkv_bias[side : side + 1, cols]
                    )
                forward_at("side%d" % side)

            def heads(here, slot, there):
                query = raw[0, here, :width]
                key_vec = jnp.concatenate(
                    [raw[0, here, width:], raw[1, here, : 2 * width - qkv_half]], axis=1
                )
                values_low[here, :] = raw[1, here, 2 * width - qkv_half :].astype(jnp.bfloat16)
                tables = (cosines[there, :], before[there, :], after[there, :])
                for vector, gain, unit, scale, turned in (
                    (query, head_gains[0:1, :], query_unit, query_scale, query_turned),
                    (key_vec, head_gains[1:2, :], key_unit, key_scale, key_turned),
                ):
                    squares = product((vector * vector).astype(jnp.bfloat16), indicator[...])
                    factor = lax.rsqrt(squares * (1.0 / HEAD_DIM) + EPS)
                    scale[here, :] = factor
                    united = vector * spread_heads(factor, spreader[...])
                    unit[here, :] = united
                    turned[here, :] = turn(united * gain, *tables).astype(jnp.bfloat16)

            row_loop(rows, length, heads)

        pl.run_scoped(
            lift,
            pltpu.VMEM((PAIR, count, row_share, qkv_half), jnp.bfloat16),
            pltpu.VMEM((width, qkv_half), jnp.bfloat16),
            pltpu.VMEM((PAIR, rows, qkv_half), jnp.float32),
        )
        forward_at("heads")

        def attend(slot, carry):
            here = pl.ds(pl.multiple_of(slot * length, length), length)
            pieces = [None] * (width // 128)
            for head in range(HEADS):
                window = head_window(head)
                mask = masks[head : head + 1, window]
                scores = (
                    product_transposed(query_turned[here, window] * mask, key_turned[here, window])
                    * HEAD_DIM**-0.5
                )
                probs = softmax(scores).astype(jnp.bfloat16)
                found = product(probs, values_low[here, window] * mask)
                for tile in range(window.start // 128, window.stop // 128):
                    part = found[:, tile * 128 - window.start : (tile + 1) * 128 - window.start]
                    pieces[tile] = part if pieces[tile] is None else pieces[tile] + part
                    if (tile + 1) * 128 <= (head + 1) * HEAD_DIM:
                        attended_low[here, tile * 128 : (tile + 1) * 128] = pieces[tile].astype(
                            jnp.bfloat16
                        )
                        pieces[tile] = None
            return carry

        lax.fori_loop(0, rows // length, attend, 0)
        forward_at("att")
        proj.complete()

        def lower(blocks, flat):
            load = pltpu.make_async_copy(proj_all, blocks, load_sems.at[0])
            load.start()
            load.wait()
            for side in range(PAIR):
                flatten_rows(blocks.at[side], flat)
                attn_out[:, side * proj_half : (side + 1) * proj_half] = (
                    product(attended_low[...], flat[...]) + proj_bias[side : side + 1, :]
                )

        pl.run_scoped(
            lower,
            pltpu.VMEM((PAIR, count, row_share, proj_half), jnp.bfloat16),
            pltpu.VMEM((width, proj_half), jnp.bfloat16),
        )
        forward_at("proj")
        keeps = [
            pltpu.make_async_copy(source, target, keep_sems.at[k])
            for k, (source, target) in enumerate(
                (
                    (mod_one, keep_one),
                    (query_unit, keep_query_unit),
                    (key_unit, keep_key_unit),
                    (query_scale, keep_query_scale),
                    (key_scale, keep_key_scale),
                    (query_turned, keep_query),
                    (key_turned, keep_key),
                    (values_low, keep_values),
                    (attended_low, keep_attended),
                )
            )
        ]
        for keep in keeps:
            keep.start()

        def norm_second(here, slot, _):
            total = tokens[here, :].astype(jnp.float32) + mod[slot, 2:3, :] * attn_out[here, :]
            residual[here, :] = total
            normed = total * norm_scale(total) * gains[1:2, :]
            mod_two[here, :] = (normed * (1.0 + mod[slot, 4:5, :]) + mod[slot, 3:4, :]).astype(
                jnp.bfloat16
            )

        row_loop(rows, length, norm_second)
        for keep in keeps:
            keep.wait()

    low = pltpu.VMEM((rows, width), jnp.bfloat16)
    wide = pltpu.VMEM((rows, width), jnp.float32)
    compact = pltpu.VMEM((rows, 128), jnp.float32)
    pl.run_scoped(attention, low, wide, wide, compact, compact, low, low, low, low)
    forward_at("norm2")
    out.complete()
    forward_at("norm2+")

    def ffn(
        turned_two, grad_low, grad_half, lifted_grad, ffn_value,
        in_blocks, in_chunk, out_chunk, in_stage, out_stage,
    ):
        def stores(step, slot):
            return [
                pltpu.make_async_copy(
                    in_stage.at[slot], in_terms.at[:, :, :, in_columns(step)], store_sems.at[slot, 0]
                ),
                pltpu.make_async_copy(
                    out_stage.at[slot], out_terms.at[:, in_columns(step)], store_sems.at[slot, 1]
                ),
            ]

        def prepare(here, slot, _):
            grad_out = (cotangent[here, :].astype(jnp.float32) * slot_weight[slot]).astype(
                jnp.bfloat16
            )
            grad_low[here, :] = grad_out
            grad_ffn = (mod[slot, 5:6, :] * grad_out.astype(jnp.float32)).astype(jnp.bfloat16)
            grad_half[0, here, :] = grad_ffn[:, :out_half]
            grad_half[1, here, :] = grad_ffn[:, out_half:]

        row_loop(rows, length, prepare)
        turned_two[...] = mod_two[...].T
        for side in range(PAIR):
            out_bias_sum[side : side + 1, :] = jnp.sum(
                grad_half[side].astype(jnp.float32), axis=0, keepdims=True
            )
        lifted_grad[...] = jnp.zeros_like(lifted_grad)
        ffn_value[...] = jnp.zeros_like(ffn_value)

        def loads(step):
            here = in_columns(step)
            return [
                pltpu.make_async_copy(in_all.at[:, :, :, here], in_blocks, load_sems.at[0]),
                pltpu.make_async_copy(
                    out_all.at[:, here], out_chunk.at[lax.rem(step, 2)], load_sems.at[1]
                ),
            ]

        def fetch(step):
            in_piece(step).complete()
            for load in loads(step):
                load.start()

        forward_at("prep")
        fetch(0)

        def step_body(step, carry):
            slot = lax.rem(step, 2)

            for moves, ahead in (("L", 5), ("P123", 3), ("ab", 2), ("c", 1)):

                @pl.when(step + ahead < steps)
                def _(moves=moves, ahead=ahead):
                    in_piece(step + ahead).run(moves)

            here = in_columns(step)
            for load in loads(step):
                load.wait()
            for side in range(PAIR):
                flatten_rows(in_blocks.at[side], in_chunk.at[side])
            gate_part = product(mod_two[...], in_chunk[0]) + in_bias[0:1, here]
            up_part = product(mod_two[...], in_chunk[1]) + in_bias[1:2, here]
            sigmoid = 1.0 / (1.0 + jnp.exp(-gate_part))
            swished = gate_part * sigmoid
            hidden_low = (swished * up_part).astype(jnp.bfloat16)
            grad_hidden = product_transposed(grad_half[0], out_chunk[slot, 0]) + product_transposed(
                grad_half[1], out_chunk[slot, 1]
            )
            grad_gate = (
                grad_hidden * up_part * (sigmoid * (1.0 + gate_part * (1.0 - sigmoid)))
            ).astype(jnp.bfloat16)
            grad_up = (grad_hidden * swished).astype(jnp.bfloat16)
            for side in range(PAIR):
                ffn_value[side] += product(hidden_low, out_chunk[slot, side])
            lifted_grad[...] += product_transposed(grad_gate, in_chunk[0])
            lifted_grad[...] += product_transposed(grad_up, in_chunk[1])

            @pl.when(step + 1 < steps)
            def _():
                fetch(step + 1)

            @pl.when(step >= 2)
            def _():
                for store in stores(step - 2, slot):
                    store.wait()

            for side, grad in ((0, grad_gate), (1, grad_up)):
                in_bias_sum[side : side + 1, here] = jnp.sum(
                    grad.astype(jnp.float32), axis=0, keepdims=True
                )
                terms = product(turned_two[...], grad)
                for block in range(count):
                    in_stage[slot, side, block] = terms[
                        block * row_share : (block + 1) * row_share
                    ].astype(jnp.bfloat16)
            turned_hidden = hidden_low.T
            for side in range(PAIR):
                out_stage[slot, side, :, :out_half] = product(
                    turned_hidden, grad_half[side]
                ).astype(jnp.bfloat16)
            for store in stores(step, slot):
                store.start()
            return carry

        lax.fori_loop(0, steps, step_body, 0)
        slot_sums[...] = jnp.zeros_like(slot_sums)
        gain_sum[...] = jnp.zeros_like(gain_sum)

        def finish(here, slot, _):
            value = (
                jnp.concatenate([ffn_value[0, here, :], ffn_value[1, here, :]], axis=1)
                + out_bias[...]
            )
            total = residual[here, :]
            output[here, :] = ((total + mod[slot, 5:6, :] * value) * slot_kept[slot]).astype(
                jnp.bfloat16
            )
            grad_out = grad_low[here, :].astype(jnp.float32)
            factor = norm_scale(total)
            unit = total * factor
            normed = unit * gains[1:2, :]
            grad_mod = lifted_grad[here, :]
            grad_normed = grad_mod * (1.0 + mod[slot, 4:5, :])
            gradient = grad_out + norm_back(grad_normed * gains[1:2, :], unit, factor)
            grad_residual[here, :] = gradient
            grad_attn[here, :] = (mod[slot, 2:3, :] * gradient).astype(jnp.bfloat16)
            for place, terms in (
                (2, gradient * attn_out[here, :]),
                (3, grad_mod),
                (4, grad_mod * normed),
                (5, grad_out * value),
            ):
                slot_sums[slot, place : place + 1, :] += jnp.sum(terms, axis=0, keepdims=True)
            gain_sum[...] += jnp.sum(grad_normed * unit, axis=0, keepdims=True)

        row_loop(rows, length, finish)
        for step in range(steps - 2, steps):
            for store in stores(step, step % 2):
                store.wait()

    pl.run_scoped(
        ffn,
        pltpu.VMEM((width, rows), jnp.bfloat16),
        low,
        pltpu.VMEM((PAIR, rows, out_half), jnp.bfloat16),
        wide,
        pltpu.VMEM((PAIR, rows, out_half), jnp.float32),
        pltpu.VMEM((PAIR, count, row_share, chunk), jnp.bfloat16),
        pltpu.VMEM((PAIR, width, chunk), jnp.bfloat16),
        pltpu.VMEM((2, PAIR, chunk, out_half), jnp.bfloat16),
        pltpu.VMEM((2, PAIR, count, row_share, chunk), jnp.bfloat16),
        pltpu.VMEM((2, PAIR, chunk, TILE), jnp.bfloat16),
    )
    for part in early + [out]:
        part.sent()

    def sent(step, carry):
        in_piece(step).sent()
        return carry

    lax.fori_loop(0, steps, sent, 0)


def forward_call(grid, collective, share, tokens, small, tables, ada, shards):
    rows, width = tokens.shape
    count = grid.count
    total = count * PAIR
    qkv, proj, ffn_in, ffn_out = shards
    hidden, out_half = ffn_in.shape[1], ffn_out.shape[1]
    chunk = 512
    steps = hidden // chunk
    f32, bf16 = jnp.float32, jnp.bfloat16
    wide = jax.ShapeDtypeStruct((rows, width), f32)
    low = jax.ShapeDtypeStruct((rows, width), bf16)
    compact = jax.ShapeDtypeStruct((rows, 128), f32)
    slots = small[8].shape[0]
    mod_shape = (total, slots, ada.shape[1])

    def blocks(shard):
        return jax.ShapeDtypeStruct((PAIR, count) + shard.shape, bf16)

    flat_out = jax.ShapeDtypeStruct((PAIR, count * ffn_out.shape[0], out_half), bf16)
    outs = [
        jax.ShapeDtypeStruct((slots, 6, width), f32),
        jax.ShapeDtypeStruct((slots, width), f32),
        jax.ShapeDtypeStruct((slots, 1, width), f32),
        low,
        wide,
        low,
        jax.ShapeDtypeStruct((slots, 6, width), f32),
        jax.ShapeDtypeStruct((1, width), f32),
        jax.ShapeDtypeStruct((PAIR, hidden), f32),
        jax.ShapeDtypeStruct((PAIR, out_half), f32),
        jax.ShapeDtypeStruct((total, 8, qkv.shape[0]), f32),
        jax.ShapeDtypeStruct(mod_shape, f32),
        blocks(qkv),
        blocks(proj),
        flat_out,
        blocks(ffn_in),
        blocks(ffn_in),
        jax.ShapeDtypeStruct((PAIR, count * ffn_out.shape[0], TILE), bf16),
    ] + [low, wide, wide, compact, compact, low, low, low, low]
    pieces = 4 + steps
    return pl.pallas_call(
        lambda *refs: forward_kernel(grid, chunk, share, refs),
        out_shape=outs,
        in_specs=[WHOLE] * 20 + [ANY] * 5,
        out_specs=[WHOLE] * 10 + [ANY] * 17,
        scratch_shapes=[
            pltpu.VMEM((rows, width), f32),
            pltpu.VMEM((rows, width), f32),
            pltpu.VMEM((rows, width), bf16),
            pltpu.VMEM(mod_shape, f32),
            pltpu.VMEM((slots, 1, width), f32),
            pltpu.VMEM((total, 8, qkv.shape[0]), f32),
            pltpu.VMEM((slots, qkv.shape[0]), f32),
            pltpu.VMEM((2, width), f32),
            pltpu.VMEM((PAIR, qkv.shape[1]), f32),
            pltpu.VMEM((PAIR, proj.shape[1]), f32),
            pltpu.VMEM((PAIR, hidden), f32),
            pltpu.VMEM((1, width), f32),
            pltpu.VMEM((6, width), f32),
            pltpu.SemaphoreType.DMA((pieces, Piece.SENDS)),
            pltpu.SemaphoreType.DMA((pieces, count)),
            pltpu.SemaphoreType.DMA((pieces, count)),
            pltpu.SemaphoreType.DMA((4,)),
            pltpu.SemaphoreType.DMA((total,)),
            pltpu.SemaphoreType.DMA((total,)),
            pltpu.SemaphoreType.DMA((total,)),
            pltpu.SemaphoreType.DMA((total,)),
            pltpu.SemaphoreType.DMA((2,)),
            pltpu.SemaphoreType.DMA((2, 2)),
            pltpu.SemaphoreType.DMA((9,)),
        ],
        compiler_params=pltpu.CompilerParams(
            collective_id=collective, has_side_effects=True, vmem_limit_bytes=56 * 2**20
        ),
    )(tokens, *small, *tables, ada, qkv, proj, ffn_out, ffn_in)


class Total:
    HELD, PAIRED, PLANE, LINE = 4, 2, 3, 2
    SIBLING, ACROSS, ALONG, STEPS = 0, 1, 2, 2

    def __init__(self, grid, index, count, source, rows, cols, deliver, buffers):
        self.grid, self.index, self.count = grid, index, count
        self.source, self.deliver = source, deliver
        self.rows, self.cols = rows, cols
        (
            self.held_all, self.paired_all, self.turned_all, self.plane_all, self.line_all,
            self.result_all, self.send_sems, self.load_sems, self.pair_sems, self.turn_sems,
            self.plane_sems, self.line_sems, self.credits,
        ) = buffers
        self.x, self.y, self.z = grid.here()
        self.core = lax.axis_index("fsdp")

    def cut(self, ref):
        lead = (slice(None),) * (len(ref.shape) - 2)
        return ref.at[lead + (slice(0, self.rows), slice(0, self.cols))]

    @property
    def held(self):
        return self.cut(self.held_all.at[self.index % self.HELD])

    @property
    def paired(self):
        return self.cut(self.paired_all.at[self.index % self.PAIRED])

    @property
    def turned(self):
        return self.cut(self.turned_all.at[self.index % self.PLANE])

    @property
    def plane(self):
        return self.cut(self.plane_all.at[self.index % self.PLANE])

    @property
    def line(self):
        return self.cut(self.line_all.at[self.index % self.LINE])

    @property
    def result(self):
        return self.cut(self.result_all.at[self.index % self.LINE])

    def place_of(self, kind):
        if kind == self.SIBLING:
            return self.grid.at(self.x, self.y, self.z), 1 - self.core
        if kind == self.ACROSS:
            return self.grid.at(1 - self.x, self.y, self.z), self.core
        if kind == self.ALONG:
            return self.grid.at(self.x, 1 - self.y, self.z), self.core
        return self.grid.at(self.x, self.y, self.z ^ (kind - self.STEPS)), self.core

    def give(self, kinds, ahead):
        if self.index + ahead < self.count:
            for kind in kinds:
                dp, core = self.place_of(kind)
                pl.semaphore_signal(
                    self.credits.at[kind],
                    inc=1,
                    device_id={"dp": dp, "fsdp": core},
                    device_id_type=MESH,
                )

    def take(self, kinds, ahead):
        if self.index >= ahead:
            for kind in kinds:
                pl.semaphore_wait(self.credits.at[kind], 1)

    def send(self, k, source, target, recv_sem, dp):
        pltpu.make_async_remote_copy(
            src_ref=source,
            dst_ref=target,
            send_sem=self.send_sems.at[self.index, k],
            recv_sem=recv_sem,
            device_id={"dp": dp, "fsdp": self.core},
            device_id_type=MESH,
        ).start()

    def pair_copy(self):
        return pltpu.make_async_remote_copy(
            src_ref=self.source(1 - self.core),
            dst_ref=self.paired,
            send_sem=self.send_sems.at[self.index, 15],
            recv_sem=self.pair_sems.at[self.index],
            device_id={"dp": self.grid.at(self.x, self.y, self.z), "fsdp": 1 - self.core},
            device_id_type=MESH,
        )

    def begin(self):
        self.take((self.SIBLING,), self.PAIRED)
        self.pair_copy().start()
        pltpu.make_async_copy(
            self.source(self.core), self.held, self.load_sems.at[self.index]
        ).start()

    def sent(self):
        block = self.held.at[0]
        for k in range(15):
            arrived(block, self.send_sems.at[self.index, k])
        self.pair_copy().wait_send()

    def pair_sum(self, block):
        held, paired = self.held, self.paired
        held[block] = (
            held[block].astype(jnp.float32) + paired[block].astype(jnp.float32)
        ).astype(jnp.bfloat16)

    def sides(self, place, odd):
        across = self.grid.at(1 - self.x, self.y, place)
        along = self.grid.at(self.x, 1 - self.y, place)
        return odd * across + (1 - odd) * along, odd * along + (1 - odd) * across

    def start(self):
        arrived(self.held, self.load_sems.at[self.index])
        arrived(self.paired, self.pair_sems.at[self.index])
        self.take((self.ACROSS, self.ALONG), self.PLANE)
        across = self.grid.at(1 - self.x, self.y, self.z)
        along = self.grid.at(self.x, 1 - self.y, self.z)
        held, turned, plane = self.held, self.turned, self.plane

        def corner(step, carry):
            place = self.z ^ (3 - step)
            odd = lax.rem(place, 2)
            block = self.grid.at(1 - self.x, 1 - self.y, place)
            self.pair_sum(block)
            self.send(
                step,
                held.at[block],
                turned.at[place],
                self.turn_sems.at[self.index, place],
                odd * across + (1 - odd) * along,
            )
            return carry

        lax.fori_loop(0, 4, corner, 0)

        def side(step, carry):
            place = self.z ^ (3 - step)
            odd = lax.rem(place, 2)
            passed, added = self.sides(place, odd)
            self.pair_sum(passed)
            self.send(
                4 + step,
                held.at[passed],
                plane.at[1 - odd, place],
                self.plane_sems.at[self.index, 1 - odd, place],
                odd * across + (1 - odd) * along,
            )
            self.pair_sum(added)
            return carry

        lax.fori_loop(0, 4, side, 0)

        def column(step, carry):
            self.pair_sum(self.grid.at(self.x, self.y, step))
            return carry

        lax.fori_loop(0, 4, column, 0)
        self.give((self.SIBLING,), self.PAIRED)

    def turn(self):
        held, turned, plane = self.held, self.turned, self.plane
        across = self.grid.at(1 - self.x, self.y, self.z)
        along = self.grid.at(self.x, 1 - self.y, self.z)

        def step_body(step, carry):
            place = self.z ^ (3 - step)
            odd = lax.rem(place, 2)
            _, block = self.sides(place, odd)
            arrived(turned.at[place], self.turn_sems.at[self.index, place])
            held[block] = (
                held[block].astype(jnp.float32) + turned[place].astype(jnp.float32)
            ).astype(jnp.bfloat16)
            self.send(
                8 + step,
                held.at[block],
                plane.at[odd, place],
                self.plane_sems.at[self.index, odd, place],
                odd * along + (1 - odd) * across,
            )
            return carry

        lax.fori_loop(0, 4, step_body, 0)

    def column(self):
        held, plane, line = self.held, self.plane, self.line
        self.take([self.STEPS + step for step in (1, 2, 3)], self.LINE)

        def total(place):
            for kind in (0, 1):
                arrived(plane.at[kind, place], self.plane_sems.at[self.index, kind, place])
            return (
                held[self.grid.at(self.x, self.y, place)].astype(jnp.float32)
                + plane[0, place].astype(jnp.float32)
                + plane[1, place].astype(jnp.float32)
            )

        def step_body(step, carry):
            place = self.z ^ (3 - step)
            block = self.grid.at(self.x, self.y, place)
            held[block] = total(place).astype(jnp.bfloat16)
            self.send(
                12 + step,
                held.at[block],
                line.at[self.z],
                self.line_sems.at[self.index, self.z],
                block,
            )
            return carry

        lax.fori_loop(0, 3, step_body, 0)
        self.result[...] = total(self.z)
        self.give((self.ACROSS, self.ALONG), self.PLANE)

    def end(self):
        line = self.line
        total = self.result[...]
        for step in (1, 2, 3):
            place = self.z ^ step
            arrived(line.at[place], self.line_sems.at[self.index, place])
            total = total + line[place].astype(jnp.float32)
        self.deliver(total)
        self.give([self.STEPS + step for step in (1, 2, 3)], self.LINE)


class Relay:
    def __init__(self, parts):
        self.parts, self.slot = parts, 0

    def part(self, back):
        place = self.slot - back
        return self.parts[place] if 0 <= place < len(self.parts) else None

    def more(self, slots=1):
        for _ in range(slots):
            for back, step in ((4, "end"), (3, "column"), (2, "turn"), (1, "start")):
                if self.part(back):
                    getattr(self.part(back), step)()
            if self.part(0):
                if self.part(Total.HELD):
                    self.part(Total.HELD).sent()
                self.part(0).begin()
            self.slot += 1

    def finish(self):
        while self.slot < len(self.parts) + 4:
            self.more()
        for part in self.parts[-Total.HELD :]:
            part.sent()


def backward_kernel(grid, refs):
    (
        mod, cond_float, gains, qk_gains, indicator, spreader, cosines, before, after, masks,
        slot_kept,
        late_sums, late_gain, in_bias_sum, out_bias_sum, silu_rows,
        tokens, keep_one, keep_query_unit, keep_key_unit, keep_query_scale, keep_key_scale,
        keep_query, keep_key, keep_values, keep_attended, grad_residual_hbm, grad_attn_hbm,
        qkv_all, proj_all, in_terms, out_terms, ada_shard,
        input_grad, in_grad, out_grad, qkv_grad, proj_grad, ada_grad, cond_grad,
        ada_bias_grad, qkv_bias_grad, proj_bias_grad, in_bias_grad, out_bias_grad, norm_grad,
        head_grad,
        cond_parts, every_mod, qkv_terms, proj_terms,
        held, paired, turned_in, plane_in, line_in, result, small_in, mod_halves, cond_blocks, small,
        head_gains,
        send_sems, load_sems, pair_sems, turn_sems, plane_sems, line_sems, credits,
        small_send, small_recv, mod_send, mod_recv, cond_send, cond_recv, local_sems, store_sems,
    ) = refs
    count = grid.count
    rows, width = tokens.shape
    length = cosines.shape[0]
    slots = rows // length
    hidden = in_grad.shape[1]
    qkv_half = qkv_all.shape[3]
    proj_half = proj_all.shape[3]
    row_share = qkv_all.shape[2]
    third = out_grad.shape[0] // 3
    out_half = out_grad.shape[1]
    x, y, z = grid.here()
    core = lax.axis_index("fsdp")
    greet_all(count)
    head_gains[...] = jnp.concatenate([qk_gains[...]] * HEADS, axis=1)

    buffers = (
        held, paired, turned_in, plane_in, line_in, result,
        send_sems, load_sems, pair_sems, turn_sems, plane_sems, line_sems, credits,
    )
    plans = []
    for cols in lane_tiles(hidden, TILE):

        def deliver(total, cols=cols):
            in_grad[:, cols] = total

        plans.append(
            (
                lambda side, cols=cols: in_terms.at[side, :, :, cols],
                row_share,
                cols.stop - cols.start,
                deliver,
            )
        )
    for place in range(3):
        here = slice(place * third, (place + 1) * third)

        def deliver(total, here=here):
            out_grad[here, :] = total[:, :out_half]

        plans.append((lambda side, here=here: out_terms.at[side, :, here], third, TILE, deliver))

    def deliver_proj(total):
        proj_grad[...] = total[:, :proj_half]

    plans.append((lambda side: proj_terms.at[side], row_share, TILE, deliver_proj))
    for cols in lane_tiles(qkv_half, TILE):

        def deliver(total, cols=cols):
            qkv_grad[:, cols] = total[:, : cols.stop - cols.start]

        wide_cols = slice(cols.start, cols.start + TILE)
        plans.append(
            (
                lambda side, wide_cols=wide_cols: qkv_terms.at[side, :, :, wide_cols],
                row_share,
                TILE,
                deliver,
            )
        )
    relay = Relay(
        [Total(grid, index, len(plans), *plan, buffers) for index, plan in enumerate(plans)]
    )
    relay.more(2)

    def fetch(*pairs):
        copies = [
            pltpu.make_async_copy(source, target, local_sems.at[k])
            for k, (source, target) in enumerate(pairs)
        ]
        for copy in copies:
            copy.start()
        return copies

    def body(grad_half, lifted_grad):
        def heads_part(grad_query, grad_key, grad_values, grad_attended):
            def first(blocks, flat, attended_low, grad_attn, turned, stage):
                loads = fetch(
                    (keep_attended, attended_low), (grad_attn_hbm, grad_attn), (proj_all, blocks)
                )
                for load in loads:
                    load.wait()
                turned[...] = attended_low[...].T
                for side in range(PAIR):
                    cols = slice(side * proj_half, (side + 1) * proj_half)
                    small[9:10, cols] = jnp.sum(
                        grad_attn[:, cols].astype(jnp.float32), axis=0, keepdims=True
                    )
                    flatten_rows(blocks.at[side], flat)
                    found = product_transposed(grad_attn[:, cols], flat[...])
                    if side == 0:
                        grad_query[...] = found
                    else:
                        grad_attended[...] = (grad_query[...] + found).astype(jnp.bfloat16)
                    terms = product(turned[...], grad_attn[:, cols])
                    for block in range(count):
                        stage[side, block, :, :proj_half] = terms[
                            block * row_share : (block + 1) * row_share
                        ].astype(jnp.bfloat16)
                store = pltpu.make_async_copy(stage, proj_terms, store_sems.at[0])
                store.start()
                store.wait()

            low = pltpu.VMEM((rows, width), jnp.bfloat16)
            pl.run_scoped(
                first,
                pltpu.VMEM((PAIR, count, row_share, proj_half), jnp.bfloat16),
                pltpu.VMEM((width, proj_half), jnp.bfloat16),
                low,
                low,
                pltpu.VMEM((width, rows), jnp.bfloat16),
                pltpu.VMEM((PAIR, count, row_share, TILE), jnp.bfloat16),
            )
            relay.more(1)

            def second(query_turned, key_turned, values_low):
                loads = fetch(
                    (keep_query, query_turned), (keep_key, key_turned), (keep_values, values_low)
                )
                for load in loads:
                    load.wait()

                def attend(slot):
                    here = slice(slot * length, (slot + 1) * length)
                    pieces = [[None] * (width // 128) for _ in range(3)]
                    for head in range(HEADS):
                        window = head_window(head)
                        mask = masks[head : head + 1, window]
                        query = query_turned[here, window] * mask
                        key_vec = key_turned[here, window]
                        value = values_low[here, window]
                        grad = grad_attended[here, window] * mask
                        probs = softmax(product_transposed(query, key_vec) * HEAD_DIM**-0.5)
                        grad_probs = product_transposed(grad, value)
                        grad_scores = (
                            probs
                            * (grad_probs - jnp.sum(probs * grad_probs, axis=-1, keepdims=True))
                        ).astype(jnp.bfloat16)
                        founds = (
                            product(grad_scores, key_vec * mask) * HEAD_DIM**-0.5,
                            transposed_product(grad_scores, query) * HEAD_DIM**-0.5,
                            transposed_product(probs.astype(jnp.bfloat16), grad),
                        )
                        for kind, (found, target) in enumerate(
                            zip(founds, (grad_query, grad_key, grad_values))
                        ):
                            for tile in range(window.start // 128, window.stop // 128):
                                begin = tile * 128 - window.start
                                part = found[:, begin : begin + 128]
                                kept = pieces[kind][tile]
                                kept = part if kept is None else kept + part
                                pieces[kind][tile] = kept
                                if (tile + 1) * 128 <= (head + 1) * HEAD_DIM:
                                    target[here, tile * 128 : (tile + 1) * 128] = kept

                for slot in range(slots):
                    attend(slot)
                    relay.more(1)

            pl.run_scoped(second, low, low, low)

            def third_part(query_unit, key_unit, query_scale, key_scale):
                loads = fetch(
                    (keep_query_unit, query_unit),
                    (keep_key_unit, key_unit),
                    (keep_query_scale, query_scale),
                    (keep_key_scale, key_scale),
                )
                for load in loads:
                    load.wait()
                small[13:15, :] = jnp.zeros((2, width), jnp.float32)

                def heads(here, slot, there):
                    tables = (cosines[there, :], before[there, :], after[there, :])
                    founds = []
                    for kind, (grad, gain, unit, scale) in enumerate(
                        (
                            (grad_query, head_gains[0:1, :], query_unit, query_scale),
                            (grad_key, head_gains[1:2, :], key_unit, key_scale),
                        )
                    ):
                        normed = turn(grad[here, :], *tables, sign=-1.0)
                        united = unit[here, :]
                        small[13 + kind : 14 + kind, :] += jnp.sum(
                            normed * united, axis=0, keepdims=True
                        )
                        normed = normed * gain
                        means = product(
                            (normed * united).astype(jnp.bfloat16), indicator[...]
                        ) * (1.0 / HEAD_DIM)
                        founds.append(
                            spread_heads(scale[here, :], spreader[...])
                            * (normed - united * spread_heads(means, spreader[...]))
                        )
                    cut = qkv_half - width
                    grad_half[0, here, :width] = founds[0].astype(jnp.bfloat16)
                    grad_half[0, here, width:] = founds[1][:, :cut].astype(jnp.bfloat16)
                    grad_half[1, here, : width - cut] = founds[1][:, cut:].astype(jnp.bfloat16)
                    grad_half[1, here, width - cut :] = grad_values[here, :].astype(jnp.bfloat16)

                row_loop(rows, length, heads)

            compact = pltpu.VMEM((rows, 128), jnp.float32)
            wide = pltpu.VMEM((rows, width), jnp.float32)
            pl.run_scoped(third_part, wide, wide, compact, compact)

        wide = pltpu.VMEM((rows, width), jnp.float32)
        low = pltpu.VMEM((rows, width), jnp.bfloat16)
        pl.run_scoped(heads_part, wide, wide, wide, low)
        relay.more(1)

        def fourth(mod_one, turned, blocks, flat, stage):
            fetch((keep_one, mod_one))[0].wait()
            turned[...] = mod_one[...].T
            number = 0
            stores = []
            for side in range(PAIR):
                fetch((qkv_all.at[side], blocks))[0].wait()
                flatten_rows(blocks, flat)
                for tile in range(3):
                    sums = jnp.sum(
                        grad_half[side, :, tile * 576 : (tile + 1) * 576].astype(jnp.float32),
                        axis=0,
                        keepdims=True,
                    )
                    start = side * qkv_half + tile * 576
                    small[
                        6 + start // width : 7 + start // width,
                        start % width : start % width + 576,
                    ] = sums
                for cols in lane_tiles(width, 384):
                    found = product_transposed(grad_half[side], flat[cols, :])
                    if side == 0:
                        lifted_grad[:, cols] = found
                    else:
                        lifted_grad[:, cols] += found
                for cols in lane_tiles(qkv_half, TILE):
                    terms = product(turned[...], grad_half[side, :, cols])
                    if number >= 2:
                        stores[number - 2].wait()
                    for block in range(count):
                        stage[number % 2, block, :, : cols.stop - cols.start] = terms[
                            block * row_share : (block + 1) * row_share
                        ].astype(jnp.bfloat16)
                    stores.append(
                        pltpu.make_async_copy(
                            stage.at[number % 2],
                            qkv_terms.at[side, :, :, cols.start : cols.start + TILE],
                            store_sems.at[number % 2],
                        )
                    )
                    stores[-1].start()
                    number += 1
                if side == 0:
                    relay.more(1)
            for store in stores[-2:]:
                store.wait()

        pl.run_scoped(
            fourth,
            low,
            pltpu.VMEM((width, rows), jnp.bfloat16),
            pltpu.VMEM((count, row_share, qkv_half), jnp.bfloat16),
            pltpu.VMEM((width, qkv_half), jnp.bfloat16),
            pltpu.VMEM((2, count, row_share, TILE), jnp.bfloat16),
        )
        relay.more(1)

        def last(token_rows, grad_residual, early):
            for load in fetch((tokens, token_rows), (grad_residual_hbm, grad_residual)):
                load.wait()
            early[...] = late_sums[...]
            small[11:12, :] = jnp.zeros((1, width), jnp.float32)
            small[12:13, :] = late_gain[...]

            def finish(here, slot, _):
                inputs = token_rows[here, :].astype(jnp.float32)
                factor = norm_scale(inputs)
                unit = inputs * factor
                normed = unit * gains[0:1, :]
                grad_mod = lifted_grad[here, :]
                grad_normed = grad_mod * (1.0 + mod[slot, 1:2, :])
                gradient = grad_residual[here, :] + norm_back(
                    grad_normed * gains[0:1, :], unit, factor
                )
                input_grad[here, :] = (gradient * slot_kept[slot]).astype(jnp.bfloat16)
                for place, terms in ((0, grad_mod), (1, grad_mod * normed)):
                    early[slot, place : place + 1, :] += jnp.sum(terms, axis=0, keepdims=True)
                small[11:12, :] += jnp.sum(grad_normed * unit, axis=0, keepdims=True)

            row_loop(rows, length, finish)
            for place in range(6):
                low_sums = jnp.concatenate(
                    [early[slot, place : place + 1, :] for slot in range(slots)]
                ).astype(jnp.bfloat16)
                mod_halves[place // 3, :, (place % 3) * width : (place % 3 + 1) * width] = low_sums
                small[place : place + 1, :] = jnp.sum(
                    low_sums.astype(jnp.float32), axis=0, keepdims=True
                )

        pl.run_scoped(last, low, wide, pltpu.VMEM(late_sums.shape, jnp.float32))

    pl.run_scoped(
        body,
        pltpu.VMEM((PAIR, rows, qkv_half), jnp.bfloat16),
        pltpu.VMEM((rows, width), jnp.float32),
    )

    def pick(other):
        return mod_halves.at[lax.rem(other, PAIR)]

    spread(count, pick, every_mod, mod_send, mod_recv)
    for side in range(PAIR):
        small[10:11, side * out_half : (side + 1) * out_half] = out_bias_sum[side : side + 1, :]
        for part in range(3):
            wide_part = min(width, hidden - part * width)
            row = 15 + 3 * side + part
            if wide_part < width:
                small[row : row + 1, :] = jnp.zeros((1, width), jnp.float32)
            small[row : row + 1, :wide_part] = in_bias_sum[
                side : side + 1, part * width : part * width + wide_part
            ]
    small[21:, :] = jnp.zeros((SMALL_ROWS - 21, width), jnp.float32)
    peers = [
        (grid.at(x, y, z), 1 - core),
        (grid.at(1 - x, y, z), core),
        (grid.at(x, 1 - y, z), core),
        (grid.at(x, y, z ^ 1), core),
        (grid.at(x, y, z ^ 2), core),
    ]
    for k, (dp, other) in enumerate(peers):
        copy = pltpu.make_async_remote_copy(
            src_ref=small,
            dst_ref=small_in.at[k],
            send_sem=small_send.at[k],
            recv_sem=small_recv.at[k],
            device_id={"dp": dp, "fsdp": other},
            device_id_type=MESH,
        )
        copy.start()
        relay.more(1)
        copy.wait()
        small[...] = small[...] + small_in[k]
    spread_wait(count, pick, every_mod, mod_send, mod_recv)

    def condition(parts, flat, ada):
        for load in fetch((every_mod, parts), (ada_shard, ada)):
            load.wait()
        for other in range(count * PAIR):
            flat[slots * other : slots * (other + 1), :] = parts[other].astype(jnp.float32)
        grads = flat[...].astype(jnp.bfloat16)
        ada_grad[...] = transposed_product(silu_rows[...], grads)
        found = product_transposed(grads, ada[...])
        for other in range(count * PAIR):
            cond_blocks[other] = found[slots * other : slots * (other + 1), :]

    pl.run_scoped(
        condition,
        pltpu.VMEM(every_mod.shape, jnp.bfloat16),
        pltpu.VMEM((count * PAIR * slots, every_mod.shape[2]), jnp.float32),
        pltpu.VMEM(ada_shard.shape, jnp.bfloat16),
    )

    def pick_cond(other):
        return cond_blocks.at[other]

    spread(count, pick_cond, cond_parts, cond_send, cond_recv)
    relay.finish()
    for target, row in ((ada_bias_grad, 0), (qkv_bias_grad, 6), (proj_bias_grad, 9), (out_bias_grad, 10)):
        for part in range(target.shape[0] // width):
            target[pl.ds(part * width, width)] = small[row + part]
    for side in range(PAIR):
        for part in range(3):
            wide_part = min(width, hidden - part * width)
            in_bias_grad[pl.ds(side * hidden + part * width, wide_part)] = small[
                15 + 3 * side + part, :wide_part
            ]
    norm_grad[...] = small[11:13, :]
    sums = small[13:15, :]
    found = sums[:, :HEAD_DIM]
    for head in range(1, HEADS):
        found = found + sums[:, head * HEAD_DIM : (head + 1) * HEAD_DIM]
    head_grad[...] = found
    spread_wait(count, pick_cond, cond_parts, cond_send, cond_recv)

    def settle(parts):
        fetch((cond_parts, parts))[0].wait()
        found = jnp.concatenate(
            [parts[PAIR * block] + parts[PAIR * block + 1] for block in range(count)], axis=1
        )
        kept = jnp.concatenate([slot_kept[slot] for slot in range(slots)])
        cond_grad[...] = found * swish_slope(cond_float[...]) * kept

    pl.run_scoped(settle, pltpu.VMEM(cond_parts.shape, jnp.float32))


def backward_call(grid, collective, whole, parts):
    count = grid.count
    total = count * PAIR
    f32, bf16 = jnp.float32, jnp.bfloat16
    tokens, grad_residual = parts[0], parts[10]
    qkv_all, proj_all, in_terms, out_terms, ada = parts[12:]
    rows, width = tokens.shape
    row_share = qkv_all.shape[2]
    slots = whole[0].shape[0]
    half_width = 3 * width
    qkv_half, proj_half, hidden = qkv_all.shape[3], proj_all.shape[3], in_terms.shape[3]
    out_rows = out_terms.shape[2]
    qkv_tiles = len(lane_tiles(qkv_half, TILE))
    pieces = len(lane_tiles(hidden, TILE)) + 3 + 1 + qkv_tiles
    block = (row_share, TILE)
    return pl.pallas_call(
        lambda *refs: backward_kernel(grid, refs),
        out_shape=[
            jax.ShapeDtypeStruct((rows, width), bf16),
            jax.ShapeDtypeStruct((row_share, hidden), f32),
            jax.ShapeDtypeStruct((out_rows, proj_half), f32),
            jax.ShapeDtypeStruct((row_share, qkv_half), f32),
            jax.ShapeDtypeStruct((row_share, proj_half), f32),
            jax.ShapeDtypeStruct(ada.shape, f32),
            jax.ShapeDtypeStruct((slots, width), f32),
            jax.ShapeDtypeStruct((6 * width,), f32),
            jax.ShapeDtypeStruct((PAIR * qkv_half,), f32),
            jax.ShapeDtypeStruct((width,), f32),
            jax.ShapeDtypeStruct((PAIR * hidden,), f32),
            jax.ShapeDtypeStruct((width,), f32),
            jax.ShapeDtypeStruct((2, width), f32),
            jax.ShapeDtypeStruct((2, HEAD_DIM), f32),
            jax.ShapeDtypeStruct((total, slots, row_share), f32),
            jax.ShapeDtypeStruct((total, slots, half_width), bf16),
            jax.ShapeDtypeStruct((PAIR, count, row_share, qkv_tiles * TILE), bf16),
            jax.ShapeDtypeStruct((PAIR, count, row_share, TILE), bf16),
        ],
        in_specs=[WHOLE] * len(whole) + [ANY] * len(parts),
        out_specs=[WHOLE] * 14 + [ANY] * 4,
        scratch_shapes=[
            pltpu.VMEM((Total.HELD, count) + block, bf16),
            pltpu.VMEM((Total.PAIRED, count) + block, bf16),
            pltpu.VMEM((Total.PLANE, 4) + block, bf16),
            pltpu.VMEM((Total.PLANE, 2, 4) + block, bf16),
            pltpu.VMEM((Total.LINE, 4) + block, bf16),
            pltpu.VMEM((Total.LINE,) + block, f32),
            pltpu.VMEM((5, SMALL_ROWS, width), f32),
            pltpu.VMEM((PAIR, slots, half_width), bf16),
            pltpu.VMEM((total, slots, row_share), f32),
            pltpu.VMEM((SMALL_ROWS, width), f32),
            pltpu.VMEM((2, width), f32),
            pltpu.SemaphoreType.DMA((pieces, 16)),
            pltpu.SemaphoreType.DMA((pieces,)),
            pltpu.SemaphoreType.DMA((pieces,)),
            pltpu.SemaphoreType.DMA((pieces, 4)),
            pltpu.SemaphoreType.DMA((pieces, 2, 4)),
            pltpu.SemaphoreType.DMA((pieces, 4)),
            pltpu.SemaphoreType.REGULAR((6,)),
            pltpu.SemaphoreType.DMA((5,)),
            pltpu.SemaphoreType.DMA((5,)),
            pltpu.SemaphoreType.DMA((total,)),
            pltpu.SemaphoreType.DMA((total,)),
            pltpu.SemaphoreType.DMA((total,)),
            pltpu.SemaphoreType.DMA((total,)),
            pltpu.SemaphoreType.DMA((4,)),
            pltpu.SemaphoreType.DMA((2,)),
        ],
        compiler_params=pltpu.CompilerParams(
            collective_id=collective, has_side_effects=True, vmem_limit_bytes=56 * 2**20
        ),
    )(*whole, *parts)


def deliver_call(arrays):
    def kernel(*refs):
        sources, targets, sems = refs[: len(arrays)], refs[len(arrays) : -1], refs[-1]
        copies = [
            pltpu.make_async_copy(source, target, sems.at[k])
            for k, (source, target) in enumerate(zip(sources, targets))
        ]
        for copy in copies:
            copy.start()
        for copy in copies:
            copy.wait()

    return pl.pallas_call(
        kernel,
        out_shape=[jax.ShapeDtypeStruct(a.shape, a.dtype) for a in arrays],
        in_specs=[WHOLE] * len(arrays),
        out_specs=[ANY] * len(arrays),
        scratch_shapes=[pltpu.SemaphoreType.DMA((len(arrays),))],
        compiler_params=pltpu.CompilerParams(vmem_limit_bytes=56 * 2**20),
    )(*arrays)


def fused_block(
    grid,
    tokens,
    conditioning,
    timestep,
    noise_bins,
    source_slot,
    cotangent,
    ada_weight,
    qkv_weight,
    proj_weight,
    ffn_in_weight,
    ffn_out_weight,
    ada_bias,
    qkv_bias,
    proj_bias,
    ffn_in_bias,
    ffn_out_bias,
    norm_gains,
    qk_gains,
):
    capacity, length, model_width = tokens.shape[1:]
    rows = capacity * length
    group_items = source_slot.shape[1]
    half_width = model_width // 2
    frequencies = np.exp(
        -math.log(10000.0) * np.arange(half_width, dtype=np.float32) / half_width
    ).astype(np.float32)
    tables = head_tables()
    token_rows = tokens.reshape(rows, model_width)
    results = forward_call(
        grid,
        1,
        group_items * PAIR / NBINS,
        token_rows,
        (
            norm_gains,
            qk_gains,
            qkv_bias,
            proj_bias,
            ffn_in_bias,
            ffn_out_bias,
            ada_bias,
            cotangent.reshape(rows, model_width),
            conditioning[0],
            timestep,
            noise_bins,
            source_slot,
            jnp.asarray(frequencies)[None],
        ),
        tables,
        ada_weight,
        (qkv_weight, proj_weight, ffn_in_weight, ffn_out_weight),
    )
    (
        modulation,
        cond_float,
        slot_kept,
        output_rows,
        grad_residual,
        grad_attn,
        late_sums,
        late_gain,
        in_bias_sum,
        out_bias_sum,
        first_in,
        _,
        qkv_all,
        proj_all,
        _,
        _,
        in_terms,
        out_terms,
        *kept,
    ) = results
    silu_rows = first_in[:, :capacity].reshape(-1, first_in.shape[2]).astype(jnp.bfloat16)
    whole = (
        modulation,
        cond_float,
        norm_gains,
        qk_gains,
        *tables,
        slot_kept,
        late_sums,
        late_gain,
        in_bias_sum,
        out_bias_sum,
        silu_rows,
    )
    parts = (
        token_rows,
        *kept,
        grad_residual,
        grad_attn,
        qkv_all,
        proj_all,
        in_terms,
        out_terms.reshape(PAIR, grid.count, -1, out_terms.shape[2]),
        ada_weight,
    )
    (
        grad_rows,
        in_grad,
        out_grad,
        qkv_grad,
        proj_grad,
        ada_grad,
        cond_grad,
        *small,
    ) = backward_call(grid, 2, whole, parts)[:14]
    delivered = deliver_call(
        (
            output_rows,
            grad_rows,
            cond_grad,
            ada_grad,
            qkv_grad,
            proj_grad,
            in_grad,
            out_grad,
            *small,
        )
    )
    return (
        delivered[0].reshape(tokens.shape),
        delivered[1].reshape(tokens.shape),
        delivered[2][None],
        *delivered[3:],
    )


def per_device(
    grid,
    tokens,
    conditioning,
    timestep,
    noise_bins,
    source_slot,
    cotangent,
    ada_weight,
    qkv_weight,
    proj_weight,
    ffn_in_weight,
    ffn_out_weight,
    ada_bias,
    qkv_bias,
    proj_bias,
    ffn_in_bias,
    ffn_out_bias,
    norm_gains,
    qk_gains,
):
    if grid.plain:
        return fused_block(
            grid,
            tokens,
            conditioning,
            timestep,
            noise_bins,
            source_slot,
            cotangent,
            ada_weight,
            qkv_weight,
            proj_weight,
            ffn_in_weight,
            ffn_out_weight,
            ada_bias,
            qkv_bias,
            proj_bias,
            ffn_in_bias,
            ffn_out_bias,
            norm_gains,
            qk_gains,
        )
    dp_count = lax.axis_size("dp")
    pair_count = lax.axis_size("fsdp")
    capacity = tokens.shape[1]
    length = tokens.shape[2]
    model_width = tokens.shape[3]
    listed = source_slot[0]
    group_items = listed.shape[0]
    row_count = capacity * length
    own_index = lax.axis_index("dp")
    own_slots = own_index * capacity + jnp.arange(capacity, dtype=jnp.int32)
    held = jnp.any(listed[None, :] == own_slots[:, None], axis=1)
    bin_hits = (
        noise_bins[0][:, None] == jnp.arange(NBINS, dtype=jnp.int32)[None, :]
    ) & held[:, None]
    local_counts = jnp.sum(bin_hits.astype(jnp.float32), axis=0)
    cond_float = lax.reduce_precision(
        conditioning[0].astype(jnp.float32) + time_embed(timestep[0], model_width), 8, 7
    )
    silu_cond = swish(cond_float).astype(jnp.bfloat16)
    row_share, half_width = ada_weight.shape
    total = dp_count * pair_count
    silu_blocks = jnp.repeat(
        silu_cond.reshape(capacity, dp_count, row_share).transpose(1, 0, 2), pair_count, axis=0
    )
    shards = (qkv_weight, proj_weight, ffn_in_weight, ffn_out_weight)
    share = group_items * pair_count / NBINS
    token_rows = tokens.reshape(row_count, model_width)
    cotangent_rows = cotangent.reshape(row_count, model_width)
    tables = head_tables()
    head_gains = jnp.tile(qk_gains, (1, HEADS))
    lanes = (capacity, 1, model_width)
    slot_kept = jnp.broadcast_to(held.astype(jnp.float32)[:, None, None], lanes)
    qkv_halves, proj_halves, in_halves = [
        bias.reshape(pair_count, -1) for bias in (qkv_bias, proj_bias, ffn_in_bias)
    ]
    every_count = lax.all_gather(local_counts, ("dp", "fsdp"))
    bin_share = share / jnp.sum(every_count, axis=0)
    slot_weight = jnp.sum(jnp.where(bin_hits, bin_share[None, :], 0.0), axis=1)
    weight_lanes = jnp.broadcast_to(slot_weight[:, None, None], lanes)
    silu_rows = lax.all_to_all(silu_blocks, ("dp", "fsdp"), 0, 0, tiled=True)
    silu_rows = silu_rows.reshape(total * capacity, row_share)
    mod_blocks = product(silu_rows, ada_weight).reshape(total, capacity, half_width)
    mod_parts = lax.all_to_all(mod_blocks, ("dp", "fsdp"), 0, 0, tiled=True)
    modulation = (
        jnp.sum(mod_parts.reshape(dp_count, pair_count, capacity, half_width), axis=0)
        .transpose(1, 0, 2)
        .reshape(capacity, -1)
        + ada_bias
    ).reshape(capacity, 6, model_width)
    fulls = [lax.all_gather(lax.all_gather(s, "dp"), "fsdp") for s in shards]
    qkv_full, proj_full, ffn_in_full, ffn_out_full = [
        full.reshape(pair_count, -1, full.shape[3]) for full in fulls
    ]
    forward = attention_forward_call(
        token_rows,
        modulation,
        norm_gains,
        head_gains,
        qkv_halves,
        proj_halves,
        tables,
        qkv_full,
        proj_full,
    )
    kept, (attn_out, residual, mod_two) = forward[:9], forward[9:]
    *middle, in_terms, out_terms = ffn_call(
        mod_two,
        residual,
        attn_out,
        cotangent_rows,
        weight_lanes,
        slot_kept,
        modulation,
        norm_gains,
        in_halves,
        ffn_out_bias[None],
        ffn_in_full,
        ffn_out_full,
    )
    (
        output_rows,
        grad_residual,
        grad_attn,
        late_sums,
        late_gain,
        in_bias_sum,
        out_bias_sum,
    ) = middle
    (
        grad_rows,
        early_sums,
        early_gain,
        head_sums,
        qkv_bias_sum,
        proj_bias_sum,
        qkv_terms,
        proj_terms,
    ) = attention_backward_call(
        token_rows,
        modulation,
        norm_gains,
        head_gains,
        tables,
        slot_kept,
        kept,
        grad_residual,
        grad_attn,
        qkv_full,
        proj_full,
    )
    ffn_grads, attn_grads = [
        [
            lax.psum_scatter(
                lax.psum_scatter(
                    term.reshape(pair_count, dp_count, -1, term.shape[-1]), "fsdp"
                ),
                "dp",
            ).astype(jnp.float32)
            for term in terms
        ]
        for terms in ((in_terms, out_terms), (qkv_terms, proj_terms))
    ]
    grad_modulation = (late_sums + early_sums).reshape(capacity, -1).astype(jnp.bfloat16)
    mod_halves = grad_modulation.reshape(capacity, pair_count, half_width).transpose(1, 0, 2)
    small_out = lax.psum(
        (
            jnp.sum(grad_modulation.astype(jnp.float32), axis=0),
            qkv_bias_sum.reshape(-1),
            proj_bias_sum.reshape(-1),
            in_bias_sum.reshape(-1),
            out_bias_sum.reshape(-1),
            jnp.concatenate([early_gain, late_gain]),
            jnp.sum(head_sums.reshape(2, HEADS, HEAD_DIM), axis=1),
        ),
        ("dp", "fsdp"),
    )
    every_mod = lax.all_gather(lax.all_to_all(mod_halves, "fsdp", 0, 0, tiled=True), "dp")
    every_mod = every_mod.reshape(total * capacity, half_width)
    ada_grad = transposed_product(silu_rows, every_mod)
    cond_blocks = product_transposed(every_mod, ada_weight)
    cond_parts = lax.all_to_all(
        cond_blocks.reshape(total, capacity, row_share), ("dp", "fsdp"), 0, 0, tiled=True
    )
    grad_cond = (
        jnp.sum(cond_parts.reshape(dp_count, pair_count, capacity, row_share), axis=1)
        .transpose(1, 0, 2)
        .reshape(capacity, model_width)
    )
    cond_grad = jnp.where(held[:, None], grad_cond * swish_slope(cond_float), 0.0)
    shape = tokens.shape
    return (
        output_rows.reshape(shape),
        grad_rows.reshape(shape),
        cond_grad[None],
        ada_grad,
        attn_grads[0],
        attn_grads[1],
        ffn_grads[0],
        ffn_grads[1],
        small_out[0],
        small_out[1],
        small_out[2],
        small_out[3],
        small_out[4],
        small_out[5],
        small_out[6],
    )


def solution(mesh):
    return jax.shard_map(
        functools.partial(per_device, Grid(mesh)),
        mesh=mesh,
        in_specs=(
            P("fsdp", "dp", None, None),
            P("fsdp", "dp", None),
            P("fsdp", "dp"),
            P("fsdp", "dp"),
            P("fsdp", None),
            P("fsdp", "dp", None, None),
            P("dp", "fsdp"),
            P("dp", "fsdp"),
            P("dp", "fsdp"),
            P("dp", "fsdp"),
            P("dp", "fsdp"),
            P(),
            P(),
            P(),
            P(),
            P(),
            P(),
            P(),
        ),
        out_specs=(
            P("fsdp", "dp", None, None),
            P("fsdp", "dp", None, None),
            P("fsdp", "dp", None),
            P("dp", "fsdp"),
            P("dp", "fsdp"),
            P("dp", "fsdp"),
            P("dp", "fsdp"),
            P("dp", "fsdp"),
            P(),
            P(),
            P(),
            P(),
            P(),
            P(),
            P(),
        ),
        check_vma=False,
    )
```
